32 devices in a mesh: dp: 8 (over y, x, core), seq: 4 (over z).
Axes of the slice: x: 2, y: 2, z: 4, core: 2. Of those that a mesh axis runs over, the one named last changes fastest.
Arguments:
- src_x: bfloat16 [16, 1024, 1024], P('dp', 'seq'), may hold values from -6 to 6
- tgt_x: bfloat16 [16, 1024, 1024], P('dp', 'seq'), may hold values from -6 to 6
- src_seg: int32 [16, 1024], P('dp'), may hold values from 0 to 3, never falling along the last dimension, each value on 1 to 512 neighbouring positions
- tgt_seg: int32 [16, 1024], P('dp'), may hold values from 0 to 3, never falling along the last dimension, each value on 1 to 512 neighbouring positions
- tgt_len: int32 [16], P('dp'), may hold values from 512 to 1024
- src_lang: int32 [16, 4], P('dp'), may hold values from 0 to 49
- tgt_lang: int32 [16, 4], P('dp'), may hold values from 0 to 49
- lang_table: bfloat16 [50, 1024], P(None, ('dp', 'seq')), may hold values from -3 to 3
- gains: bfloat16 [5, 1024], P(None, ('dp', 'seq')), may hold values from 0.25 to 1.75
- biases: bfloat16 [16, 1024], P(None, ('dp', 'seq')), may hold values from -2 to 2
- ff_biases: bfloat16 [2, 4096], P(None, ('dp', 'seq')), may hold values from -2 to 2
- enc_proj: bfloat16 [3, 1024, 1024], P(None, ('dp', 'seq')), may hold values from -0.1875 to 0.1875
- enc_oproj: bfloat16 [1024, 1024], P(('dp', 'seq')), may hold values from -0.5 to 0.5
- enc_in: bfloat16 [1024, 4096], P(('dp', 'seq')), may hold values from -0.1875 to 0.1875
- enc_out: bfloat16 [4096, 1024], P(('dp', 'seq')), may hold values from -0.09375 to 0.09375
- dec_proj: bfloat16 [6, 1024, 1024], P(None, ('dp', 'seq')), may hold values from -0.1875 to 0.1875
- dec_oproj: bfloat16 [2, 1024, 1024], P(None, ('dp', 'seq')), may hold values from -0.5 to 0.5
- dec_in: bfloat16 [1024, 4096], P(('dp', 'seq')), may hold values from -0.1875 to 0.1875
- dec_out: bfloat16 [4096, 1024], P(('dp', 'seq')), may hold values from -0.09375 to 0.09375
- src_cot: bfloat16 [16, 1024, 1024], P('dp', 'seq'), may hold values from -6 to 6
- tgt_cot: bfloat16 [16, 1024, 1024], P('dp', 'seq'), may hold values from -6 to 6
Outputs:
- enc_y: bfloat16 [16, 1024, 1024], P('dp', 'seq')
- dec_y: bfloat16 [16, 1024, 1024], P('dp', 'seq')
- src_grad: float32 [16, 1024, 1024], P('dp', 'seq')
- tgt_grad: float32 [16, 1024, 1024], P('dp', 'seq')
- lang_table_grad: float32 [50, 1024], P(None, ('dp', 'seq'))
- gains_grad: float32 [5, 1024], P(None, ('dp', 'seq'))
- biases_grad: float32 [16, 1024], P(None, ('dp', 'seq'))
- ff_biases_grad: float32 [2, 4096], P(None, ('dp', 'seq'))
- enc_proj_grad: float32 [3, 1024, 1024], P(None, ('dp', 'seq'))
- enc_oproj_grad: float32 [1024, 1024], P(('dp', 'seq'))
- enc_in_grad: float32 [1024, 4096], P(('dp', 'seq'))
- enc_out_grad: float32 [4096, 1024], P(('dp', 'seq'))
- dec_proj_grad: float32 [6, 1024, 1024], P(None, ('dp', 'seq'))
- dec_oproj_grad: float32 [2, 1024, 1024], P(None, ('dp', 'seq'))
- dec_in_grad: float32 [1024, 4096], P(('dp', 'seq'))
- dec_out_grad: float32 [4096, 1024], P(('dp', 'seq'))
The draws below stay inside these ranges and needn't reach their ends.
Inputs may be any that keep to these rules, and one draw needn't show every extreme that they name: `src_seg`: along each row the document numbers never fall, and every one of 0 to 3 appears. `tgt_seg`: along each row the document numbers never fall, and every one of 0 to 3 appears. `tgt_len`: target positions at or beyond the row's length are padding.
All inputs are finite; a program needn't handle non-finite values.
Results may differ from the reference program's by a relative error of at most 0.04.
Values may be sent and summed in bfloat16 or wider, within the bound.
A program may use at most 512 MiB of HBM per device.

```python
import math
import jax
import jax.numpy as jnp
import numpy as np
from jax import lax

D = 1024
HEAD_DIM = 64
FF = 4096
LANGS = 50
LEN = 1024
SEGS = 4
BATCH = 16


def with_ends(array, rng, smallest, high):
    spot = [jax.random.randint(jax.random.fold_in(rng, axis), (), 0, length) for axis, length in enumerate(array.shape)]
    widest = array.shape.index(max(array.shape))
    beside = spot[:widest] + [(spot[widest] + 1) % array.shape[widest]] + spot[widest + 1:]
    return array.at[tuple(spot)].set(smallest).at[tuple(beside)].set(high)


def steps_of(own_key, shape, cuts, least, top_value):
    factor_of, own = 1.0, jax.random.fold_in(own_key, 6)
    for axis_at, shards_of in cuts:
        steps = jnp.exp(jax.random.uniform(jax.random.fold_in(own, axis_at), (shards_of,), jnp.float32, least / len(cuts), top_value / len(cuts)))
        factor_of = factor_of * jnp.repeat(steps, shape[axis_at] // shards_of).reshape([-1 if axis == axis_at else 1 for axis in range(len(shape))])
    return factor_of


def split_up(amount, total, limit, slope):
    weights = [(1 << 20) // math.isqrt(grade ** slope) + 1 for grade in range(2, amount + 1)]
    spare, holding = total - limit - (amount - 1), [1] * (amount - 1)
    while spare > 0:
        candidates = [i for i in range(amount - 1) if holding[i] < limit]
        pool, left = sum([weights[i] for i in candidates]), spare
        for i in candidates:
            addition = min(limit - holding[i], max(1, left * weights[i] // pool), spare)
            holding[i] = holding[i] + addition
            spare = spare - addition
    return np.array([limit] + holding)


def ragged(stream_key, count, total, reach, slope):
    if count == 2:
        one = jax.random.randint(stream_key, (), max(1, total - reach), min(reach, total - 1) + 1)
        return jnp.stack([one, total - one])
    sizes = jnp.asarray(split_up(count, total, reach, slope), jnp.int32)
    couples = (count - 1) // 2
    donor, sink = sizes[1:1 + 2 * couples:2], sizes[2:2 + 2 * couples:2]
    room = jnp.minimum(donor - 1, reach - sink)
    passed = jax.random.randint(jax.random.fold_in(stream_key, 1), (couples,), 0, 1 << 20) % (room + 1)
    sizes = sizes.at[1:1 + 2 * couples:2].set(donor - passed).at[2:2 + 2 * couples:2].set(sink + passed)
    return sizes[jax.random.permutation(jax.random.fold_in(stream_key, 2), count)]


def bell_draw(rng, extent, deviation, most, split=(), kind=jnp.bfloat16):
    level = steps_of(rng, extent, split, -0.22, 0.18) if split else 1.0
    drawn = jax.random.normal(rng, extent, jnp.float32) * deviation * level
    return jnp.minimum(jnp.maximum(drawn, -most), most).astype(kind)


def setup_inputs(seed: int = 0) -> dict:
    splits = jax.random.split(jax.random.key(seed), 22)
    src_x = bell_draw(splits[0], (BATCH, LEN, D), 1.0, 6.0, ((0, 8), (1, 4)))
    tgt_x = bell_draw(splits[1], (BATCH, LEN, D), 1.0, 6.0, ((0, 8), (1, 4)))
    src_seg = jax.vmap(lambda own: jnp.searchsorted(jnp.cumsum(ragged(own, SEGS, LEN, LEN // 2, 2)), jnp.arange(LEN), side="right"))(jax.random.split(splits[2], BATCH)).reshape((BATCH, LEN)).astype(jnp.int32)
    tgt_seg = jax.vmap(lambda own: jnp.searchsorted(jnp.cumsum(ragged(own, SEGS, LEN, LEN // 2, 2)), jnp.arange(LEN), side="right"))(jax.random.split(splits[3], BATCH)).reshape((BATCH, LEN)).astype(jnp.int32)
    tgt_len = with_ends(jax.random.randint(splits[4], (BATCH,), LEN // 2, LEN + 1), jax.random.fold_in(splits[4], 1), LEN // 2, LEN).astype(jnp.int32)
    src_lang = with_ends(jax.random.randint(splits[5], (BATCH, SEGS), 0, LANGS), jax.random.fold_in(splits[5], 1), 0, LANGS - 1).astype(jnp.int32)
    tgt_lang = with_ends(jax.random.randint(splits[6], (BATCH, SEGS), 0, LANGS), jax.random.fold_in(splits[6], 1), 0, LANGS - 1).astype(jnp.int32)
    lang_table = bell_draw(splits[7], (LANGS, D), 0.5, 3.0, ((1, 32),))
    gains = jnp.clip(1.0 + 0.15 * jax.random.normal(splits[8], (5, D), jnp.float32), 0.25, 1.75).astype(jnp.bfloat16)
    biases = bell_draw(splits[9], (16, D), 0.3, 2.0, ((1, 32),))
    ff_biases = bell_draw(splits[10], (2, FF), 0.3, 2.0, ((1, 32),))
    enc_proj = bell_draw(splits[11], (3, D, D), D ** -0.5, 0.1875, ((1, 32),))
    enc_oproj = bell_draw(splits[12], (D, D), (D // 8) ** -0.5, 0.5, ((0, 32),))
    enc_in = bell_draw(splits[13], (D, FF), D ** -0.5, 0.1875, ((0, 32),))
    enc_out = bell_draw(splits[14], (FF, D), FF ** -0.5, 0.09375, ((0, 32),))
    dec_proj = bell_draw(splits[15], (6, D, D), D ** -0.5, 0.1875, ((1, 32),))
    dec_oproj = bell_draw(splits[16], (2, D, D), (D // 8) ** -0.5, 0.5, ((1, 32),))
    dec_in = bell_draw(splits[17], (D, FF), D ** -0.5, 0.1875, ((0, 32),))
    dec_out = bell_draw(splits[18], (FF, D), FF ** -0.5, 0.09375, ((0, 32),))
    src_cot = bell_draw(splits[19], (BATCH, LEN, D), 1.0, 6.0, ((0, 8), (1, 4)))
    tgt_cot = bell_draw(splits[20], (BATCH, LEN, D), 1.0, 6.0, ((0, 8), (1, 4)))
    return {"src_x": src_x, "tgt_x": tgt_x, "src_seg": src_seg, "tgt_seg": tgt_seg, "tgt_len": tgt_len, "src_lang": src_lang, "tgt_lang": tgt_lang, "lang_table": lang_table, "gains": gains, "biases": biases, "ff_biases": ff_biases, "enc_proj": enc_proj, "enc_oproj": enc_oproj, "enc_in": enc_in, "enc_out": enc_out, "dec_proj": dec_proj, "dec_oproj": dec_oproj, "dec_in": dec_in, "dec_out": dec_out, "src_cot": src_cot, "tgt_cot": tgt_cot}


@jax.custom_vjp
def low(v):
    return lax.optimization_barrier(v.astype(jnp.bfloat16)).astype(jnp.float32)

@jax.custom_vjp
def low_back(v):
    return v

def low_keep(v):
    return (low(v), None)

def low_pass(kept, grad):
    return (grad,)

def back_keep(v):
    return (v, None)

def back_low(kept, grad):
    return (low(grad),)
low.defvjp(low_keep, low_pass)
low_back.defvjp(back_keep, back_low)
HIGHEST = lax.Precision.HIGHEST

def product(left, right):
    return jnp.dot(left, right, precision=HIGHEST, preferred_element_type=jnp.float32)

def rounded_both(value):
    return low_back(low(value))

def layer_norm(hidden, gain_row, shift_row):
    centred = hidden - lax.optimization_barrier(jnp.mean(hidden, axis=-1, keepdims=True))
    spread = lax.optimization_barrier(jnp.mean(centred * centred, axis=-1, keepdims=True))
    return centred * lax.rsqrt(spread + 1e-05) * gain_row + shift_row

def language_rows(segments, languages):
    token_language = languages[segments]
    return (token_language[:, None] == jnp.arange(LANGS, dtype=jnp.int32)[None, :]).astype(jnp.float32)

def attend(queries, keys, values, allowed):
    count = queries.shape[0]
    query_heads = queries.reshape(count, -1, HEAD_DIM)
    key_heads = keys.reshape(keys.shape[0], -1, HEAD_DIM)
    value_heads = values.reshape(values.shape[0], -1, HEAD_DIM)
    scores = jnp.einsum('qhd,khd->hqk', query_heads, key_heads, precision=HIGHEST) * HEAD_DIM ** (-0.5)
    scores = low_back(jnp.where(allowed[None], scores, -1000000000.0))
    highest = lax.optimization_barrier(jnp.max(scores, axis=-1, keepdims=True))
    exponent = jnp.exp(scores - highest)
    weights = low(exponent / lax.optimization_barrier(jnp.sum(exponent, axis=-1, keepdims=True)))
    mixed = jnp.einsum('hqk,khd->qhd', weights, value_heads, precision=HIGHEST)
    return rounded_both(mixed.reshape(count, -1))

def feed_forward(hidden, gain_row, shift_row, w_in, in_bias, w_out, out_bias):
    normed = low(layer_norm(hidden, gain_row, shift_row))
    inner = low_back(product(normed, w_in) + in_bias)
    acted = low(jax.nn.gelu(inner, approximate=False))
    return hidden + low_back(product(acted, w_out) + out_bias)

def layer_pair(params, source, target, src_seg, tgt_seg, tgt_len, src_lang, tgt_lang):
    lang_table, gains, biases, ff_biases, enc_proj, enc_oproj, enc_in, enc_out, dec_proj, dec_oproj, dec_in, dec_out = params
    columns = jnp.arange(LEN, dtype=jnp.int32)
    hidden = source + product(language_rows(src_seg, src_lang), lang_table)
    normed = low(layer_norm(hidden, gains[0], biases[0]))
    queries = rounded_both(product(normed, enc_proj[0]) + biases[1])
    keys = rounded_both(product(normed, enc_proj[1]))
    values = rounded_both(product(normed, enc_proj[2]) + biases[2])
    mixed = attend(queries, keys, values, src_seg[:, None] == src_seg[None, :])
    hidden = hidden + low_back(product(mixed, enc_oproj) + biases[3])
    encoded = feed_forward(hidden, gains[1], biases[4], enc_in, ff_biases[0], enc_out, biases[5])
    memory = low(encoded)
    hidden = target + product(language_rows(tgt_seg, tgt_lang), lang_table)
    normed = low(layer_norm(hidden, gains[2], biases[6]))
    queries = rounded_both(product(normed, dec_proj[0]) + biases[7])
    keys = rounded_both(product(normed, dec_proj[1]))
    values = rounded_both(product(normed, dec_proj[2]) + biases[8])
    valid = columns < tgt_len
    allowed = (tgt_seg[:, None] == tgt_seg[None, :]) & (columns[None, :] <= columns[:, None])
    allowed = allowed & (valid[None, :] | (columns[None, :] == columns[:, None]))
    mixed = attend(queries, keys, values, allowed)
    hidden = hidden + low_back(product(mixed, dec_oproj[0]) + biases[9])
    normed = low(layer_norm(hidden, gains[3], biases[10]))
    queries = rounded_both(product(normed, dec_proj[3]) + biases[11])
    keys = rounded_both(product(memory, dec_proj[4]))
    values = rounded_both(product(memory, dec_proj[5]) + biases[12])
    mixed = attend(queries, keys, values, tgt_seg[:, None] == src_seg[None, :])
    hidden = hidden + low_back(product(mixed, dec_oproj[1]) + biases[13])
    decoded = feed_forward(hidden, gains[4], biases[14], dec_in, ff_biases[1], dec_out, biases[15])
    return (encoded, decoded)

def reference(src_x, tgt_x, src_seg, tgt_seg, tgt_len, src_lang, tgt_lang, lang_table, gains, biases, ff_biases, enc_proj, enc_oproj, enc_in, enc_out, dec_proj, dec_oproj, dec_in, dec_out, src_cot, tgt_cot):
    params = tuple((weight.astype(jnp.float32) for weight in (lang_table, gains, biases, ff_biases, enc_proj, enc_oproj, enc_in, enc_out, dec_proj, dec_oproj, dec_in, dec_out)))
    start = tuple((jnp.zeros(weight.shape, jnp.float32) for weight in params))

    def one_pair(totals, row):
        source, target, row_src_seg, row_tgt_seg, row_tgt_len, row_src_lang, row_tgt_lang, row_src_cot, row_tgt_cot = row

        def forward(weights, source_in, target_in):
            return layer_pair(weights, source_in, target_in, row_src_seg, row_tgt_seg, row_tgt_len, row_src_lang, row_tgt_lang)
        outputs, pullback = jax.vjp(forward, params, source.astype(jnp.float32), target.astype(jnp.float32))
        weight_grads, source_grad, target_grad = pullback((row_src_cot.astype(jnp.float32), row_tgt_cot.astype(jnp.float32)))
        totals = tuple((total + grad for total, grad in zip(totals, weight_grads)))
        return (totals, (outputs[0].astype(jnp.bfloat16), outputs[1].astype(jnp.bfloat16), source_grad, target_grad))
    totals, outputs = lax.scan(one_pair, start, (src_x, tgt_x, src_seg, tgt_seg, tgt_len, src_lang, tgt_lang, src_cot, tgt_cot))
    return (outputs[0], outputs[1], outputs[2], outputs[3], totals[0], totals[1], totals[2], totals[3], totals[4], totals[5], totals[6], totals[7], totals[8], totals[9], totals[10], totals[11])
```

```python
import functools

import jax
import jax.numpy as jnp
from jax import lax
from jax.experimental import pallas as pl
from jax.experimental.pallas import tpu as pltpu
from jax.sharding import PartitionSpec as P

HEAD_DIM = 64
EPSILON = 1e-05
MASKED = -1000000000.0
BLOCK = 256
PAIR = 2 * HEAD_DIM
B16 = jnp.bfloat16
F32 = jnp.float32


def product(left, right):
    return jnp.dot(left, right, preferred_element_type=F32)


def product_tn(left, right):
    return lax.dot_general(left, right, (((0,), (0,)), ((), ())), preferred_element_type=F32)


def product_nt(left, right):
    return lax.dot_general(left, right, (((1,), (1,)), ((), ())), preferred_element_type=F32)


def column_sum(values):
    return jnp.sum(values.astype(F32), axis=0)


def norm_parts(hidden):
    centred = hidden - jnp.mean(hidden, axis=-1, keepdims=True)
    spread = jnp.mean(centred * centred, axis=-1, keepdims=True)
    scale = lax.rsqrt(spread + EPSILON)
    return centred * scale, scale


def layer_norm(hidden, gain_row, shift_row):
    return (norm_parts(hidden)[0] * gain_row + shift_row).astype(B16)


def norm_backward(hidden, gain_row, grad):
    unit, scale = norm_parts(hidden)
    weighted = grad * gain_row
    grad_hidden = scale * (
        weighted
        - jnp.mean(weighted, axis=-1, keepdims=True)
        - unit * jnp.mean(weighted * unit, axis=-1, keepdims=True)
    )
    return grad_hidden, jnp.sum(grad * unit, axis=0), jnp.sum(grad, axis=0)


def gelu_both(values):
    below = 0.5 * (1.0 + lax.erf(values * (0.5**0.5)))
    density = jnp.exp(-0.5 * values * values) * (0.5 / jnp.pi) ** 0.5
    return (values * below).astype(B16), (below + values * density).astype(B16)


def allowed_block(causal, kseg_ref, qseg, length, key_at, query_at):
    allowed = kseg_ref[key_at : key_at + BLOCK, :] == qseg
    if causal:
        keys = key_at + lax.broadcasted_iota(jnp.int32, (BLOCK, BLOCK), 0)
        queries = query_at + lax.broadcasted_iota(jnp.int32, (BLOCK, BLOCK), 1)
        allowed = allowed & (keys <= queries) & ((keys < length) | (keys == queries))
    return allowed


def head_lanes(head, shape):
    lane = lax.broadcasted_iota(jnp.int32, shape, 1)
    return (lane >= head * HEAD_DIM) & (lane < (head + 1) * HEAD_DIM)


def dot_nt(left, right):
    return lax.dot_general(left, right, (((1,), (1,)), ((), ())), preferred_element_type=F32)


def forward_kernel(causal, info_ref, q_ref, k_ref, v_ref, qseg_ref, kseg_ref, o_ref, lse_ref, vt_ref, s_ref, acc_ref, stat_ref):
    block = pl.program_id(1)
    blocks = k_ref.shape[0] // BLOCK
    length = info_ref[blocks * blocks]

    @pl.when(block == 0)
    def _():
        vt_ref[...] = v_ref[...].T

    qseg = qseg_ref[...]
    scaled = q_ref[...] * jnp.asarray(HEAD_DIM**-0.5, B16)
    zero = jnp.zeros_like(scaled)
    heads = [jnp.where(head_lanes(h, scaled.shape), scaled, zero) for h in range(2)]
    stat_ref[0:16, :] = jnp.full((16, BLOCK), -1e30, F32)
    stat_ref[16:32, :] = jnp.zeros((16, BLOCK), F32)
    acc_ref[...] = jnp.zeros_like(acc_ref)
    for j in range(blocks):

        @pl.when(info_ref[block * blocks + j] > 0)
        def _(j=j):
            keys = k_ref[j * BLOCK : (j + 1) * BLOCK, :]
            allowed = allowed_block(causal, kseg_ref, qseg, length, j * BLOCK, block * BLOCK)
            for h in range(2):
                scores = jnp.where(allowed, dot_nt(keys, heads[h]), MASKED)
                s_ref[h, j * BLOCK : (j + 1) * BLOCK, :] = scores
                top = jnp.max(scores.reshape(BLOCK // 8, 8, BLOCK), axis=0)
                stat_ref[h * 8 : h * 8 + 8, :] = jnp.maximum(stat_ref[h * 8 : h * 8 + 8, :], top)

    highest = [jnp.max(stat_ref[h * 8 : h * 8 + 8, :], axis=0, keepdims=True) for h in range(2)]
    for j in range(blocks):

        @pl.when(info_ref[block * blocks + j] > 0)
        def _(j=j):
            for h in range(2):
                weights = jnp.exp(s_ref[h, j * BLOCK : (j + 1) * BLOCK, :] - highest[h])
                total = jnp.sum(weights.reshape(BLOCK // 8, 8, BLOCK), axis=0)
                stat_ref[16 + h * 8 : 24 + h * 8, :] += total
                rows = pl.ds(h * HEAD_DIM, HEAD_DIM)
                acc_ref[rows, :] += jnp.dot(
                    vt_ref[rows, j * BLOCK : (j + 1) * BLOCK],
                    weights.astype(B16),
                    preferred_element_type=F32,
                )

    lse_ref[...] = jnp.zeros_like(lse_ref)
    for h in range(2):
        total = jnp.sum(stat_ref[16 + h * 8 : 24 + h * 8, :], axis=0, keepdims=True)
        rows = pl.ds(h * HEAD_DIM, HEAD_DIM)
        acc_ref[rows, :] = acc_ref[rows, :] / total
        lse_ref[0, h : h + 1, :] = highest[h] + jnp.log(total)
    o_ref[...] = acc_ref[...].T.astype(B16)


def backward_kernel(
    causal,
    info_ref,
    q_ref,
    k_ref,
    v_ref,
    o_ref,
    do_ref,
    lse_ref,
    qseg_ref,
    kseg_ref,
    dq_ref,
    dk_ref,
    dv_ref,
    kt_ref,
    dqt_ref,
    sums_ref,
):
    block = pl.program_id(1)
    blocks = k_ref.shape[0] // BLOCK
    length = info_ref[blocks * blocks]

    @pl.when(block == 0)
    def _():
        kt_ref[...] = k_ref[...].T
        sums_ref[...] = jnp.zeros_like(sums_ref)

    qseg = qseg_ref[...]
    scaled = q_ref[...] * jnp.asarray(HEAD_DIM**-0.5, B16)
    grads = do_ref[...]
    zero = jnp.zeros_like(scaled)
    lanes = [head_lanes(h, scaled.shape) for h in range(2)]
    query_heads = [jnp.where(lanes[h], scaled, zero) for h in range(2)]
    grad_heads = [jnp.where(lanes[h], grads, zero) for h in range(2)]
    mixed = grads.astype(F32) * o_ref[...].astype(F32)
    picks = jnp.concatenate(
        [head_lanes(h, (8, PAIR)).astype(F32) for h in range(2)], axis=0
    )
    inner_both = lax.dot_general(
        picks, mixed, (((1,), (1,)), ((), ())), precision=lax.Precision.HIGHEST, preferred_element_type=F32
    )
    inner = [inner_both[8 * h : 8 * h + 1, :] for h in range(2)]
    lse = [lse_ref[0, h : h + 1, :] for h in range(2)]
    dqt_ref[...] = jnp.zeros_like(dqt_ref)
    for j in range(blocks):

        @pl.when(info_ref[block * blocks + j] > 0)
        def _(j=j):
            rows = slice(j * BLOCK, (j + 1) * BLOCK)
            keys = k_ref[rows, :]
            values = v_ref[rows, :]
            allowed = allowed_block(causal, kseg_ref, qseg, length, j * BLOCK, block * BLOCK)
            key_sum = sums_ref[0, rows, :]
            value_sum = sums_ref[1, rows, :]
            for h in range(2):
                scores = dot_nt(keys, query_heads[h])
                chances = jnp.where(allowed, jnp.exp(scores - lse[h]), 0.0)
                grad_chances = dot_nt(values, grad_heads[h])
                grad_scores = (chances * (grad_chances - inner[h])).astype(B16)
                value_sum += jnp.dot(chances.astype(B16), grad_heads[h], preferred_element_type=F32)
                key_sum += jnp.dot(grad_scores, query_heads[h], preferred_element_type=F32)
                part = pl.ds(h * HEAD_DIM, HEAD_DIM)
                dqt_ref[part, :] += jnp.dot(kt_ref[part, rows], grad_scores, preferred_element_type=F32)
            sums_ref[0, rows, :] = key_sum
            sums_ref[1, rows, :] = value_sum

    dq_ref[...] = (dqt_ref[...].T * HEAD_DIM**-0.5).astype(B16)

    @pl.when(block == blocks - 1)
    def _():
        dk_ref[...] = sums_ref[0].astype(B16)
        dv_ref[...] = sums_ref[1].astype(B16)


def block_info(causal, query_seg, key_seg, length):
    blocks = query_seg.shape[0] // BLOCK
    query_low, query_high = query_seg[::BLOCK], query_seg[BLOCK - 1 :: BLOCK]
    key_low, key_high = key_seg[::BLOCK], key_seg[BLOCK - 1 :: BLOCK]
    meets = (key_low[None, :] <= query_high[:, None]) & (key_high[None, :] >= query_low[:, None])
    if causal:
        at = jnp.arange(blocks)
        meets = meets & (at[None, :] <= at[:, None])
    return jnp.concatenate([meets.astype(jnp.int32).reshape(-1), length[None]])


def attention_specs(count, offsets):
    query = pl.BlockSpec((BLOCK, PAIR), lambda p, i, info: (i, p + offsets[0]))
    key = pl.BlockSpec((count, PAIR), lambda p, i, info: (0, p + offsets[1]))
    value = pl.BlockSpec((count, PAIR), lambda p, i, info: (0, p + offsets[2]))
    plain = pl.BlockSpec((BLOCK, PAIR), lambda p, i, info: (i, p))
    whole = pl.BlockSpec((count, PAIR), lambda p, i, info: (0, p))
    stats = pl.BlockSpec((1, 8, BLOCK), lambda p, i, info: (p, 0, i))
    qseg = pl.BlockSpec((1, BLOCK), lambda p, i, info: (0, i))
    kseg = pl.BlockSpec((count, 1), lambda p, i, info: (0, 0))
    return query, key, value, plain, whole, stats, qseg, kseg


def attend_forward(causal, masks, queries, keys, values, offsets, width):
    info, qseg_row, kseg_column = masks
    count = queries.shape[0]
    pairs = width // PAIR
    query, key, value, plain, _, stats, qseg, kseg = attention_specs(count, offsets)
    return pl.pallas_call(
        functools.partial(forward_kernel, causal),
        grid_spec=pltpu.PrefetchScalarGridSpec(
            num_scalar_prefetch=1,
            grid=(pairs, count // BLOCK),
            in_specs=[query, key, value, qseg, kseg],
            out_specs=[plain, stats],
            scratch_shapes=[pltpu.VMEM((PAIR, count), B16), pltpu.VMEM((2, count, BLOCK), F32), pltpu.VMEM((PAIR, BLOCK), F32), pltpu.VMEM((32, BLOCK), F32)],
        ),
        out_shape=[
            jax.ShapeDtypeStruct((count, width), B16),
            jax.ShapeDtypeStruct((pairs, 8, count), F32),
        ],
        compiler_params=pltpu.CompilerParams(vmem_limit_bytes=24 * 2**20),
        cost_estimate=pl.CostEstimate(
            flops=2 * 2 * count * count * width * 2, bytes_accessed=count * width * 8, transcendentals=0
        ),
        name="attend_causal" if causal else "attend",
    )(info, queries, keys, values, qseg_row, kseg_column)


def attend_backward(causal, masks, queries, keys, values, offsets, width, mixed, lse, grad):
    info, qseg_row, kseg_column = masks
    count = queries.shape[0]
    pairs = width // PAIR
    query, key, value, plain, whole, stats, qseg, kseg = attention_specs(count, offsets)
    return pl.pallas_call(
        functools.partial(backward_kernel, causal),
        grid_spec=pltpu.PrefetchScalarGridSpec(
            num_scalar_prefetch=1,
            grid=(pairs, count // BLOCK),
            in_specs=[query, key, value, plain, plain, stats, qseg, kseg],
            out_specs=[plain, whole, whole],
            scratch_shapes=[
                pltpu.VMEM((PAIR, count), B16),
                pltpu.VMEM((PAIR, BLOCK), F32),
                pltpu.VMEM((2, count, PAIR), F32),
            ],
        ),
        out_shape=[jax.ShapeDtypeStruct((count, width), B16)] * 3,
        compiler_params=pltpu.CompilerParams(vmem_limit_bytes=24 * 2**20),
        cost_estimate=pl.CostEstimate(
            flops=5 * 2 * count * count * width * 2, bytes_accessed=count * width * 16, transcendentals=0
        ),
        name="attend_grad_causal" if causal else "attend_grad",
    )(info, queries, keys, values, mixed, grad, lse, qseg_row, kseg_column)


def xor_arrange(pieces, place):
    pieces, bit = list(pieces), 0
    while 1 << bit < len(pieces):
        odd = ((place >> bit) & 1) == 1
        pieces = [jnp.where(odd, pieces[k ^ (1 << bit)], pieces[k]) for k in range(len(pieces))]
        bit += 1
    return pieces


class Place:
    def __init__(self, dp, seq):
        self.dp, self.seq = dp, seq
        self.at = lax.axis_index("dp")
        self.z = lax.axis_index("seq")
        self.core = self.at % 2
        self.x = (self.at // 2) % 2
        self.y = self.at // 4

    def over_dp(self, value, mask):
        return lax.ppermute(value, "dp", [(i, i ^ mask) for i in range(self.dp)])

    def over_seq(self, value, mask):
        return lax.ppermute(value, "seq", [(i, i ^ mask) for i in range(self.seq)])

    def over_core(self, value):
        return self.over_dp(value, 1)

    def row_in(self, array):
        parts = array.reshape(2, array.shape[1], 2, -1)
        got = []
        for m in range(4):
            code = self.z ^ m
            piece = lax.dynamic_index_in_dim(parts, code // 2, 0, keepdims=False)
            piece = lax.dynamic_index_in_dim(piece, code % 2, 1, keepdims=False)
            moves = []
            for d in range(self.dp):
                for z in range(4):
                    q = m ^ z
                    moves.append((d * 4 + z, (d - d % 2 + q % 2) * 4 + 2 * (d % 2) + q // 2))
            got.append(lax.ppermute(piece, ("dp", "seq"), moves))
        half = jnp.concatenate(xor_arrange(got, (self.z % 2) * 2 + self.core), axis=0)
        return jnp.concatenate(xor_arrange([half, self.over_core(half)], self.core), axis=1)

    def row_out(self, row):
        parts = row.reshape(4, -1, 2, row.shape[1] // 2)
        mine = lax.dynamic_index_in_dim(parts, self.core, 2, keepdims=False)
        q_here = (self.z % 2) * 2 + self.core
        got = []
        for m in range(4):
            piece = lax.dynamic_index_in_dim(mine, q_here ^ m, 0, keepdims=False)
            moves = []
            for d in range(self.dp):
                for z in range(4):
                    q = (z % 2) * 2 + d % 2
                    moves.append((d * 4 + z, (d - d % 2 + z // 2) * 4 + (m ^ q)))
            got.append(lax.ppermute(piece, ("dp", "seq"), moves))
        placed = xor_arrange(got, self.z)
        return jnp.stack([jnp.concatenate(placed[2 * i : 2 * i + 2], axis=1) for i in range(2)])

    def both_cores(self, part):
        part = part.astype(B16)
        return part.astype(F32) + self.over_core(part).astype(F32)


def own_columns(array, core, runs=8):
    split = array.reshape(array.shape[:-1] + (runs // 2, 2, array.shape[-1] // runs))
    mine = lax.dynamic_index_in_dim(split, core, split.ndim - 2, keepdims=False)
    return mine.reshape(array.shape[:-1] + (array.shape[-1] // 2,))


def lay_side(array):
    return jnp.concatenate([array[i] for i in range(array.shape[0])], axis=1)


class Tree:
    def __init__(self, place):
        self.place = place

    def gather(self, local, x_first):
        place = self.place
        pieces = [local] + [place.over_seq(local, j) for j in range(1, 4)]
        held = jnp.stack(xor_arrange(pieces, place.z))
        if x_first:
            held = jnp.stack(xor_arrange([held, place.over_dp(held, 2)], place.x))
            return jnp.stack(xor_arrange([held, place.over_dp(held, 4)], place.y))
        held = jnp.stack(xor_arrange([held, place.over_dp(held, 4)], place.y))
        return jnp.stack(xor_arrange([held, place.over_dp(held, 2)], place.x), axis=1)

    def by_columns(self, local, x_first):
        core = self.place.core
        mine = lay_side(own_columns(local, core))
        other = lay_side(own_columns(local, 1 - core))
        both = jnp.stack(xor_arrange([mine, self.place.over_core(other)], core))
        full = self.gather(both, x_first)
        return full.transpose(0, 1, 3, 2, 4, 5).reshape(-1, full.shape[-1])

    def by_rows(self, local, x_first):
        return self.gather(local, x_first).reshape(-1, local.shape[-1])

    def sum_chips(self, features, grad, x_first):
        place = self.place
        count, size = features.shape
        quarter = size // 4
        split = features.reshape(count, 2, 2, quarter)
        axis, here, mask = (2, place.x, 2) if x_first else (1, place.y, 4)
        here_two, mask_two = (place.y, 4) if x_first else (place.x, 2)

        def part(index):
            cut = lax.dynamic_index_in_dim(split, index, axis, keepdims=False)
            return product_tn(cut.reshape(count, size // 2), grad)

        sent = place.over_dp(part(1 - here).astype(B16), mask)
        kept = (part(here) + sent.astype(F32)).astype(B16).reshape(2, quarter, grad.shape[1])
        away = lax.dynamic_index_in_dim(kept, 1 - here_two, 0, keepdims=False)
        stay = lax.dynamic_index_in_dim(kept, here_two, 0, keepdims=False)
        return (stay.astype(F32) + place.over_dp(away, mask_two).astype(F32)).astype(B16)

    def sum_z(self, value, axis):
        place = self.place
        total = lax.dynamic_index_in_dim(value, place.z, axis, keepdims=False).astype(F32)
        for j in range(1, 4):
            piece = lax.dynamic_index_in_dim(value, place.z ^ j, axis, keepdims=False)
            total = total + place.over_seq(piece, j).astype(F32)
        return total

    def grad_by_columns(self, features, grad, x_first, parts):
        place = self.place
        value = self.sum_chips(features, grad, x_first)
        rows = value.shape[0] // 8
        total = self.sum_z(value.reshape(2, 4, rows, value.shape[1]), 1)
        mine = lax.dynamic_index_in_dim(total, place.core, 0, keepdims=False)
        other = lax.dynamic_index_in_dim(total, 1 - place.core, 0, keepdims=False).astype(B16)
        got = place.over_core(other).astype(F32)
        both = [v.reshape(rows, parts, 4, -1) for v in xor_arrange([mine, got], place.core)]
        return jnp.stack(both, axis=3).reshape(rows, parts, -1).transpose(1, 0, 2)

    def grad_by_rows(self, features, grad, x_first):
        value = self.sum_chips(features, grad, x_first)
        return self.sum_z(value.reshape(4, -1, value.shape[1]), 0)

    def small(self, table, hidden):
        place = self.place
        n, m = table.shape[0], hidden.shape[0]
        both = jnp.concatenate(
            [
                table.reshape(n, 2, 2, 4, -1).transpose(1, 2, 3, 0, 4).reshape(2, 2, 4, -1),
                hidden.reshape(m, 2, 2, 4, -1).transpose(1, 2, 3, 0, 4).reshape(2, 2, 4, -1),
            ],
            axis=-1,
        )
        for here, mask in ((place.y, 4), (place.x, 2)):
            away = lax.dynamic_index_in_dim(both, 1 - here, 0, keepdims=False)
            both = lax.dynamic_index_in_dim(both, here, 0, keepdims=False) + place.over_dp(away, mask)
        flat = self.sum_z(both, 0)
        edge = table.shape[1] // 16 * n
        return flat[:edge].reshape(n, -1), flat[edge:].reshape(m, -1)


class Plain:
    def __init__(self, place):
        self.place = place
        self.axes = ("dp", "seq")

    def by_columns(self, local, x_first):
        full = lax.all_gather(local, self.axes, axis=1, tiled=True)
        return lay_side(own_columns(full, self.place.core))

    def by_rows(self, local, x_first):
        full = lax.all_gather(local, self.axes, axis=0, tiled=True)
        split = full.reshape(4, 2, full.shape[0] // 8, full.shape[1])
        return lax.dynamic_index_in_dim(split, self.place.core, 1, keepdims=False).reshape(-1, full.shape[1])

    def spread(self, half, axis):
        shape = half.shape[:axis] + (4, 1, half.shape[axis] // 4) + half.shape[axis + 1 :]
        half = half.reshape(shape)
        empty = jnp.zeros_like(half)
        first = jnp.where(self.place.core == 0, half, empty)
        second = jnp.where(self.place.core == 1, half, empty)
        both = jnp.concatenate([first, second], axis=axis + 1)
        return both.reshape(shape[:axis] + (-1,) + shape[axis + 3 :])

    def grad_by_columns(self, features, grad, x_first, parts):
        full = product_tn(features, grad)
        full = full.reshape(full.shape[0], parts, -1).transpose(1, 0, 2).astype(B16)
        full = self.spread(full, 2)
        return lax.psum_scatter(full, self.axes, scatter_dimension=1, tiled=True).astype(F32)

    def grad_by_rows(self, features, grad, x_first):
        full = self.spread(product_tn(features, grad).astype(B16), 0)
        return lax.psum_scatter(full, self.axes, scatter_dimension=0, tiled=True).astype(F32)

    def small(self, table, hidden):
        return tuple(
            lax.psum_scatter(self.spread(v, 1), self.axes, scatter_dimension=1, tiled=True)
            for v in (table, hidden)
        )


def on_device(
    dp,
    seq,
    src_x,
    tgt_x,
    src_seg,
    tgt_seg,
    tgt_len,
    src_lang,
    tgt_lang,
    lang_table,
    gains,
    biases,
    ff_biases,
    enc_proj,
    enc_oproj,
    enc_in,
    enc_out,
    dec_proj,
    dec_oproj,
    dec_in,
    dec_out,
    src_cot,
    tgt_cot,
):
    place = Place(dp, seq)
    core = place.core
    moves = Tree(place) if (dp, seq) == (8, 4) else Plain(place)
    width = enc_oproj.shape[1]
    half = width // 2
    langs = lang_table.shape[0]

    n_small = langs + gains.shape[0] + biases.shape[0]
    table = jnp.concatenate([lang_table, gains, biases], axis=0)
    flat = jnp.concatenate([table.reshape(-1), ff_biases.reshape(-1)])
    everything = lax.all_gather(flat, ("dp", "seq"), axis=0, tiled=False)
    edge = table.size
    table = everything[:, :edge].reshape(dp * seq, n_small, -1).transpose(1, 0, 2).reshape(n_small, width)
    ffb = everything[:, edge:].reshape(dp * seq, 2, -1).transpose(1, 0, 2).reshape(2, -1)
    languages = table[:langs]
    gain_f = table[langs : langs + gains.shape[0]].astype(F32)
    bias_f = table[langs + gains.shape[0] :].astype(F32)
    ffb_own = own_columns(ffb.astype(F32), core)
    bias_own = own_columns(bias_f, core)

    meta = jnp.concatenate([src_seg, tgt_seg, tgt_len[:, None], src_lang, tgt_lang], axis=1)
    rows = jnp.where(place.z // 2 == core, meta, place.over_core(meta))
    row = lax.dynamic_index_in_dim(rows, place.z % 2, 0, keepdims=False)
    count, segs = src_seg.shape[1], src_lang.shape[1]
    s_seg, t_seg, t_len = row[:count], row[count : 2 * count], row[2 * count]
    s_lang, t_lang = row[2 * count + 1 : 2 * count + 1 + segs], row[2 * count + 1 + segs :]

    def onehot(segments, chosen):
        member = segments[:, None] == jnp.arange(segs, dtype=jnp.int32)[None, :]
        token = jnp.sum(jnp.where(member, chosen[None, :], 0), axis=1)
        return (token[:, None] == jnp.arange(langs, dtype=jnp.int32)[None, :]).astype(B16)

    src_hot, tgt_hot = onehot(s_seg, s_lang), onehot(t_seg, t_lang)
    enc_masks = (block_info(False, s_seg, s_seg, t_len), s_seg[None, :], s_seg[:, None])
    dec_masks = (block_info(True, t_seg, t_seg, t_len), t_seg[None, :], t_seg[:, None])
    cross_masks = (block_info(False, t_seg, s_seg, t_len), t_seg[None, :], s_seg[:, None])

    source = place.row_in(src_x)
    target = place.row_in(tgt_x)
    target_cot = place.row_in(tgt_cot)
    source_cot = place.row_in(src_cot)

    enc_qkv_w = moves.by_columns(enc_proj, True)
    enc_o_w = moves.by_rows(enc_oproj, False)
    enc_in_w = moves.by_columns(enc_in[None], False)
    enc_out_w = moves.by_rows(enc_out, True)
    dec_qkv_w = moves.by_columns(dec_proj[0:3], False)
    dec_o_w = moves.by_rows(dec_oproj[0], True)
    cross_w = moves.by_columns(dec_proj[3:6], True)
    cross_o_w = moves.by_rows(dec_oproj[1], False)
    dec_in_w = moves.by_columns(dec_in[None], False)
    dec_out_w = moves.by_rows(dec_out, True)

    none = jnp.zeros((half,), F32)
    packed = (0, half // PAIR, 2 * half // PAIR)

    enc_h0 = source.astype(F32) + product(src_hot, languages)
    enc_n1 = layer_norm(enc_h0, gain_f[0], bias_f[0])
    enc_qkv_bias = jnp.concatenate([bias_own[1], none, bias_own[2]])
    enc_qkv = (product(enc_n1, enc_qkv_w) + enc_qkv_bias).astype(B16)
    enc_mixed, enc_lse = attend_forward(False, enc_masks, enc_qkv, enc_qkv, enc_qkv, packed, half)
    enc_h1 = enc_h0 + place.both_cores(product(enc_mixed, enc_o_w)) + bias_f[3]
    enc_n2 = layer_norm(enc_h1, gain_f[1], bias_f[4])
    enc_acted, enc_slope = gelu_both(product(enc_n2, enc_in_w) + ffb_own[0])
    encoded = enc_h1 + place.both_cores(product(enc_acted, enc_out_w)) + bias_f[5]
    memory = encoded.astype(B16)

    dec_h0 = target.astype(F32) + product(tgt_hot, languages)
    dec_n1 = layer_norm(dec_h0, gain_f[2], bias_f[6])
    dec_qkv_bias = jnp.concatenate([bias_own[7], none, bias_own[8]])
    dec_qkv = (product(dec_n1, dec_qkv_w) + dec_qkv_bias).astype(B16)
    dec_mixed, dec_lse = attend_forward(True, dec_masks, dec_qkv, dec_qkv, dec_qkv, packed, half)
    dec_h1 = dec_h0 + place.both_cores(product(dec_mixed, dec_o_w)) + bias_f[9]
    dec_n2 = layer_norm(dec_h1, gain_f[3], bias_f[10])
    cross_q = (product(dec_n2, cross_w[:, :half]) + bias_own[11]).astype(B16)
    cross_kv_bias = jnp.concatenate([none, bias_own[12]])
    cross_kv = (product(memory, cross_w[:, half:]) + cross_kv_bias).astype(B16)
    apart = (0, 0, half // PAIR)
    cross_mixed, cross_lse = attend_forward(False, cross_masks, cross_q, cross_kv, cross_kv, apart, half)
    dec_h2 = dec_h1 + place.both_cores(product(cross_mixed, cross_o_w)) + bias_f[13]
    dec_n3 = layer_norm(dec_h2, gain_f[4], bias_f[14])
    dec_acted, dec_slope = gelu_both(product(dec_n3, dec_in_w) + ffb_own[1])
    decoded = dec_h2 + place.both_cores(product(dec_acted, dec_out_w)) + bias_f[15]

    dec_du = (product_nt(target_cot, dec_out_w) * dec_slope.astype(F32)).astype(B16)
    dec_dn3 = place.both_cores(product_nt(dec_du, dec_in_w))
    dec_out_grad = moves.grad_by_rows(dec_acted, target_cot, True)
    dec_in_grad = moves.grad_by_columns(dec_n3, dec_du, False, 1)[0]
    target_cot_f = target_cot.astype(F32)
    step, gain_four, shift_14 = norm_backward(dec_h2, gain_f[4], dec_dn3)
    grad_h2 = target_cot_f + step

    cross_branch = grad_h2.astype(B16)
    cross_do = product_nt(cross_branch, cross_o_w).astype(B16)
    cross_dq, cross_dk, cross_dv = attend_backward(
        False, cross_masks, cross_q, cross_kv, cross_kv, apart, half, cross_mixed, cross_lse, cross_do
    )
    cross_dkv = jnp.concatenate([cross_dk, cross_dv], axis=1)
    grad_memory = place.both_cores(product_nt(cross_dkv, cross_w[:, half:]))
    dec_dn2 = place.both_cores(product_nt(cross_dq, cross_w[:, :half]))
    cross_o_grad = moves.grad_by_rows(cross_mixed, cross_branch, True)
    cross_q_grad = moves.grad_by_columns(dec_n2, cross_dq, True, 1)
    cross_kv_grad = moves.grad_by_columns(memory, cross_dkv, False, 2)

    source_cot_f = source_cot.astype(F32) + grad_memory
    enc_ff_branch = source_cot_f.astype(B16)
    enc_du = (product_nt(enc_ff_branch, enc_out_w) * enc_slope.astype(F32)).astype(B16)
    enc_dn2 = place.both_cores(product_nt(enc_du, enc_in_w))
    enc_out_grad = moves.grad_by_rows(enc_acted, enc_ff_branch, True)
    enc_in_grad = moves.grad_by_columns(enc_n2, enc_du, False, 1)[0]

    step, gain_three, shift_10 = norm_backward(dec_h1, gain_f[3], dec_dn2)
    grad_h1 = grad_h2 + step
    self_branch = grad_h1.astype(B16)
    dec_do = product_nt(self_branch, dec_o_w).astype(B16)
    dec_dqkv = jnp.concatenate(
        attend_backward(
            True, dec_masks, dec_qkv, dec_qkv, dec_qkv, packed, half, dec_mixed, dec_lse, dec_do
        ),
        axis=1,
    )
    dec_dn1 = place.both_cores(product_nt(dec_dqkv, dec_qkv_w))
    dec_o_grad = moves.grad_by_rows(dec_mixed, self_branch, False)
    dec_qkv_grad = moves.grad_by_columns(dec_n1, dec_dqkv, True, 3)
    step, gain_two, shift_6 = norm_backward(dec_h0, gain_f[2], dec_dn1)
    target_grad = grad_h1 + step

    step, gain_one, shift_4 = norm_backward(enc_h1, gain_f[1], enc_dn2)
    grad_e1 = source_cot_f + step
    enc_branch = grad_e1.astype(B16)
    enc_do = product_nt(enc_branch, enc_o_w).astype(B16)
    enc_dqkv = jnp.concatenate(
        attend_backward(
            False, enc_masks, enc_qkv, enc_qkv, enc_qkv, packed, half, enc_mixed, enc_lse, enc_do
        ),
        axis=1,
    )
    enc_dn1 = place.both_cores(product_nt(enc_dqkv, enc_qkv_w))
    enc_o_grad = moves.grad_by_rows(enc_mixed, enc_branch, False)
    enc_qkv_grad = moves.grad_by_columns(enc_n1, enc_dqkv, True, 3)
    step, gain_zero, shift_0 = norm_backward(enc_h0, gain_f[0], enc_dn1)
    source_grad = grad_e1 + step

    def split_two(value):
        high = value.astype(B16)
        return high, (value - high.astype(F32)).astype(B16)

    lang_grad = 0.0
    for hot, value in ((src_hot, source_grad), (tgt_hot, target_grad)):
        for piece in split_two(own_columns(value, core)):
            lang_grad = lang_grad + product_tn(hot, piece)
    own = functools.partial(own_columns, core=core)
    gain_rows = jnp.stack([gain_zero, gain_one, gain_two, gain_three, gain_four])
    enc_qkv_sum, dec_qkv_sum = column_sum(enc_dqkv), column_sum(dec_dqkv)
    bias_rows = jnp.stack(
        [
            own(shift_0),
            enc_qkv_sum[:half],
            enc_qkv_sum[2 * half :],
            own(column_sum(enc_branch)),
            own(shift_4),
            own(column_sum(enc_ff_branch)),
            own(shift_6),
            dec_qkv_sum[:half],
            dec_qkv_sum[2 * half :],
            own(column_sum(self_branch)),
            own(shift_10),
            column_sum(cross_dq),
            column_sum(cross_dv),
            own(column_sum(cross_branch)),
            own(shift_14),
            own(column_sum(target_cot)),
        ]
    )
    small, ffb_grad = moves.small(
        jnp.concatenate([lang_grad, own(gain_rows), bias_rows], axis=0),
        jnp.stack([column_sum(enc_du), column_sum(dec_du)]),
    )
    return (
        place.row_out(memory),
        place.row_out(decoded.astype(B16)),
        place.row_out(source_grad.astype(B16)).astype(F32),
        place.row_out(target_grad.astype(B16)).astype(F32),
        small[:langs],
        small[langs : langs + 5],
        small[langs + 5 :],
        ffb_grad,
        enc_qkv_grad,
        enc_o_grad,
        enc_in_grad,
        enc_out_grad,
        jnp.concatenate([dec_qkv_grad, cross_q_grad, cross_kv_grad], axis=0),
        jnp.stack([dec_o_grad, cross_o_grad]),
        dec_in_grad,
        dec_out_grad,
    )


def solution(mesh):
    rows = P("dp", "seq", None)
    columns = P(None, ("dp", "seq"))
    middle = P(None, ("dp", "seq"), None)
    first = P(("dp", "seq"), None)
    weights = (columns, columns, columns, columns, middle, first, first, first, middle, middle, first, first)
    return jax.shard_map(
        functools.partial(on_device, mesh.shape["dp"], mesh.shape["seq"]),
        mesh=mesh,
        in_specs=(rows, rows, P("dp", None), P("dp", None), P("dp"), P("dp", None), P("dp", None))
        + weights
        + (rows, rows),
        out_specs=(rows, rows, rows, rows) + weights,
        check_vma=False,
    )
```

```python
import functools

import jax
import jax.numpy as jnp
from jax import lax
from jax.experimental import pallas as pl
from jax.experimental.pallas import tpu as pltpu
from jax.sharding import PartitionSpec as P

HEAD_DIM = 64
EPSILON = 1e-05
MASKED = -1000000000.0
BLOCK = 256
PAIR = 2 * HEAD_DIM
B16 = jnp.bfloat16
F32 = jnp.float32


def product(left, right):
    return jnp.dot(left, right, preferred_element_type=F32)


def product_tn(left, right):
    return lax.dot_general(left, right, (((0,), (0,)), ((), ())), preferred_element_type=F32)


def product_nt(left, right):
    return lax.dot_general(left, right, (((1,), (1,)), ((), ())), preferred_element_type=F32)


def column_sum(values):
    return jnp.sum(values.astype(F32), axis=0)


def norm_parts(hidden):
    centred = hidden - jnp.mean(hidden, axis=-1, keepdims=True)
    spread = jnp.mean(centred * centred, axis=-1, keepdims=True)
    scale = lax.rsqrt(spread + EPSILON)
    return centred * scale, scale


def layer_norm(hidden, gain_row, shift_row):
    return (norm_parts(hidden)[0] * gain_row + shift_row).astype(B16)


def norm_backward(hidden, gain_row, grad):
    unit, scale = norm_parts(hidden)
    weighted = grad * gain_row
    grad_hidden = scale * (
        weighted
        - jnp.mean(weighted, axis=-1, keepdims=True)
        - unit * jnp.mean(weighted * unit, axis=-1, keepdims=True)
    )
    return grad_hidden, jnp.sum(grad * unit, axis=0), jnp.sum(grad, axis=0)


def gelu_both(values):
    below = 0.5 * (1.0 + lax.erf(values * (0.5**0.5)))
    density = jnp.exp(-0.5 * values * values) * (0.5 / jnp.pi) ** 0.5
    return (values * below).astype(B16), (below + values * density).astype(B16)


def allowed_block(causal, kseg_ref, qseg, length, key_at, query_at):
    allowed = kseg_ref[key_at : key_at + BLOCK, :] == qseg
    if causal:
        keys = key_at + lax.broadcasted_iota(jnp.int32, (BLOCK, BLOCK), 0)
        queries = query_at + lax.broadcasted_iota(jnp.int32, (BLOCK, BLOCK), 1)
        allowed = allowed & (keys <= queries) & ((keys < length) | (keys == queries))
    return allowed


def head_lanes(head, shape):
    lane = lax.broadcasted_iota(jnp.int32, shape, 1)
    return (lane >= head * HEAD_DIM) & (lane < (head + 1) * HEAD_DIM)


def dot_nt(left, right):
    return lax.dot_general(left, right, (((1,), (1,)), ((), ())), preferred_element_type=F32)


def forward_kernel(causal, info_ref, q_ref, k_ref, v_ref, qseg_ref, kseg_ref, o_ref, lse_ref, vt_ref, s_ref, acc_ref, stat_ref):
    block = pl.program_id(1)
    blocks = k_ref.shape[0] // BLOCK
    length = info_ref[blocks * blocks]

    @pl.when(block == 0)
    def _():
        vt_ref[...] = v_ref[...].T

    qseg = qseg_ref[...]
    scaled = q_ref[...] * jnp.asarray(HEAD_DIM**-0.5, B16)
    zero = jnp.zeros_like(scaled)
    heads = [jnp.where(head_lanes(h, scaled.shape), scaled, zero) for h in range(2)]
    stat_ref[0:16, :] = jnp.full((16, BLOCK), -1e30, F32)
    stat_ref[16:32, :] = jnp.zeros((16, BLOCK), F32)
    acc_ref[...] = jnp.zeros_like(acc_ref)
    for j in range(blocks):

        @pl.when(info_ref[block * blocks + j] > 0)
        def _(j=j):
            keys = k_ref[j * BLOCK : (j + 1) * BLOCK, :]
            allowed = allowed_block(causal, kseg_ref, qseg, length, j * BLOCK, block * BLOCK)
            for h in range(2):
                scores = jnp.where(allowed, dot_nt(keys, heads[h]), MASKED)
                s_ref[h, j * BLOCK : (j + 1) * BLOCK, :] = scores
                top = jnp.max(scores.reshape(BLOCK // 8, 8, BLOCK), axis=0)
                stat_ref[h * 8 : h * 8 + 8, :] = jnp.maximum(stat_ref[h * 8 : h * 8 + 8, :], top)

    highest = [jnp.max(stat_ref[h * 8 : h * 8 + 8, :], axis=0, keepdims=True) for h in range(2)]
    for j in range(blocks):

        @pl.when(info_ref[block * blocks + j] > 0)
        def _(j=j):
            for h in range(2):
                weights = jnp.exp(s_ref[h, j * BLOCK : (j + 1) * BLOCK, :] - highest[h])
                total = jnp.sum(weights.reshape(BLOCK // 8, 8, BLOCK), axis=0)
                stat_ref[16 + h * 8 : 24 + h * 8, :] += total
                rows = pl.ds(h * HEAD_DIM, HEAD_DIM)
                acc_ref[rows, :] += jnp.dot(
                    vt_ref[rows, j * BLOCK : (j + 1) * BLOCK],
                    weights.astype(B16),
                    preferred_element_type=F32,
                )

    lse_ref[...] = jnp.zeros_like(lse_ref)
    for h in range(2):
        total = jnp.sum(stat_ref[16 + h * 8 : 24 + h * 8, :], axis=0, keepdims=True)
        rows = pl.ds(h * HEAD_DIM, HEAD_DIM)
        acc_ref[rows, :] = acc_ref[rows, :] / total
        lse_ref[0, h : h + 1, :] = highest[h] + jnp.log(total)
    o_ref[...] = acc_ref[...].T.astype(B16)


def backward_kernel(
    causal,
    info_ref,
    q_ref,
    k_ref,
    v_ref,
    o_ref,
    do_ref,
    lse_ref,
    qseg_ref,
    kseg_ref,
    dq_ref,
    dk_ref,
    dv_ref,
    kt_ref,
    dqt_ref,
    sums_ref,
):
    block = pl.program_id(1)
    blocks = k_ref.shape[0] // BLOCK
    length = info_ref[blocks * blocks]

    @pl.when(block == 0)
    def _():
        kt_ref[...] = k_ref[...].T
        sums_ref[...] = jnp.zeros_like(sums_ref)

    qseg = qseg_ref[...]
    scaled = q_ref[...] * jnp.asarray(HEAD_DIM**-0.5, B16)
    grads = do_ref[...]
    zero = jnp.zeros_like(scaled)
    lanes = [head_lanes(h, scaled.shape) for h in range(2)]
    query_heads = [jnp.where(lanes[h], scaled, zero) for h in range(2)]
    grad_heads = [jnp.where(lanes[h], grads, zero) for h in range(2)]
    mixed = grads.astype(F32) * o_ref[...].astype(F32)
    picks = jnp.concatenate(
        [head_lanes(h, (8, PAIR)).astype(F32) for h in range(2)], axis=0
    )
    inner_both = lax.dot_general(
        picks, mixed, (((1,), (1,)), ((), ())), precision=lax.Precision.HIGHEST, preferred_element_type=F32
    )
    inner = [inner_both[8 * h : 8 * h + 1, :] for h in range(2)]
    lse = [lse_ref[0, h : h + 1, :] for h in range(2)]
    dqt_ref[...] = jnp.zeros_like(dqt_ref)
    for j in range(blocks):

        @pl.when(info_ref[block * blocks + j] > 0)
        def _(j=j):
            rows = slice(j * BLOCK, (j + 1) * BLOCK)
            keys = k_ref[rows, :]
            values = v_ref[rows, :]
            allowed = allowed_block(causal, kseg_ref, qseg, length, j * BLOCK, block * BLOCK)
            key_sum = sums_ref[0, rows, :]
            value_sum = sums_ref[1, rows, :]
            for h in range(2):
                scores = dot_nt(keys, query_heads[h])
                chances = jnp.where(allowed, jnp.exp(scores - lse[h]), 0.0)
                grad_chances = dot_nt(values, grad_heads[h])
                grad_scores = (chances * (grad_chances - inner[h])).astype(B16)
                value_sum += jnp.dot(chances.astype(B16), grad_heads[h], preferred_element_type=F32)
                key_sum += jnp.dot(grad_scores, query_heads[h], preferred_element_type=F32)
                part = pl.ds(h * HEAD_DIM, HEAD_DIM)
                dqt_ref[part, :] += jnp.dot(kt_ref[part, rows], grad_scores, preferred_element_type=F32)
            sums_ref[0, rows, :] = key_sum
            sums_ref[1, rows, :] = value_sum

    dq_ref[...] = (dqt_ref[...].T * HEAD_DIM**-0.5).astype(B16)

    @pl.when(block == blocks - 1)
    def _():
        dk_ref[...] = sums_ref[0].astype(B16)
        dv_ref[...] = sums_ref[1].astype(B16)


def block_info(causal, query_seg, key_seg, length):
    blocks = query_seg.shape[0] // BLOCK
    query_low, query_high = query_seg[::BLOCK], query_seg[BLOCK - 1 :: BLOCK]
    key_low, key_high = key_seg[::BLOCK], key_seg[BLOCK - 1 :: BLOCK]
    meets = (key_low[None, :] <= query_high[:, None]) & (key_high[None, :] >= query_low[:, None])
    if causal:
        at = jnp.arange(blocks)
        meets = meets & (at[None, :] <= at[:, None])
    return jnp.concatenate([meets.astype(jnp.int32).reshape(-1), length[None]])


def attention_specs(count, offsets):
    query = pl.BlockSpec((BLOCK, PAIR), lambda p, i, info: (i, p + offsets[0]))
    key = pl.BlockSpec((count, PAIR), lambda p, i, info: (0, p + offsets[1]))
    value = pl.BlockSpec((count, PAIR), lambda p, i, info: (0, p + offsets[2]))
    plain = pl.BlockSpec((BLOCK, PAIR), lambda p, i, info: (i, p))
    whole = pl.BlockSpec((count, PAIR), lambda p, i, info: (0, p))
    stats = pl.BlockSpec((1, 8, BLOCK), lambda p, i, info: (p, 0, i))
    qseg = pl.BlockSpec((1, BLOCK), lambda p, i, info: (0, i))
    kseg = pl.BlockSpec((count, 1), lambda p, i, info: (0, 0))
    return query, key, value, plain, whole, stats, qseg, kseg


def attend_forward(causal, masks, queries, keys, values, offsets, width):
    info, qseg_row, kseg_column = masks
    count = queries.shape[0]
    pairs = width // PAIR
    query, key, value, plain, _, stats, qseg, kseg = attention_specs(count, offsets)
    return pl.pallas_call(
        functools.partial(forward_kernel, causal),
        grid_spec=pltpu.PrefetchScalarGridSpec(
            num_scalar_prefetch=1,
            grid=(pairs, count // BLOCK),
            in_specs=[query, key, value, qseg, kseg],
            out_specs=[plain, stats],
            scratch_shapes=[pltpu.VMEM((PAIR, count), B16), pltpu.VMEM((2, count, BLOCK), F32), pltpu.VMEM((PAIR, BLOCK), F32), pltpu.VMEM((32, BLOCK), F32)],
        ),
        out_shape=[
            jax.ShapeDtypeStruct((count, width), B16),
            jax.ShapeDtypeStruct((pairs, 8, count), F32),
        ],
        compiler_params=pltpu.CompilerParams(vmem_limit_bytes=24 * 2**20),
        cost_estimate=pl.CostEstimate(
            flops=2 * 2 * count * count * width * 2, bytes_accessed=count * width * 8, transcendentals=0
        ),
        name="attend_causal" if causal else "attend",
    )(info, queries, keys, values, qseg_row, kseg_column)


def attend_backward(causal, masks, queries, keys, values, offsets, width, mixed, lse, grad):
    info, qseg_row, kseg_column = masks
    count = queries.shape[0]
    pairs = width // PAIR
    query, key, value, plain, whole, stats, qseg, kseg = attention_specs(count, offsets)
    return pl.pallas_call(
        functools.partial(backward_kernel, causal),
        grid_spec=pltpu.PrefetchScalarGridSpec(
            num_scalar_prefetch=1,
            grid=(pairs, count // BLOCK),
            in_specs=[query, key, value, plain, plain, stats, qseg, kseg],
            out_specs=[plain, whole, whole],
            scratch_shapes=[
                pltpu.VMEM((PAIR, count), B16),
                pltpu.VMEM((PAIR, BLOCK), F32),
                pltpu.VMEM((2, count, PAIR), F32),
            ],
        ),
        out_shape=[jax.ShapeDtypeStruct((count, width), B16)] * 3,
        compiler_params=pltpu.CompilerParams(vmem_limit_bytes=24 * 2**20),
        cost_estimate=pl.CostEstimate(
            flops=5 * 2 * count * count * width * 2, bytes_accessed=count * width * 16, transcendentals=0
        ),
        name="attend_grad_causal" if causal else "attend_grad",
    )(info, queries, keys, values, mixed, grad, lse, qseg_row, kseg_column)


MESH = pl.DeviceIdType.MESH


def own_columns(array, core, runs=8):
    split = array.reshape(array.shape[:-1] + (runs // 2, 2, array.shape[-1] // runs))
    mine = lax.dynamic_index_in_dim(split, core, split.ndim - 2, keepdims=False)
    return mine.reshape(array.shape[:-1] + (array.shape[-1] // 2,))


def lay_side(array):
    return jnp.concatenate([array[i] for i in range(array.shape[0])], axis=1)


def xor_arrange(pieces, place):
    pieces, bit = list(pieces), 0
    while 1 << bit < len(pieces):
        odd = ((place >> bit) & 1) == 1
        pieces = [jnp.where(odd, pieces[k ^ (1 << bit)], pieces[k]) for k in range(len(pieces))]
        bit += 1
    return pieces


class Here:
    def __init__(self):
        self.at = lax.axis_index("dp")
        self.z = lax.axis_index("seq")
        self.c = self.at % 2
        self.x = (self.at // 2) % 2
        self.y = self.at // 4
        self.core_peer = (self.at + 1 - 2 * self.c, self.z)
        self.x_peer = (self.at + 2 - 4 * self.x, self.z)
        self.y_peer = (self.at + 4 - 8 * self.y, self.z)

    def z_flip(self, j):
        return (self.z // 2 + j // 2) % 2 * 2 + (self.z % 2 + j % 2) % 2

    def z_peer(self, j):
        return (self.at, self.z_flip(j))

    def enter(self):
        barrier = pltpu.get_barrier_semaphore()
        peers = [self.x_peer, self.y_peer, self.core_peer]
        other = self.at + 1 - 2 * self.c
        for j in range(1, 4):
            peers += [(self.at, self.z_flip(j)), (other, self.z_flip(j))]
        for peer in peers:
            pl.semaphore_signal(barrier, inc=1, device_id=peer, device_id_type=MESH)
        pl.semaphore_wait(barrier, len(peers))


def remote(source, target, send_sem, recv_sem, peer):
    return pltpu.make_async_remote_copy(
        src_ref=source,
        dst_ref=target,
        send_sem=send_sem,
        recv_sem=recv_sem,
        device_id=peer,
        device_id_type=MESH,
    )


class GatherItem:
    def __init__(self, here, mine, other, out, send, recv, local):
        self.here, self.mine, self.other, self.out = here, mine, other, out
        self.send, self.recv, self.local = send, recv, local
        self.half = out.shape[-1] // 2
        self.core = here.c if other is not None else 0
        self.copies = {}

    def go(self, slot, region, peer):
        self.copies[slot] = remote(region, region, self.send.at[slot], self.recv.at[slot], peer)
        self.copies[slot].start()

    def begin(self):
        here = self.here
        block = self.out.at[here.y, here.x, self.core, here.z]
        self.own = pltpu.make_async_copy(self.mine, block, self.local)
        self.own.start()
        if self.other is not None:
            self.copies[0] = remote(self.other, block, self.send.at[0], self.recv.at[0], here.core_peer)
            self.copies[0].start()

    def stage_z(self):
        here = self.here
        self.own.wait()
        if self.other is not None:
            self.copies[0].wait_recv()
        for j in range(1, 4):
            self.go(j, self.out.at[here.y, here.x, :, here.z], here.z_peer(j))

    def stage_one(self):
        here, h = self.here, self.half
        for j in range(1, 4):
            self.copies[j].wait_recv()
        self.go(4, self.out.at[here.y, here.x, :, :, :, pl.ds(0, h)], here.x_peer)
        self.go(5, self.out.at[here.y, here.x, :, :, :, pl.ds(h, h)], here.y_peer)

    def stage_two(self):
        here, h = self.here, self.half
        self.copies[4].wait_recv()
        self.go(6, self.out.at[here.y, :, :, :, :, pl.ds(0, h)], here.y_peer)
        self.copies[5].wait_recv()
        self.go(7, self.out.at[:, here.x, :, :, :, pl.ds(h, h)], here.x_peer)

    def finish(self):
        self.copies[6].wait_recv()
        self.copies[7].wait_recv()
        for copy in self.copies.values():
            copy.wait_send()


class RowIn:
    def __init__(self, here, source, out, send, recv, local):
        self.here, self.source, self.out = here, source, out
        self.send, self.recv, self.local = send, recv, local
        self.half = source.shape[-1] // 2

    def lanes(self, f):
        return pl.ds(f * self.half, self.half) if isinstance(f, int) else pl.ds(pl.multiple_of(f * self.half, 128), self.half)

    def parts(self):
        here = self.here
        for i in range(2):
            for f in range(2):
                source = self.source.at[i, :, self.lanes(f)]
                target = self.out.at[here.z, :, self.lanes(f)]
                self_sent = (2 * here.c + i == here.z) & (here.c == f)
                peer = (here.at - here.c + f, 2 * here.c + i)
                away = remote(source, target, self.send.at[2 * i + f], self.recv.at[here.z], peer)
                stay = pltpu.make_async_copy(source, target, self.local)
                yield self_sent, away, stay

    def begin(self):
        for self_sent, away, stay in self.parts():
            pl.when(self_sent)(stay.start)
            pl.when(jnp.logical_not(self_sent))(away.start)

    def across(self):
        here = self.here
        lanes = self.lanes(here.c)
        for k in range(4):
            target = self.out.at[k, :, lanes]
            from_self = (here.z == k) & (here.z // 2 == here.c)
            stay = pltpu.make_async_copy(target, target, self.local)
            away = remote(target, target, self.send.at[0], self.recv.at[k], here.core_peer)
            pl.when(from_self)(stay.wait)
            pl.when(jnp.logical_not(from_self))(away.wait_recv)
        region = self.out.at[:, :, lanes]
        self.copy = remote(region, region, self.send.at[4], self.recv.at[4], here.core_peer)
        self.copy.start()

    def finish(self):
        self.copy.wait()
        for self_sent, away, _ in self.parts():
            pl.when(jnp.logical_not(self_sent))(away.wait_send)


def gather_kernel(kinds, rows_at, refs):
    here = Here()
    refs = list(refs)
    take = lambda n: [refs.pop(0) for _ in range(n)]
    count = len(kinds)
    ins = [take(2) if columns else take(1) + [None] for columns in kinds]
    row_ins = take(len(rows_at))
    outs = take(count)
    row_outs = take(len(rows_at))
    send, recv, local, row_send, row_recv, row_local = refs
    items = [
        GatherItem(here, mine, other, outs[k], send.at[k], recv.at[k], local.at[k])
        for k, (mine, other) in enumerate(ins)
    ]
    rows = [
        RowIn(here, row_ins[t], row_outs[t], row_send.at[t], row_recv.at[t], row_local.at[t])
        for t in range(len(rows_at))
    ]
    here.enter()
    for item in items:
        item.begin()
    for step in range(count + 3):
        for t, start in enumerate(rows_at):
            if start == step:
                rows[t].begin()
            if start + 1 == step:
                rows[t].across()
        if step < count:
            items[step].stage_z()
        if 0 <= step - 1 < count:
            items[step - 1].stage_one()
        if 0 <= step - 2 < count:
            items[step - 2].stage_two()
        if 0 <= step - 3 < count:
            items[step - 3].finish()
    for row in rows:
        row.finish()


def gather_all(locals_, rows, rows_at):
    kinds = [other is not None for _, other in locals_]
    inputs = [v for pair in locals_ for v in pair if v is not None] + list(rows)
    shapes = [
        jax.ShapeDtypeStruct((2, 2, 2 if other is not None else 1, 4) + mine.shape, mine.dtype)
        for mine, other in locals_
    ] + [jax.ShapeDtypeStruct((4,) + row.shape[1:], row.dtype) for row in rows]
    count, tensors = len(kinds), len(rows)
    hbm = pl.BlockSpec(memory_space=pl.ANY)

    def kernel(*refs):
        gather_kernel(kinds, rows_at, refs)

    dma = pltpu.SemaphoreType.DMA
    return pl.pallas_call(
        kernel,
        in_specs=[hbm] * len(inputs),
        out_specs=[hbm] * len(shapes),
        out_shape=shapes,
        scratch_shapes=[
            dma((count, 8)),
            dma((count, 8)),
            dma((count,)),
            dma((tensors, 5)),
            dma((tensors, 5)),
            dma((tensors,)),
        ],
        compiler_params=pltpu.CompilerParams(collective_id=0, has_side_effects=True),
        name="gather_all",
    )(*inputs)


class SumItem:
    def __init__(self, here, source, out, scratch, send, recv, local):
        self.here, self.source, self.out = here, source, out
        self.own, self.b1, self.b2, self.b3 = scratch[:4]
        self.columns = source.shape[2] == 2
        if self.columns:
            self.b4, self.b4s = scratch[4:]
        self.send, self.recv, self.local = send, recv, local
        self.half = source.shape[-1] // 2
        self.sides = ((pl.ds(0, self.half)), (pl.ds(self.half, self.half)))
        self.copies = {}

    def go(self, slot, source, target, peer):
        self.copies[slot] = remote(source, target, self.send.at[slot], self.recv.at[slot], peer)
        self.copies[slot].start()

    def blocks(self, body):
        cores = self.b2.shape[0]

        def step(k, carry):
            body(k // 4, k % 4)
            return carry

        lax.fori_loop(0, cores * 4, step, 0)

    def stage_one(self):
        here, (a, b), source = self.here, self.sides, self.source
        self.go(0, source.at[:, 1 - here.x, :, :, :, a], self.b1.at[:, :, :, :, a], here.x_peer)
        self.go(1, source.at[1 - here.y, :, :, :, :, b], self.b1.at[:, :, :, :, b], here.y_peer)
        self.loads = [
            pltpu.make_async_copy(source.at[:, here.x, :, :, :, a], self.own.at[:, :, :, :, a], self.local.at[0]),
            pltpu.make_async_copy(source.at[here.y, :, :, :, :, b], self.own.at[:, :, :, :, b], self.local.at[1]),
        ]
        for load in self.loads:
            load.start()

    def stage_two(self):
        here = self.here
        for side, near, peer in ((0, here.y, here.y_peer), (1, here.x, here.x_peer)):
            lanes = self.sides[side]
            away = 1 - near
            self.loads[side].wait()
            self.copies[side].wait_recv()

            def add(c, z, away=away, lanes=lanes):
                total = self.own[away, c, z, :, lanes].astype(F32) + self.b1[away, c, z, :, lanes].astype(F32)
                self.own[away, c, z, :, lanes] = total.astype(self.own.dtype)

            self.blocks(add)
            self.go(2 + side, self.own.at[away, :, :, :, lanes], self.b2.at[:, :, :, lanes], peer)

    def stage_three(self):
        here = self.here
        for side, near in ((0, here.y), (1, here.x)):
            lanes = self.sides[side]
            self.copies[2 + side].wait_recv()

            def add(c, z, near=near, lanes=lanes):
                total = self.own[near, c, z, :, lanes].astype(F32) + self.b1[near, c, z, :, lanes].astype(F32)
                total = total + self.b2[c, z, :, lanes].astype(F32)
                self.b2[c, z, :, lanes] = total.astype(self.b2.dtype)

            self.blocks(add)
        for j in range(1, 4):
            self.go(3 + j, self.b2.at[:, here.z_flip(j)], self.b3.at[j - 1], here.z_peer(j))

    def total(self, c):
        total = self.b2[c, self.here.z].astype(F32)
        for j in range(3):
            total = total + self.b3[j, c].astype(F32)
        return total

    def stage_four(self):
        here = self.here
        for j in range(1, 4):
            self.copies[3 + j].wait_recv()
        if self.columns:
            self.b4s[...] = self.total(1 - here.c).astype(self.b4s.dtype)
            self.go(7, self.b4s, self.b4, here.core_peer)
            self.out[here.c] = self.total(here.c)
        else:
            self.out[...] = self.total(0)

    def finish(self):
        if self.columns:
            self.copies[7].wait_recv()
            self.out[1 - self.here.c] = self.b4[...].astype(F32)
        for copy in self.copies.values():
            copy.wait_send()


class RowOut:
    def __init__(self, here, source, out, send, recv, local):
        self.here, self.source, self.out = here, source, out
        self.send, self.recv, self.local = send, recv, local
        self.half = source.shape[-1] // 2

    def parts(self):
        here = self.here
        lanes = pl.ds(pl.multiple_of(here.c * self.half, 128), self.half)
        for k in range(4):
            source = self.source.at[k, :, lanes]
            target = self.out.at[here.z % 2, :, lanes]
            self_sent = (here.z == k) & (here.z // 2 == here.c)
            peer = (here.at - here.c + here.z // 2, k)
            away = remote(source, target, self.send.at[k], self.recv.at[here.z % 2 * 2 + here.c], peer)
            yield self_sent, away, pltpu.make_async_copy(source, target, self.local)

    def begin(self):
        for self_sent, away, stay in self.parts():
            pl.when(self_sent)(stay.start)
            pl.when(jnp.logical_not(self_sent))(away.start)

    def finish(self):
        here = self.here
        for i in range(2):
            for f in range(2):
                target = self.out.at[i, :, pl.ds(f * self.half, self.half)]
                from_self = (2 * here.c + i == here.z) & (here.c == f)
                away = remote(target, target, self.send.at[0], self.recv.at[2 * i + f], here.core_peer)
                stay = pltpu.make_async_copy(target, target, self.local)
                pl.when(from_self)(stay.wait)
                pl.when(jnp.logical_not(from_self))(away.wait_recv)
        for self_sent, away, _ in self.parts():
            pl.when(jnp.logical_not(self_sent))(away.wait_send)


def sum_kernel(column_flags, tensors, refs):
    here = Here()
    refs = list(refs)
    take = lambda n: [refs.pop(0) for _ in range(n)]
    count = len(column_flags)
    sources, row_sources = take(count), take(tensors)
    outs, row_outs = take(count), take(tensors)
    scratch = [take(6 if columns else 4) for columns in column_flags]
    send, recv, local, row_send, row_recv, row_local = refs
    items = [
        SumItem(here, sources[k], outs[k], scratch[k], send.at[k], recv.at[k], local.at[k]) for k in range(count)
    ]
    rows = [
        RowOut(here, row_sources[t], row_outs[t], row_send.at[t], row_recv.at[t], row_local.at[t])
        for t in range(tensors)
    ]
    here.enter()
    for step in range(count + 4):
        if step < count:
            items[step].stage_one()
        if 0 <= step - 1 < count:
            items[step - 1].stage_two()
        if 0 <= step - 2 < count:
            items[step - 2].stage_three()
        if 0 <= step - 3 < count:
            items[step - 3].stage_four()
        if 0 <= step - 4 < count:
            items[step - 4].finish()
        if step < 2 * tensors and step % 2 == 0:
            rows[step // 2].begin()
    for row in rows:
        row.finish()


def sum_all(grads, rows):
    flags = [grad.shape[2] == 2 for grad in grads]
    hbm = pl.BlockSpec(memory_space=pl.ANY)
    vmem = pl.BlockSpec(memory_space=pltpu.VMEM)
    shapes, scratch = [], []
    for grad, columns in zip(grads, flags):
        _, _, cores, places, r, n = grad.shape
        shapes.append(jax.ShapeDtypeStruct((2, r, n) if columns else (r, n), F32))
        sizes = [(2, cores, places, r, n)] * 2 + [(cores, places, r, n), (3, cores, r, n)]
        sizes += [(r, n)] * 2 if columns else []
        scratch += [pltpu.VMEM(size, grad.dtype) for size in sizes]
    count, tensors = len(grads), len(rows)
    row_shapes = [jax.ShapeDtypeStruct((2,) + row.shape[1:], row.dtype) for row in rows]

    def kernel(*refs):
        sum_kernel(flags, tensors, refs)

    dma = pltpu.SemaphoreType.DMA
    return pl.pallas_call(
        kernel,
        in_specs=[hbm] * (count + tensors),
        out_specs=[vmem] * count + [hbm] * tensors,
        out_shape=shapes + row_shapes,
        scratch_shapes=scratch
        + [
            dma((count, 8)),
            dma((count, 8)),
            dma((count, 2)),
            dma((tensors, 4)),
            dma((tensors, 4)),
            dma((tensors,)),
        ],
        compiler_params=pltpu.CompilerParams(
            collective_id=1, has_side_effects=True, vmem_limit_bytes=60 * 2**20
        ),
        name="sum_all",
    )(*grads, *rows)


class Place:
    def __init__(self, dp, seq):
        self.dp, self.seq = dp, seq
        self.at = lax.axis_index("dp")
        self.z = lax.axis_index("seq")
        self.core = self.at % 2

    def over_core(self, value):
        return lax.ppermute(value, "dp", [(i, i ^ 1) for i in range(self.dp)])

    def both_cores(self, part):
        part = part.astype(B16)
        return part.astype(F32) + self.over_core(part).astype(F32)


class Tree:
    def __init__(self, place):
        self.place = place

    def gather(self, flat, columns, rows, tensors, tensors_at):
        core = self.place.core
        padded = jnp.pad(flat, (0, -flat.shape[0] % 4096)).reshape(16, -1)
        locals_ = {-1: (padded, padded)}
        for key, value in columns.items():
            locals_[key] = (lay_side(own_columns(value, core)), lay_side(own_columns(value, 1 - core)))
        for key, value in rows.items():
            locals_[key] = (value, None)
        keys = sorted(locals_)
        outs = gather_all([locals_[key] for key in keys], tensors, tensors_at)
        whole = {key: out for key, out in zip(keys, outs)}
        small = whole.pop(-1).reshape(32, -1)[:, : flat.shape[0]]
        weights = {key: value.reshape(-1, value.shape[-1]) for key, value in whole.items()}
        return small, weights, [out.reshape(-1, out.shape[-1]) for out in outs[len(keys) :]]

    def sums(self, columns, rows, table, hidden, tensors):
        n, m = table.shape[0], hidden.shape[0]
        both = jnp.concatenate(
            [
                table.reshape(n, 2, 2, 4, -1).transpose(1, 2, 3, 0, 4).reshape(2, 2, 4, -1),
                hidden.reshape(m, 2, 2, 4, -1).transpose(1, 2, 3, 0, 4).reshape(2, 2, 4, -1),
            ],
            axis=-1,
        )
        size = both.shape[-1]
        both = jnp.pad(both, ((0, 0), (0, 0), (0, 0), (0, -size % 2048))).reshape(2, 2, 1, 4, 8, -1)
        grads, keys = [], []
        for key, (features, grad, _) in columns.items():
            value = product_tn(features, grad).astype(B16)
            grads.append(value.reshape(2, 2, 2, 4, value.shape[0] // 32, value.shape[1]))
            keys.append(key)
        for key, (features, grad) in rows.items():
            value = product_tn(features, grad).astype(B16)
            grads.append(value.reshape(2, 2, 1, 4, value.shape[0] // 16, value.shape[1]))
            keys.append(key)
        order = sorted(range(len(keys)), key=lambda k: keys[k])
        outs = sum_all([grads[k] for k in order] + [both], [t.reshape(4, -1, t.shape[-1]) for t in tensors])
        result = {}
        for k, out in zip(order, outs):
            key = keys[k]
            if key in columns:
                parts, r = columns[key][2], out.shape[1]
                result[key] = out.reshape(2, r, parts, 4, -1).transpose(2, 1, 3, 0, 4).reshape(parts, r, -1)
            else:
                result[key] = out
        flat = outs[len(keys)].reshape(-1)[:size]
        edge = table.shape[1] // 16 * n
        return result, flat[:edge].reshape(n, -1), flat[edge:].reshape(m, -1), outs[len(keys) + 1 :]


class Plain:
    def __init__(self, place):
        self.place = place
        self.axes = ("dp", "seq")

    def row_in(self, array):
        place = self.place
        parts = array.reshape(2, array.shape[1], 2, -1)
        got = []
        for m in range(4):
            code = place.z ^ m
            piece = lax.dynamic_index_in_dim(parts, code // 2, 0, keepdims=False)
            piece = lax.dynamic_index_in_dim(piece, code % 2, 1, keepdims=False)
            moves = []
            for d in range(place.dp):
                for z in range(4):
                    q = m ^ z
                    moves.append((d * 4 + z, (d - d % 2 + q % 2) * 4 + 2 * (d % 2) + q // 2))
            got.append(lax.ppermute(piece, self.axes, moves))
        half = jnp.concatenate(xor_arrange(got, (place.z % 2) * 2 + place.core), axis=0)
        return jnp.concatenate(xor_arrange([half, place.over_core(half)], place.core), axis=1)

    def row_out(self, row):
        place = self.place
        parts = row.reshape(4, -1, 2, row.shape[1] // 2)
        mine = lax.dynamic_index_in_dim(parts, place.core, 2, keepdims=False)
        q_here = (place.z % 2) * 2 + place.core
        got = []
        for m in range(4):
            piece = lax.dynamic_index_in_dim(mine, q_here ^ m, 0, keepdims=False)
            moves = []
            for d in range(place.dp):
                for z in range(4):
                    q = (z % 2) * 2 + d % 2
                    moves.append((d * 4 + z, (d - d % 2 + z // 2) * 4 + (m ^ q)))
            got.append(lax.ppermute(piece, self.axes, moves))
        placed = xor_arrange(got, place.z)
        return jnp.stack([jnp.concatenate(placed[2 * i : 2 * i + 2], axis=1) for i in range(2)])

    def gather(self, flat, columns, rows, tensors, tensors_at):
        small = lax.all_gather(flat, self.axes, axis=0, tiled=False)
        weights = {}
        for key, value in columns.items():
            full = lax.all_gather(value, self.axes, axis=1, tiled=True)
            weights[key] = lay_side(own_columns(full, self.place.core))
        for key, value in rows.items():
            full = lax.all_gather(value, self.axes, axis=0, tiled=True)
            split = full.reshape(4, 2, full.shape[0] // 8, full.shape[1])
            mine = lax.dynamic_index_in_dim(split, self.place.core, 1, keepdims=False)
            weights[key] = mine.reshape(-1, full.shape[1])
        return small, weights, [self.row_in(tensor) for tensor in tensors]

    def spread(self, half, axis):
        shape = half.shape[:axis] + (4, 1, half.shape[axis] // 4) + half.shape[axis + 1 :]
        half = half.reshape(shape)
        empty = jnp.zeros_like(half)
        first = jnp.where(self.place.core == 0, half, empty)
        second = jnp.where(self.place.core == 1, half, empty)
        both = jnp.concatenate([first, second], axis=axis + 1)
        return both.reshape(shape[:axis] + (-1,) + shape[axis + 3 :])

    def scatter(self, value, axis):
        return lax.psum_scatter(value, self.axes, scatter_dimension=axis, tiled=True).astype(F32)

    def sums(self, columns, rows, table, hidden, tensors):
        result = {}
        for key, (features, grad, parts) in columns.items():
            full = product_tn(features, grad)
            full = full.reshape(full.shape[0], parts, -1).transpose(1, 0, 2).astype(B16)
            result[key] = self.scatter(self.spread(full, 2), 1)
        for key, (features, grad) in rows.items():
            result[key] = self.scatter(self.spread(product_tn(features, grad).astype(B16), 0), 0)
        small = [self.scatter(self.spread(v, 1), 1) for v in (table, hidden)]
        return result, small[0], small[1], [self.row_out(tensor) for tensor in tensors]


def on_device(
    dp,
    seq,
    src_x,
    tgt_x,
    src_seg,
    tgt_seg,
    tgt_len,
    src_lang,
    tgt_lang,
    lang_table,
    gains,
    biases,
    ff_biases,
    enc_proj,
    enc_oproj,
    enc_in,
    enc_out,
    dec_proj,
    dec_oproj,
    dec_in,
    dec_out,
    src_cot,
    tgt_cot,
):
    place = Place(dp, seq)
    core = place.core
    moves = Tree(place) if (dp, seq) == (8, 4) else Plain(place)
    width = enc_oproj.shape[1]
    half = width // 2
    langs = lang_table.shape[0]

    n_small = langs + gains.shape[0] + biases.shape[0]
    table = jnp.concatenate([lang_table, gains, biases], axis=0)
    flat = jnp.concatenate([table.reshape(-1), ff_biases.reshape(-1)])
    edge = table.size
    everything, weights, tensors = moves.gather(
        flat,
        {0: enc_proj, 2: enc_in[None], 4: dec_proj[0:3], 6: dec_proj[3:6], 8: dec_in[None]},
        {1: enc_oproj, 3: enc_out, 5: dec_oproj[0], 7: dec_oproj[1], 9: dec_out},
        [src_x, tgt_x, tgt_cot, src_cot],
        [0, 3, 5, 7],
    )
    source, target, target_cot, source_cot = tensors
    enc_qkv_w, enc_o_w, enc_in_w, enc_out_w, dec_qkv_w, dec_o_w, cross_w, cross_o_w, dec_in_w, dec_out_w = (
        weights[k] for k in range(10)
    )
    table = everything[:, :edge].reshape(dp * seq, n_small, -1).transpose(1, 0, 2).reshape(n_small, width)
    ffb = everything[:, edge:].reshape(dp * seq, 2, -1).transpose(1, 0, 2).reshape(2, -1)
    languages = table[:langs]
    gain_f = table[langs : langs + gains.shape[0]].astype(F32)
    bias_f = table[langs + gains.shape[0] :].astype(F32)
    ffb_own = own_columns(ffb.astype(F32), core)
    bias_own = own_columns(bias_f, core)

    meta = jnp.concatenate([src_seg, tgt_seg, tgt_len[:, None], src_lang, tgt_lang], axis=1)
    rows = jnp.where(place.z // 2 == core, meta, place.over_core(meta))
    row = lax.dynamic_index_in_dim(rows, place.z % 2, 0, keepdims=False)
    count, segs = src_seg.shape[1], src_lang.shape[1]
    s_seg, t_seg, t_len = row[:count], row[count : 2 * count], row[2 * count]
    s_lang, t_lang = row[2 * count + 1 : 2 * count + 1 + segs], row[2 * count + 1 + segs :]

    def onehot(segments, chosen):
        member = segments[:, None] == jnp.arange(segs, dtype=jnp.int32)[None, :]
        token = jnp.sum(jnp.where(member, chosen[None, :], 0), axis=1)
        return (token[:, None] == jnp.arange(langs, dtype=jnp.int32)[None, :]).astype(B16)

    src_hot, tgt_hot = onehot(s_seg, s_lang), onehot(t_seg, t_lang)
    enc_masks = (block_info(False, s_seg, s_seg, t_len), s_seg[None, :], s_seg[:, None])
    dec_masks = (block_info(True, t_seg, t_seg, t_len), t_seg[None, :], t_seg[:, None])
    cross_masks = (block_info(False, t_seg, s_seg, t_len), t_seg[None, :], s_seg[:, None])

    none = jnp.zeros((half,), F32)
    packed = (0, half // PAIR, 2 * half // PAIR)

    enc_h0 = source.astype(F32) + product(src_hot, languages)
    enc_n1 = layer_norm(enc_h0, gain_f[0], bias_f[0])
    enc_qkv_bias = jnp.concatenate([bias_own[1], none, bias_own[2]])
    enc_qkv = (product(enc_n1, enc_qkv_w) + enc_qkv_bias).astype(B16)
    enc_mixed, enc_lse = attend_forward(False, enc_masks, enc_qkv, enc_qkv, enc_qkv, packed, half)
    enc_h1 = enc_h0 + place.both_cores(product(enc_mixed, enc_o_w)) + bias_f[3]
    enc_n2 = layer_norm(enc_h1, gain_f[1], bias_f[4])
    enc_acted, enc_slope = gelu_both(product(enc_n2, enc_in_w) + ffb_own[0])
    encoded = enc_h1 + place.both_cores(product(enc_acted, enc_out_w)) + bias_f[5]
    memory = encoded.astype(B16)

    dec_h0 = target.astype(F32) + product(tgt_hot, languages)
    dec_n1 = layer_norm(dec_h0, gain_f[2], bias_f[6])
    dec_qkv_bias = jnp.concatenate([bias_own[7], none, bias_own[8]])
    dec_qkv = (product(dec_n1, dec_qkv_w) + dec_qkv_bias).astype(B16)
    dec_mixed, dec_lse = attend_forward(True, dec_masks, dec_qkv, dec_qkv, dec_qkv, packed, half)
    dec_h1 = dec_h0 + place.both_cores(product(dec_mixed, dec_o_w)) + bias_f[9]
    dec_n2 = layer_norm(dec_h1, gain_f[3], bias_f[10])
    cross_q = (product(dec_n2, cross_w[:, :half]) + bias_own[11]).astype(B16)
    cross_kv_bias = jnp.concatenate([none, bias_own[12]])
    cross_kv = (product(memory, cross_w[:, half:]) + cross_kv_bias).astype(B16)
    apart = (0, 0, half // PAIR)
    cross_mixed, cross_lse = attend_forward(False, cross_masks, cross_q, cross_kv, cross_kv, apart, half)
    dec_h2 = dec_h1 + place.both_cores(product(cross_mixed, cross_o_w)) + bias_f[13]
    dec_n3 = layer_norm(dec_h2, gain_f[4], bias_f[14])
    dec_acted, dec_slope = gelu_both(product(dec_n3, dec_in_w) + ffb_own[1])
    decoded = dec_h2 + place.both_cores(product(dec_acted, dec_out_w)) + bias_f[15]

    dec_du = (product_nt(target_cot, dec_out_w) * dec_slope.astype(F32)).astype(B16)
    dec_dn3 = place.both_cores(product_nt(dec_du, dec_in_w))
    target_cot_f = target_cot.astype(F32)
    step, gain_four, shift_14 = norm_backward(dec_h2, gain_f[4], dec_dn3)
    grad_h2 = target_cot_f + step

    cross_branch = grad_h2.astype(B16)
    cross_do = product_nt(cross_branch, cross_o_w).astype(B16)
    cross_dq, cross_dk, cross_dv = attend_backward(
        False, cross_masks, cross_q, cross_kv, cross_kv, apart, half, cross_mixed, cross_lse, cross_do
    )
    cross_dkv = jnp.concatenate([cross_dk, cross_dv], axis=1)
    grad_memory = place.both_cores(product_nt(cross_dkv, cross_w[:, half:]))
    dec_dn2 = place.both_cores(product_nt(cross_dq, cross_w[:, :half]))

    source_cot_f = source_cot.astype(F32) + grad_memory
    enc_ff_branch = source_cot_f.astype(B16)
    enc_du = (product_nt(enc_ff_branch, enc_out_w) * enc_slope.astype(F32)).astype(B16)
    enc_dn2 = place.both_cores(product_nt(enc_du, enc_in_w))

    step, gain_three, shift_10 = norm_backward(dec_h1, gain_f[3], dec_dn2)
    grad_h1 = grad_h2 + step
    self_branch = grad_h1.astype(B16)
    dec_do = product_nt(self_branch, dec_o_w).astype(B16)
    dec_dqkv = jnp.concatenate(
        attend_backward(
            True, dec_masks, dec_qkv, dec_qkv, dec_qkv, packed, half, dec_mixed, dec_lse, dec_do
        ),
        axis=1,
    )
    dec_dn1 = place.both_cores(product_nt(dec_dqkv, dec_qkv_w))
    step, gain_two, shift_6 = norm_backward(dec_h0, gain_f[2], dec_dn1)
    target_grad = grad_h1 + step

    step, gain_one, shift_4 = norm_backward(enc_h1, gain_f[1], enc_dn2)
    grad_e1 = source_cot_f + step
    enc_branch = grad_e1.astype(B16)
    enc_do = product_nt(enc_branch, enc_o_w).astype(B16)
    enc_dqkv = jnp.concatenate(
        attend_backward(
            False, enc_masks, enc_qkv, enc_qkv, enc_qkv, packed, half, enc_mixed, enc_lse, enc_do
        ),
        axis=1,
    )
    enc_dn1 = place.both_cores(product_nt(enc_dqkv, enc_qkv_w))
    step, gain_zero, shift_0 = norm_backward(enc_h0, gain_f[0], enc_dn1)
    source_grad = grad_e1 + step

    def split_two(value):
        high = value.astype(B16)
        return high, (value - high.astype(F32)).astype(B16)

    lang_grad = 0.0
    for hot, value in ((src_hot, source_grad), (tgt_hot, target_grad)):
        for piece in split_two(own_columns(value, core)):
            lang_grad = lang_grad + product_tn(hot, piece)
    own = functools.partial(own_columns, core=core)
    gain_rows = jnp.stack([gain_zero, gain_one, gain_two, gain_three, gain_four])
    enc_qkv_sum, dec_qkv_sum = column_sum(enc_dqkv), column_sum(dec_dqkv)
    bias_rows = jnp.stack(
        [
            own(shift_0),
            enc_qkv_sum[:half],
            enc_qkv_sum[2 * half :],
            own(column_sum(enc_branch)),
            own(shift_4),
            own(column_sum(enc_ff_branch)),
            own(shift_6),
            dec_qkv_sum[:half],
            dec_qkv_sum[2 * half :],
            own(column_sum(self_branch)),
            own(shift_10),
            column_sum(cross_dq),
            column_sum(cross_dv),
            own(column_sum(cross_branch)),
            own(shift_14),
            own(column_sum(target_cot)),
        ]
    )
    grads, small, ffb_grad, outputs = moves.sums(
        {
            0: (dec_n3, dec_du, 1),
            2: (dec_n2, cross_dq, 1),
            3: (memory, cross_dkv, 2),
            5: (enc_n2, enc_du, 1),
            7: (dec_n1, dec_dqkv, 3),
            9: (enc_n1, enc_dqkv, 3),
        },
        {
            1: (dec_acted, target_cot),
            4: (cross_mixed, cross_branch),
            6: (enc_acted, enc_ff_branch),
            8: (dec_mixed, self_branch),
            10: (enc_mixed, enc_branch),
        },
        jnp.concatenate([lang_grad, own(gain_rows), bias_rows], axis=0),
        jnp.stack([column_sum(enc_du), column_sum(dec_du)]),
        [memory, decoded.astype(B16), source_grad.astype(B16), target_grad.astype(B16)],
    )
    return (
        outputs[0],
        outputs[1],
        outputs[2].astype(F32),
        outputs[3].astype(F32),
        small[:langs],
        small[langs : langs + 5],
        small[langs + 5 :],
        ffb_grad,
        grads[9],
        grads[10],
        grads[5][0],
        grads[6],
        jnp.concatenate([grads[7], grads[2], grads[3]], axis=0),
        jnp.stack([grads[8], grads[4]]),
        grads[0][0],
        grads[1],
    )


def solution(mesh):
    rows = P("dp", "seq", None)
    columns = P(None, ("dp", "seq"))
    middle = P(None, ("dp", "seq"), None)
    first = P(("dp", "seq"), None)
    weights = (columns, columns, columns, columns, middle, first, first, first, middle, middle, first, first)
    return jax.shard_map(
        functools.partial(on_device, mesh.shape["dp"], mesh.shape["seq"]),
        mesh=mesh,
        in_specs=(rows, rows, P("dp", None), P("dp", None), P("dp"), P("dp", None), P("dp", None))
        + weights
        + (rows, rows),
        out_specs=(rows, rows, rows, rows) + weights,
        check_vma=False,
    )
```

```python
import functools

import jax
import jax.numpy as jnp
from jax import lax
from jax.experimental import pallas as pl
from jax.experimental.pallas import tpu as pltpu
from jax.sharding import Mesh
from jax.sharding import PartitionSpec as P

HEAD_DIM = 64
EPSILON = 1e-05
MASKED = -1000000000.0
BLOCK = 256
HEADS = 4
GROUP = HEADS * HEAD_DIM
B16 = jnp.bfloat16
F32 = jnp.float32


def product(left, right):
    return jnp.dot(left, right, preferred_element_type=F32)


def product_tn(left, right):
    return lax.dot_general(left, right, (((0,), (0,)), ((), ())), preferred_element_type=F32)


def product_nt(left, right):
    return lax.dot_general(left, right, (((1,), (1,)), ((), ())), preferred_element_type=F32)


def column_sum(values):
    return jnp.sum(values.astype(F32), axis=0)


def norm_parts(hidden):
    centred = hidden - jnp.mean(hidden, axis=-1, keepdims=True)
    spread = jnp.mean(centred * centred, axis=-1, keepdims=True)
    scale = lax.rsqrt(spread + EPSILON)
    return centred * scale, scale


def layer_norm(hidden, gain_row, shift_row):
    return (norm_parts(hidden)[0] * gain_row + shift_row).astype(B16)


def norm_backward(hidden, gain_row, grad):
    unit, scale = norm_parts(hidden)
    weighted = grad * gain_row
    grad_hidden = scale * (
        weighted
        - jnp.mean(weighted, axis=-1, keepdims=True)
        - unit * jnp.mean(weighted * unit, axis=-1, keepdims=True)
    )
    return grad_hidden, jnp.sum(grad * unit, axis=0), jnp.sum(grad, axis=0)


def gelu_both(values):
    below = 0.5 * (1.0 + lax.erf(values * (0.5**0.5)))
    density = jnp.exp(-0.5 * values * values) * (0.5 / jnp.pi) ** 0.5
    return (values * below).astype(B16), (below + values * density).astype(B16)


def allowed_block(causal, kseg_ref, qseg, length, key_at, query_at):
    allowed = kseg_ref[key_at : key_at + BLOCK, :] == qseg
    if causal:
        keys = key_at + lax.broadcasted_iota(jnp.int32, (BLOCK, BLOCK), 0)
        queries = query_at + lax.broadcasted_iota(jnp.int32, (BLOCK, BLOCK), 1)
        allowed = allowed & (keys <= queries) & ((keys < length) | (keys == queries))
    return allowed


def dot_nt(left, right):
    return lax.dot_general(left, right, (((1,), (1,)), ((), ())), preferred_element_type=F32)


def head_masked(value):
    lane = lax.broadcasted_iota(jnp.int32, value.shape, 1) // HEAD_DIM
    zero = jnp.zeros_like(value)
    return [jnp.where(lane == h, value, zero) for h in range(HEADS)]


def fold_rows(value, combine):
    return combine(value.reshape(value.shape[0] // 8, 8, value.shape[1]), axis=0)


def forward_kernel(
    causal, info_ref, q_ref, k_ref, v_ref, qseg_ref, kseg_ref, o_ref, lse_ref, vt_ref, s_ref, acc_ref, top_ref, sum_ref
):
    block = pl.program_id(1)
    blocks = k_ref.shape[0] // BLOCK
    length = info_ref[blocks * blocks]

    @pl.when(block == 0)
    def _():
        vt_ref[...] = v_ref[...].T

    qseg = qseg_ref[...]
    heads = head_masked(q_ref[...] * jnp.asarray(HEAD_DIM**-0.5, B16))
    top_ref[...] = jnp.full(top_ref.shape, -1e30, F32)
    sum_ref[...] = jnp.zeros_like(sum_ref)
    acc_ref[...] = jnp.zeros_like(acc_ref)
    for j in range(blocks):

        @pl.when(info_ref[block * blocks + j] > 0)
        def _(j=j):
            keys = k_ref[j * BLOCK : (j + 1) * BLOCK, :]
            allowed = allowed_block(causal, kseg_ref, qseg, length, j * BLOCK, block * BLOCK)
            for h in range(HEADS):
                scores = jnp.where(allowed, dot_nt(keys, heads[h]), MASKED)
                s_ref[h, j * BLOCK : (j + 1) * BLOCK, :] = scores
                top_ref[h] = jnp.maximum(top_ref[h], fold_rows(scores, jnp.max))

    highest = [jnp.max(top_ref[h], axis=0, keepdims=True) for h in range(HEADS)]
    for j in range(blocks):

        @pl.when(info_ref[block * blocks + j] > 0)
        def _(j=j):
            for h in range(HEADS):
                weights = jnp.exp(s_ref[h, j * BLOCK : (j + 1) * BLOCK, :] - highest[h])
                sum_ref[h] += fold_rows(weights, jnp.sum)
                rows = slice(h * HEAD_DIM, (h + 1) * HEAD_DIM)
                acc_ref[rows, :] += jnp.dot(
                    vt_ref[rows, j * BLOCK : (j + 1) * BLOCK],
                    weights.astype(B16),
                    preferred_element_type=F32,
                )

    lse_ref[...] = jnp.zeros_like(lse_ref)
    for h in range(HEADS):
        total = jnp.sum(sum_ref[h], axis=0, keepdims=True)
        rows = slice(h * HEAD_DIM, (h + 1) * HEAD_DIM)
        acc_ref[rows, :] = acc_ref[rows, :] / total
        lse_ref[0, h : h + 1, :] = highest[h] + jnp.log(total)
    o_ref[...] = acc_ref[...].T.astype(B16)


def backward_kernel(
    causal,
    info_ref,
    q_ref,
    k_ref,
    v_ref,
    o_ref,
    do_ref,
    lse_ref,
    qseg_ref,
    kseg_ref,
    *rest,
):
    *outs, kt_ref, dqt_ref, sums_ref, done_ref, sems = rest
    group, block = pl.program_id(0), pl.program_id(1)
    groups = pl.num_programs(0)
    blocks = k_ref.shape[0] // BLOCK
    length = info_ref[blocks * blocks]

    @pl.when(block == 0)
    def _():
        kt_ref[...] = k_ref[...].T
        sums_ref[...] = jnp.zeros_like(sums_ref)

    qseg = qseg_ref[...]
    grads = do_ref[...]
    query_heads = head_masked(q_ref[...] * jnp.asarray(HEAD_DIM**-0.5, B16))
    grad_heads = head_masked(grads)
    queries_down = jnp.concatenate(query_heads, axis=0)
    grads_down = jnp.concatenate(grad_heads, axis=0)
    mixed = grads.astype(F32) * o_ref[...].astype(F32)
    lane = lax.broadcasted_iota(jnp.int32, (8, GROUP), 1) // HEAD_DIM
    picks = (lane == lax.broadcasted_iota(jnp.int32, (8, GROUP), 0)).astype(F32)
    inner = lax.dot_general(
        picks, mixed, (((1,), (1,)), ((), ())), precision=lax.Precision.HIGHEST, preferred_element_type=F32
    )
    dqt_ref[...] = jnp.zeros_like(dqt_ref)
    for j in range(blocks):

        @pl.when(info_ref[block * blocks + j] > 0)
        def _(j=j):
            rows = slice(j * BLOCK, (j + 1) * BLOCK)
            keys = k_ref[rows, :]
            values = v_ref[rows, :]
            allowed = allowed_block(causal, kseg_ref, qseg, length, j * BLOCK, block * BLOCK)
            all_chances, all_scores = [], []
            for h in range(HEADS):
                scores = dot_nt(keys, query_heads[h])
                chances = jnp.where(allowed, jnp.exp(scores - lse_ref[0, h : h + 1, :]), 0.0)
                grad_chances = dot_nt(values, grad_heads[h])
                grad_scores = (chances * (grad_chances - inner[h : h + 1, :])).astype(B16)
                all_chances.append(chances.astype(B16))
                all_scores.append(grad_scores)
                part = slice(h * HEAD_DIM, (h + 1) * HEAD_DIM)
                dqt_ref[part, :] += jnp.dot(kt_ref[part, rows], grad_scores, preferred_element_type=F32)
            sums_ref[0, rows, :] += jnp.dot(
                jnp.concatenate(all_scores, axis=1), queries_down, preferred_element_type=F32
            )
            sums_ref[1, rows, :] += jnp.dot(
                jnp.concatenate(all_chances, axis=1), grads_down, preferred_element_type=F32
            )

    here = pl.ds(pl.multiple_of(block * BLOCK, BLOCK), BLOCK)
    done_ref[0, here, :] = (dqt_ref[...].T * HEAD_DIM**-0.5).astype(B16)

    @pl.when(block == blocks - 1)
    def _():
        done_ref[1] = sums_ref[0].astype(B16)
        done_ref[2] = sums_ref[1].astype(B16)
        width = k_ref.shape[1]
        copies = []
        for k in range(3):
            out, place = (outs[0], k) if len(outs) == 1 else (outs[min(k, 1)], max(k - 1, 0))
            lanes = pl.ds(pl.multiple_of((place * groups + group) * width, width), width)
            copies.append(pltpu.make_async_copy(done_ref.at[k], out.at[:, lanes], sems.at[k]))
        for copy in copies:
            copy.start()
        for copy in copies:
            copy.wait()


def block_info(causal, query_seg, key_seg, length):
    blocks = query_seg.shape[0] // BLOCK
    query_low, query_high = query_seg[::BLOCK], query_seg[BLOCK - 1 :: BLOCK]
    key_low, key_high = key_seg[::BLOCK], key_seg[BLOCK - 1 :: BLOCK]
    meets = (key_low[None, :] <= query_high[:, None]) & (key_high[None, :] >= query_low[:, None])
    if causal:
        at = jnp.arange(blocks)
        meets = meets & (at[None, :] <= at[:, None])
    return jnp.concatenate([meets.astype(jnp.int32).reshape(-1), length[None]])


def attention_specs(count, offsets):
    query = pl.BlockSpec((BLOCK, GROUP), lambda p, i, info: (i, p + offsets[0]))
    key = pl.BlockSpec((count, GROUP), lambda p, i, info: (0, p + offsets[1]))
    value = pl.BlockSpec((count, GROUP), lambda p, i, info: (0, p + offsets[2]))
    plain = pl.BlockSpec((BLOCK, GROUP), lambda p, i, info: (i, p))
    whole = pl.BlockSpec((count, GROUP), lambda p, i, info: (0, p))
    stats = pl.BlockSpec((1, 8, BLOCK), lambda p, i, info: (p, 0, i))
    qseg = pl.BlockSpec((1, BLOCK), lambda p, i, info: (0, i))
    kseg = pl.BlockSpec((count, 1), lambda p, i, info: (0, 0))
    return query, key, value, plain, whole, stats, qseg, kseg


def attend_forward(causal, masks, queries, keys, values, offsets, width):
    info, qseg_row, kseg_column = masks
    count = queries.shape[0]
    groups = width // GROUP
    query, key, value, plain, _, stats, qseg, kseg = attention_specs(count, offsets)
    return pl.pallas_call(
        functools.partial(forward_kernel, causal),
        grid_spec=pltpu.PrefetchScalarGridSpec(
            num_scalar_prefetch=1,
            grid=(groups, count // BLOCK),
            in_specs=[query, key, value, qseg, kseg],
            out_specs=[plain, stats],
            scratch_shapes=[pltpu.VMEM((GROUP, count), B16), pltpu.VMEM((HEADS, count, BLOCK), F32), pltpu.VMEM((GROUP, BLOCK), F32)]
            + [pltpu.VMEM((HEADS, 8, BLOCK), F32)] * 2,
        ),
        out_shape=[
            jax.ShapeDtypeStruct((count, width), B16),
            jax.ShapeDtypeStruct((groups, 8, count), F32),
        ],
        compiler_params=pltpu.CompilerParams(vmem_limit_bytes=24 * 2**20),
        cost_estimate=pl.CostEstimate(
            flops=2 * 2 * count * count * width * 2, bytes_accessed=count * width * 8, transcendentals=0
        ),
        name="attend_causal" if causal else "attend",
    )(info, queries, keys, values, qseg_row, kseg_column)


def attend_backward(causal, masks, queries, keys, values, offsets, width, mixed, lse, grad):
    widths = (3 * width,) if queries is keys else (width, 2 * width)
    info, qseg_row, kseg_column = masks
    count = queries.shape[0]
    groups = width // GROUP
    query, key, value, plain, _, stats, qseg, kseg = attention_specs(count, offsets)
    return pl.pallas_call(
        functools.partial(backward_kernel, causal),
        grid_spec=pltpu.PrefetchScalarGridSpec(
            num_scalar_prefetch=1,
            grid=(groups, count // BLOCK),
            in_specs=[query, key, value, plain, plain, stats, qseg, kseg],
            out_specs=[pl.BlockSpec(memory_space=pl.ANY)] * len(widths),
            scratch_shapes=[
                pltpu.VMEM((GROUP, count), B16),
                pltpu.VMEM((GROUP, BLOCK), F32),
                pltpu.VMEM((2, count, GROUP), F32),
                pltpu.VMEM((3, count, GROUP), B16),
                pltpu.SemaphoreType.DMA((3,)),
            ],
        ),
        out_shape=[jax.ShapeDtypeStruct((count, w), B16) for w in widths],
        compiler_params=pltpu.CompilerParams(vmem_limit_bytes=24 * 2**20),
        cost_estimate=pl.CostEstimate(
            flops=5 * 2 * count * count * width * 2, bytes_accessed=count * width * 16, transcendentals=0
        ),
        name="attend_grad_causal" if causal else "attend_grad",
    )(info, queries, keys, values, mixed, grad, lse, qseg_row, kseg_column)


MESH = pl.DeviceIdType.MESH
GATHER_LAGS = (0, 1, 2, 3)
ROW_LAG = 4
SUM_CUT = 20
SUM_ROWS = [1, 3, 5, 7]


def own_columns(array, core, runs=8):
    split = array.reshape(array.shape[:-1] + (runs // 2, 2, array.shape[-1] // runs))
    mine = lax.dynamic_index_in_dim(split, core, split.ndim - 2, keepdims=False)
    return mine.reshape(array.shape[:-1] + (array.shape[-1] // 2,))


def lay_side(array):
    return jnp.concatenate([array[i] for i in range(array.shape[0])], axis=1)


def lay_wide(arrays):
    return arrays[0] if len(arrays) == 1 else jnp.concatenate(arrays, axis=1)


def xor_arrange(pieces, place):
    pieces, bit = list(pieces), 0
    while 1 << bit < len(pieces):
        odd = ((place >> bit) & 1) == 1
        pieces = [jnp.where(odd, pieces[k ^ (1 << bit)], pieces[k]) for k in range(len(pieces))]
        bit += 1
    return pieces


class Here:
    def __init__(self):
        self.at = lax.axis_index("dp")
        self.c = lax.axis_index("core")
        self.z = lax.axis_index("seq")
        self.x = self.at % 2
        self.y = self.at // 2
        self.core_peer = (self.at, 1 - self.c, self.z)
        self.x_peer = (self.at + 1 - 2 * self.x, self.c, self.z)
        self.y_peer = (self.at + 2 - 4 * self.y, self.c, self.z)
        self.edge = (self.z % 3) == 0
        self.inner = jnp.logical_not(self.edge)

    def z_flip(self, j):
        return (self.z // 2 + j // 2) % 2 * 2 + (self.z % 2 + j % 2) % 2

    def z_peer(self, j):
        return (self.at, self.c, self.z_flip(j))

    def enter(self):
        barrier = pltpu.get_barrier_semaphore()
        peers = [self.x_peer, self.y_peer, self.core_peer]
        for j in range(1, 4):
            peers += [(self.at, self.c, self.z_flip(j)), (self.at, 1 - self.c, self.z_flip(j))]
        for peer in peers:
            pl.semaphore_signal(barrier, inc=1, device_id=peer, device_id_type=MESH)
        pl.semaphore_wait(barrier, len(peers))


def remote(source, target, send_sem, recv_sem, peer):
    return pltpu.make_async_remote_copy(
        src_ref=source,
        dst_ref=target,
        send_sem=send_sem,
        recv_sem=recv_sem,
        device_id=peer,
        device_id_type=MESH,
    )


class GatherItem:
    def __init__(self, here, mine, other, out, start, size, send, recv, local):
        self.here, self.mine, self.other, self.out = here, mine, other, out
        self.send, self.recv, self.local = send, recv, local
        self.all = pl.ds(start, size)
        self.sides = pl.ds(start, size // 2), pl.ds(start + size // 2, size // 2)
        self.core = here.c if other is not None else 0
        self.copies = {}

    def move(self, slot, region, peer, arrive=None):
        recv = self.recv.at[slot if arrive is None else arrive]
        self.copies[slot] = remote(region, region, self.send.at[slot], recv, peer)
        return self.copies[slot]

    def begin(self):
        here = self.here
        block = self.out.at[here.y, here.x, self.core, here.z, :, self.all]
        self.own = pltpu.make_async_copy(self.mine.at[:, self.all], block, self.local)
        self.own.start()
        if self.other is not None:
            other = self.other.at[:, self.all]
            self.copies[0] = remote(other, block, self.send.at[0], self.recv.at[0], here.core_peer)
            self.copies[0].start()

    def stage_z(self):
        here = self.here
        self.own.wait()
        if self.other is not None:
            self.copies[0].wait_recv()
        block = self.out.at[here.y, here.x, :, here.z, :, self.all]
        self.move(1, block, here.z_peer(1)).start()
        self.move(2, block, here.z_peer(2)).start()
        pl.when(here.inner)(self.move(3, block, here.z_peer(3)).start)

    def stage_pass(self):
        here = self.here
        self.copies[2].wait_recv()
        block = self.out.at[here.y, here.x, :, here.z_flip(2), :, self.all]
        pl.when(here.inner)(self.move(8, block, here.z_peer(1), arrive=3).start)

    def stage_one(self):
        here, (a, b) = self.here, self.sides
        self.copies[1].wait_recv()
        self.copies[3].wait_recv()
        self.move(4, self.out.at[here.y, here.x, :, :, :, a], here.x_peer).start()
        self.move(5, self.out.at[here.y, here.x, :, :, :, b], here.y_peer).start()

    def stage_two(self):
        here, (a, b) = self.here, self.sides
        self.copies[4].wait_recv()
        self.move(6, self.out.at[here.y, :, :, :, :, a], here.y_peer).start()
        self.copies[5].wait_recv()
        self.move(7, self.out.at[:, here.x, :, :, :, b], here.x_peer).start()

    def finish(self):
        self.copies[6].wait_recv()
        self.copies[7].wait_recv()
        for slot, copy in self.copies.items():
            if slot in (3, 8):
                pl.when(self.here.inner)(copy.wait_send)
            else:
                copy.wait_send()


class RowIn:
    def __init__(self, here, source, out, send, recv, local):
        self.here, self.source, self.out = here, source, out
        self.send, self.recv, self.local = send, recv, local
        self.half = source.shape[-1] // 2

    def lanes(self, f):
        return pl.ds(f * self.half, self.half) if isinstance(f, int) else pl.ds(pl.multiple_of(f * self.half, 128), self.half)

    def parts(self):
        here = self.here
        for i in range(2):
            for f in range(2):
                source = self.source.at[i, :, self.lanes(f)]
                target = self.out.at[here.z, :, self.lanes(f)]
                self_sent = (2 * here.c + i == here.z) & (here.c == f)
                peer = (here.at, f, 2 * here.c + i)
                away = remote(source, target, self.send.at[2 * i + f], self.recv.at[here.z], peer)
                stay = pltpu.make_async_copy(source, target, self.local)
                yield self_sent, away, stay

    def begin(self):
        for self_sent, away, stay in self.parts():
            pl.when(self_sent)(stay.start)
            pl.when(jnp.logical_not(self_sent))(away.start)

    def across(self):
        here = self.here
        lanes = self.lanes(here.c)
        for k in range(4):
            target = self.out.at[k, :, lanes]
            from_self = (here.z == k) & (here.z // 2 == here.c)
            stay = pltpu.make_async_copy(target, target, self.local)
            away = remote(target, target, self.send.at[0], self.recv.at[k], here.core_peer)
            pl.when(from_self)(stay.wait)
            pl.when(jnp.logical_not(from_self))(away.wait_recv)
        region = self.out.at[:, :, lanes]
        self.copy = remote(region, region, self.send.at[4], self.recv.at[4], here.core_peer)
        self.copy.start()

    def finish(self):
        self.copy.wait()
        for self_sent, away, _ in self.parts():
            pl.when(jnp.logical_not(self_sent))(away.wait_send)


def gather_kernel(kinds, cuts, rows_at, refs):
    here = Here()
    refs = list(refs)
    take = lambda n: [refs.pop(0) for _ in range(n)]
    count = len(kinds)
    ins = [take(2) if columns else take(1) + [None] for columns in kinds]
    row_ins = take(len(rows_at))
    outs = take(count)
    row_outs = take(len(rows_at))
    send, recv, local, row_send, row_recv, row_local = refs
    items = []
    for k, (mine, other) in enumerate(ins):
        size = mine.shape[-1] // cuts[k]
        for cut in range(cuts[k]):
            n = len(items)
            items.append(
                GatherItem(here, mine, other, outs[k], cut * size, size, send.at[n], recv.at[n], local.at[n])
            )
    count = len(items)
    rows = [
        RowIn(here, row_ins[t], row_outs[t], row_send.at[t], row_recv.at[t], row_local.at[t])
        for t in range(len(rows_at))
    ]
    here.enter()
    for item in items:
        item.begin()
    steps = (GatherItem.stage_z, GatherItem.stage_pass, GatherItem.stage_one, GatherItem.stage_two)
    for step in range(count + GATHER_LAGS[-1] + 1):
        for t, start in enumerate(rows_at):
            if start == step:
                rows[t].begin()
            if min(start + ROW_LAG, count + GATHER_LAGS[-1]) == step:
                rows[t].across()
        for stage, lag in zip(steps, GATHER_LAGS):
            if 0 <= step - lag < count:
                stage(items[step - lag])
    for item in items:
        item.finish()
    for row in rows:
        row.finish()


def gather_all(locals_, rows, rows_at):
    kinds = [other is not None for _, other in locals_]
    inputs = [v for pair in locals_ for v in pair if v is not None] + list(rows)
    shapes = [
        jax.ShapeDtypeStruct((2, 2, 2 if other is not None else 1, 4) + mine.shape, mine.dtype)
        for mine, other in locals_
    ] + [jax.ShapeDtypeStruct((4,) + row.shape[1:], row.dtype) for row in rows]
    cuts = [2 if mine.size * (1 + columns) > 2**17 else 1 for (mine, _), columns in zip(locals_, kinds)]
    count, tensors = sum(cuts), len(rows)
    hbm = pl.BlockSpec(memory_space=pl.ANY)

    def kernel(*refs):
        gather_kernel(kinds, cuts, rows_at, refs)

    dma = pltpu.SemaphoreType.DMA
    return pl.pallas_call(
        kernel,
        in_specs=[hbm] * len(inputs),
        out_specs=[hbm] * len(shapes),
        out_shape=shapes,
        scratch_shapes=[
            dma((count, 9)),
            dma((count, 9)),
            dma((count,)),
            dma((tensors, 5)),
            dma((tensors, 5)),
            dma((tensors,)),
        ],
        compiler_params=pltpu.CompilerParams(collective_id=0, has_side_effects=True),
        name="gather_all",
    )(*inputs)


class SumItem:
    def __init__(self, here, source, out, start, scratch, send, recv, local):
        self.here, self.source, self.out = here, source, out
        self.own, self.b1, self.b2, self.b3, self.met = scratch[:5]
        self.columns = source.shape[2] == 2
        if self.columns:
            self.b4, self.b4s = scratch[5:]
        self.send, self.recv, self.local = send, recv, local
        size = self.own.shape[-1]
        self.half = size // 2
        self.sides = pl.ds(0, self.half), pl.ds(self.half, self.half)
        self.cut = slice(start, start + size)
        self.source_sides = pl.ds(start, self.half), pl.ds(start + self.half, self.half)
        self.copies = {}

    def make(self, slot, source, target, peer):
        self.copies[slot] = remote(source, target, self.send.at[slot], self.recv.at[slot], peer)
        return self.copies[slot]

    def go(self, slot, source, target, peer):
        self.make(slot, source, target, peer).start()

    def blocks(self, body):
        cores = self.b2.shape[0]

        def step(k, carry):
            body(k // 4, k % 4)
            return carry

        lax.fori_loop(0, cores * 4, step, 0)

    def stage_one(self):
        here, (a, b), source = self.here, self.sides, self.source
        first, second = self.source_sides
        self.go(0, source.at[:, 1 - here.x, :, :, :, first], self.b1.at[:, :, :, :, a], here.x_peer)
        self.go(1, source.at[1 - here.y, :, :, :, :, second], self.b1.at[:, :, :, :, b], here.y_peer)
        self.loads = [
            pltpu.make_async_copy(source.at[:, here.x, :, :, :, first], self.own.at[:, :, :, :, a], self.local.at[0]),
            pltpu.make_async_copy(source.at[here.y, :, :, :, :, second], self.own.at[:, :, :, :, b], self.local.at[1]),
        ]
        for load in self.loads:
            load.start()

        @pl.when(here.edge)
        def _():
            self.b3[2] = jnp.zeros(self.b3.shape[1:], self.b3.dtype)

    def stage_two(self):
        here = self.here
        for side, near, peer in ((0, here.y, here.y_peer), (1, here.x, here.x_peer)):
            lanes = self.sides[side]
            away = 1 - near
            self.loads[side].wait()
            self.copies[side].wait_recv()

            def add(c, z, away=away, lanes=lanes):
                total = self.own[away, c, z, :, lanes].astype(F32) + self.b1[away, c, z, :, lanes].astype(F32)
                self.own[away, c, z, :, lanes] = total.astype(self.own.dtype)

            self.blocks(add)
            self.go(2 + side, self.own.at[away, :, :, :, lanes], self.b2.at[:, :, :, lanes], peer)

    def stage_three(self):
        here = self.here
        for side, near in ((0, here.y), (1, here.x)):
            lanes = self.sides[side]
            self.copies[2 + side].wait_recv()

            def add(c, z, near=near, lanes=lanes):
                total = self.own[near, c, z, :, lanes].astype(F32) + self.b1[near, c, z, :, lanes].astype(F32)
                total = total + self.b2[c, z, :, lanes].astype(F32)
                self.b2[c, z, :, lanes] = total.astype(self.b2.dtype)

            self.blocks(add)
        piece = lambda j: self.b2.at[:, here.z_flip(j)]
        self.go(4, piece(1), self.b3.at[0], here.z_peer(1))
        pl.when(here.edge)(self.make(5, piece(2), self.b3.at[1], here.z_peer(2)).start)
        pl.when(here.inner)(self.make(6, piece(3), self.b3.at[2], here.z_peer(3)).start)
        pl.when(here.edge)(self.make(8, piece(3), self.met, here.z_peer(1)).start)

    def stage_meet(self):
        here = self.here

        @pl.when(here.inner)
        def _():
            self.copies[8].wait_recv()
            for c in range(self.b2.shape[0]):
                place = here.z_flip(2)
                total = self.b2[c, place].astype(F32) + self.met[c].astype(F32)
                self.b2[c, place] = total.astype(self.b2.dtype)
            self.copies[5].start()

    def total(self, c):
        total = self.b2[c, self.here.z].astype(F32)
        for j in range(3):
            total = total + self.b3[j, c].astype(F32)
        return total

    def stage_four(self):
        here = self.here
        self.copies[4].wait_recv()
        self.copies[5].wait_recv()
        pl.when(here.inner)(self.copies[6].wait_recv)
        if self.columns:
            self.b4s[...] = self.total(1 - here.c).astype(self.b4s.dtype)
            self.go(7, self.b4s, self.b4, here.core_peer)
            self.out[here.c, :, self.cut] = self.total(here.c)
        else:
            self.out[:, self.cut] = self.total(0)

    def finish(self):
        if self.columns:
            self.copies[7].wait_recv()
            self.out[1 - self.here.c, :, self.cut] = self.b4[...].astype(F32)
        for slot, copy in self.copies.items():
            if slot == 6:
                pl.when(self.here.inner)(copy.wait_send)
            elif slot == 8:
                pl.when(self.here.edge)(copy.wait_send)
            else:
                copy.wait_send()


class RowOut:
    def __init__(self, here, source, out, send, recv, local):
        self.here, self.source, self.out = here, source, out
        self.send, self.recv, self.local = send, recv, local
        self.half = source.shape[-1] // 2

    def parts(self):
        here = self.here
        lanes = pl.ds(pl.multiple_of(here.c * self.half, 128), self.half)
        for k in range(4):
            source = self.source.at[k, :, lanes]
            target = self.out.at[here.z % 2, :, lanes]
            self_sent = (here.z == k) & (here.z // 2 == here.c)
            peer = (here.at, here.z // 2, k)
            away = remote(source, target, self.send.at[k], self.recv.at[here.z % 2 * 2 + here.c], peer)
            yield self_sent, away, pltpu.make_async_copy(source, target, self.local)

    def begin(self):
        for self_sent, away, stay in self.parts():
            pl.when(self_sent)(stay.start)
            pl.when(jnp.logical_not(self_sent))(away.start)

    def finish(self):
        here = self.here
        for i in range(2):
            for f in range(2):
                target = self.out.at[i, :, pl.ds(f * self.half, self.half)]
                from_self = (2 * here.c + i == here.z) & (here.c == f)
                away = remote(target, target, self.send.at[0], self.recv.at[2 * i + f], here.core_peer)
                stay = pltpu.make_async_copy(target, target, self.local)
                pl.when(from_self)(stay.wait)
                pl.when(jnp.logical_not(from_self))(away.wait_recv)
        for self_sent, away, _ in self.parts():
            pl.when(jnp.logical_not(self_sent))(away.wait_send)


def sum_kernel(column_flags, cuts, rows_at, refs):
    here = Here()
    refs = list(refs)
    take = lambda n: [refs.pop(0) for _ in range(n)]
    grads, tensors = len(column_flags), len(rows_at)
    sources, row_sources = take(grads), take(tensors)
    outs, row_outs = take(grads), take(tensors)
    scratch = [[take(7 if columns else 5) for _ in range(cut)] for columns, cut in zip(column_flags, cuts)]
    send, recv, local, row_send, row_recv, row_local = refs
    items = []
    for k in range(grads):
        for cut in range(cuts[k]):
            n, start = len(items), cut * (sources[k].shape[-1] // cuts[k])
            items.append(
                SumItem(here, sources[k], outs[k], start, scratch[k][cut], send.at[n], recv.at[n], local.at[n])
            )
    count = len(items)
    rows = [
        RowOut(here, row_sources[t], row_outs[t], row_send.at[t], row_recv.at[t], row_local.at[t])
        for t in range(tensors)
    ]
    here.enter()
    for step in range(count + 5):
        if step < count:
            items[step].stage_one()
        if 0 <= step - 1 < count:
            items[step - 1].stage_two()
        if 0 <= step - 2 < count:
            items[step - 2].stage_three()
        if 0 <= step - 3 < count:
            items[step - 3].stage_meet()
        if 0 <= step - 4 < count:
            items[step - 4].stage_four()
        if 0 <= step - 5 < count:
            items[step - 5].finish()
        for t, start in enumerate(rows_at):
            if start == step:
                rows[t].begin()
    for row in rows:
        row.finish()


def sum_all(grads, rows, rows_at):
    flags = [grad.shape[2] == 2 for grad in grads]
    hbm = pl.BlockSpec(memory_space=pl.ANY)
    vmem = pl.BlockSpec(memory_space=pltpu.VMEM)
    shapes, scratch, cuts = [], [], []
    for grad, columns in zip(grads, flags):
        _, _, cores, places, r, n = grad.shape
        shapes.append(jax.ShapeDtypeStruct((2, r, n) if columns else (r, n), F32))
        cuts.append(2 if grad.size > 2**SUM_CUT else 1)
        n = n // cuts[-1]
        sizes = [(2, cores, places, r, n)] * 2 + [(cores, places, r, n), (3, cores, r, n), (cores, r, n)]
        sizes += [(r, n)] * 2 if columns else []
        scratch += [pltpu.VMEM(size, grad.dtype) for size in sizes] * cuts[-1]
    count, tensors = sum(cuts), len(rows)
    row_shapes = [jax.ShapeDtypeStruct((2,) + row.shape[1:], row.dtype) for row in rows]

    def kernel(*refs):
        sum_kernel(flags, cuts, rows_at, refs)

    dma = pltpu.SemaphoreType.DMA
    return pl.pallas_call(
        kernel,
        in_specs=[hbm] * (len(grads) + tensors),
        out_specs=[vmem] * len(grads) + [hbm] * tensors,
        out_shape=shapes + row_shapes,
        scratch_shapes=scratch
        + [
            dma((count, 9)),
            dma((count, 9)),
            dma((count, 2)),
            dma((tensors, 4)),
            dma((tensors, 4)),
            dma((tensors,)),
        ],
        compiler_params=pltpu.CompilerParams(
            collective_id=1, has_side_effects=True, vmem_limit_bytes=60 * 2**20
        ),
        name="sum_all",
    )(*grads, *rows)


class Place:
    def __init__(self):
        self.core = lax.axis_index("core")
        self.z = lax.axis_index("seq")

    def over_core(self, value):
        return lax.ppermute(value, "core", [(0, 1), (1, 0)])

    def both_cores(self, part):
        part = part.astype(B16)
        return part.astype(F32) + self.over_core(part).astype(F32)


class Tree:
    def __init__(self, place):
        self.place = place

    def gather(self, flat, columns, rows, tensors, tensors_at):
        core = self.place.core
        padded = jnp.pad(flat, (0, -flat.shape[0] % 4096)).reshape(16, -1)
        locals_ = {-1: (padded, padded)}
        for key, value in columns.items():
            locals_[key] = (lay_side(own_columns(value, core)), lay_side(own_columns(value, 1 - core)))
        for key, value in rows.items():
            locals_[key] = (value, None)
        keys = sorted(locals_)
        outs = gather_all([locals_[key] for key in keys], tensors, tensors_at)
        whole = {key: out for key, out in zip(keys, outs)}
        small = whole.pop(-1).reshape(32, -1)[:, : flat.shape[0]]
        weights = {key: value.reshape(-1, value.shape[-1]) for key, value in whole.items()}
        return small, weights, [out.reshape(-1, out.shape[-1]) for out in outs[len(keys) :]]

    def gather_late(self, columns, rows, after):
        core = self.place.core
        mine, other = lay_side(own_columns(columns, core)), lay_side(own_columns(columns, 1 - core))
        both = jnp.stack(xor_arrange([mine, self.place.over_core(other)], core))
        both, rows, _ = lax.optimization_barrier((both, rows, after))
        full = lax.all_gather(both, ("dp", "seq"), axis=0, tiled=False)
        full = full.reshape((4, 4) + both.shape).transpose(0, 2, 1, 3, 4)
        return full.reshape(-1, full.shape[-1]), lax.all_gather(rows, ("dp", "seq"), axis=0, tiled=True)

    def early_columns(self, pairs, parts):
        core = self.place.core
        value = lay_wide([product_tn(features, grad).astype(B16) for features, grad in pairs])
        value = value.reshape(4, 2, 4, -1, value.shape[1]).transpose(0, 2, 1, 3, 4)
        value = value.reshape(16, -1, value.shape[-1])
        total = lax.psum_scatter(value, ("dp", "seq"), scatter_dimension=0, tiled=True)
        total = total.reshape(2, -1, total.shape[-1])
        mine = lax.dynamic_index_in_dim(total, core, 0, keepdims=False)
        other = lax.dynamic_index_in_dim(total, 1 - core, 0, keepdims=False)
        both = jnp.stack(xor_arrange([mine, self.place.over_core(other)], core))
        return self.weave(both, parts)

    def early_both(self, pairs, parts, features, grad):
        core = self.place.core
        values = [product_tn(f, g).astype(B16) for f, g in pairs]
        width = values[0].shape[1]
        cut = [v[:, k : k + width] for v in values for k in range(0, v.shape[1], width)]
        cut = [v.reshape(4, 2, 4, -1, width).transpose(0, 2, 1, 3, 4).reshape(16, -1, width) for v in cut]
        rows = product_tn(features, grad).astype(B16)
        rows = rows.reshape(16, -1, rows.shape[1])
        r = rows.shape[1]
        cut += [rows[:, :, k : k + width] for k in range(0, rows.shape[2], width)]
        total = lax.psum_scatter(jnp.concatenate(cut, axis=1), ("dp", "seq"), scatter_dimension=0, tiled=True)[0]
        columns, rest = total[: 2 * r * parts].reshape(parts, 2, r, width), total[2 * r * parts :]
        mine = lax.dynamic_index_in_dim(columns, core, 1, keepdims=False)
        other = lax.dynamic_index_in_dim(columns, 1 - core, 1, keepdims=False)
        both = jnp.stack(xor_arrange([mine, self.place.over_core(other)], core))
        both = both.astype(F32).reshape(2, parts, r, 4, -1).transpose(1, 2, 3, 0, 4).reshape(parts, r, -1)
        return both, rest.astype(F32).reshape(-1, r, width).transpose(1, 0, 2).reshape(r, -1)

    def early_rows(self, features, grad):
        value = product_tn(features, grad).astype(B16)
        return lax.psum_scatter(value, ("dp", "seq"), scatter_dimension=0, tiled=True).astype(F32)

    def weave(self, both, parts):
        r = both.shape[1]
        both = both.astype(F32).reshape(2, r, parts, 4, -1)
        return both.transpose(2, 1, 3, 0, 4).reshape(parts, r, -1)

    def sums(self, columns, rows, table, hidden, tensors):
        n, m = table.shape[0], hidden.shape[0]
        both = jnp.concatenate(
            [
                table.reshape(n, 2, 2, 4, -1).transpose(1, 2, 3, 0, 4).reshape(2, 2, 4, -1),
                hidden.reshape(m, 2, 2, 4, -1).transpose(1, 2, 3, 0, 4).reshape(2, 2, 4, -1),
            ],
            axis=-1,
        )
        size = both.shape[-1]
        both = jnp.pad(both, ((0, 0), (0, 0), (0, 0), (0, -size % 2048))).reshape(2, 2, 1, 4, 8, -1)
        grads, keys = [], []
        for key, (features, grad, _) in columns.items():
            value = product_tn(features, grad).astype(B16)
            grads.append(value.reshape(2, 2, 2, 4, value.shape[0] // 32, value.shape[1]))
            keys.append(key)
        for key, (features, grad) in rows.items():
            value = product_tn(features, grad).astype(B16)
            grads.append(value.reshape(2, 2, 1, 4, value.shape[0] // 16, value.shape[1]))
            keys.append(key)
        order = sorted(range(len(keys)), key=lambda k: keys[k])
        outs = sum_all([grads[k] for k in order] + [both], [t.reshape(4, -1, t.shape[-1]) for t in tensors], SUM_ROWS)
        result = {}
        for k, out in zip(order, outs):
            key = keys[k]
            if key in columns:
                result[key] = self.weave(out, columns[key][2])
            else:
                result[key] = out
        flat = outs[len(keys)].reshape(-1)[:size]
        edge = table.shape[1] // 16 * n
        return result, flat[:edge].reshape(n, -1), flat[edge:].reshape(m, -1), outs[len(keys) + 1 :]


class Plain:
    def __init__(self, place):
        self.place = place
        self.axes = ("dp", "core", "seq")

    def row_in(self, array):
        place = self.place
        parts = array.reshape(2, array.shape[1], 2, -1)
        got = []
        for m in range(4):
            code = place.z ^ m
            piece = lax.dynamic_index_in_dim(parts, code // 2, 0, keepdims=False)
            piece = lax.dynamic_index_in_dim(piece, code % 2, 1, keepdims=False)
            moves = []
            for c in range(2):
                for z in range(4):
                    q = m ^ z
                    moves.append((c * 4 + z, q % 2 * 4 + 2 * c + q // 2))
            got.append(lax.ppermute(piece, ("core", "seq"), moves))
        half = jnp.concatenate(xor_arrange(got, (place.z % 2) * 2 + place.core), axis=0)
        return jnp.concatenate(xor_arrange([half, place.over_core(half)], place.core), axis=1)

    def row_out(self, row):
        place = self.place
        parts = row.reshape(4, -1, 2, row.shape[1] // 2)
        mine = lax.dynamic_index_in_dim(parts, place.core, 2, keepdims=False)
        q_here = (place.z % 2) * 2 + place.core
        got = []
        for m in range(4):
            piece = lax.dynamic_index_in_dim(mine, q_here ^ m, 0, keepdims=False)
            moves = []
            for c in range(2):
                for z in range(4):
                    q = (z % 2) * 2 + c
                    moves.append((c * 4 + z, z // 2 * 4 + (m ^ q)))
            got.append(lax.ppermute(piece, ("core", "seq"), moves))
        placed = xor_arrange(got, place.z)
        return jnp.stack([jnp.concatenate(placed[2 * i : 2 * i + 2], axis=1) for i in range(2)])

    def gather(self, flat, columns, rows, tensors, tensors_at):
        small = lax.all_gather(flat, self.axes, axis=0, tiled=False)
        weights = {}
        for key, value in columns.items():
            weights[key] = self.whole_columns(value)
        for key, value in rows.items():
            weights[key] = self.whole_rows(value)
        return small, weights, [self.row_in(tensor) for tensor in tensors]

    def whole_columns(self, value):
        full = lax.all_gather(value, self.axes, axis=1, tiled=True)
        return lay_side(own_columns(full, self.place.core))

    def whole_rows(self, value):
        full = lax.all_gather(value, self.axes, axis=0, tiled=True)
        split = full.reshape(4, 2, full.shape[0] // 8, full.shape[1])
        mine = lax.dynamic_index_in_dim(split, self.place.core, 1, keepdims=False)
        return mine.reshape(-1, full.shape[1])

    def gather_late(self, columns, rows, after):
        return self.whole_columns(columns), self.whole_rows(rows)

    def early_columns(self, pairs, parts):
        full = lay_wide([product_tn(features, grad) for features, grad in pairs])
        full = full.reshape(full.shape[0], parts, -1).transpose(1, 0, 2).astype(B16)
        return self.scatter(self.spread(full, 2), 1)

    def early_both(self, pairs, parts, features, grad):
        return self.early_columns(pairs, parts), self.early_rows(features, grad)

    def early_rows(self, features, grad):
        return self.scatter(self.spread(product_tn(features, grad).astype(B16), 0), 0)

    def spread(self, half, axis):
        shape = half.shape[:axis] + (4, 1, half.shape[axis] // 4) + half.shape[axis + 1 :]
        half = half.reshape(shape)
        empty = jnp.zeros_like(half)
        first = jnp.where(self.place.core == 0, half, empty)
        second = jnp.where(self.place.core == 1, half, empty)
        both = jnp.concatenate([first, second], axis=axis + 1)
        return both.reshape(shape[:axis] + (-1,) + shape[axis + 3 :])

    def scatter(self, value, axis):
        return lax.psum_scatter(value, self.axes, scatter_dimension=axis, tiled=True).astype(F32)

    def sums(self, columns, rows, table, hidden, tensors):
        result = {}
        for key, (features, grad, parts) in columns.items():
            result[key] = self.early_columns([(features, grad)], parts)
        for key, (features, grad) in rows.items():
            result[key] = self.early_rows(features, grad)
        small = [self.scatter(self.spread(v, 1), 1) for v in (table, hidden)]
        return result, small[0], small[1], [self.row_out(tensor) for tensor in tensors]


def on_device(
    dp,
    seq,
    src_x,
    tgt_x,
    src_seg,
    tgt_seg,
    tgt_len,
    src_lang,
    tgt_lang,
    lang_table,
    gains,
    biases,
    ff_biases,
    enc_proj,
    enc_oproj,
    enc_in,
    enc_out,
    dec_proj,
    dec_oproj,
    dec_in,
    dec_out,
    src_cot,
    tgt_cot,
):
    place = Place()
    core = place.core
    moves = Tree(place) if (dp, seq) == (4, 4) else Plain(place)
    width = enc_oproj.shape[1]
    half = width // 2
    langs = lang_table.shape[0]

    n_small = langs + gains.shape[0] + biases.shape[0]
    table = jnp.concatenate([lang_table, gains, biases], axis=0)
    flat = jnp.concatenate([table.reshape(-1), ff_biases.reshape(-1)])
    edge = table.size
    everything, weights, tensors = moves.gather(
        flat,
        {0: enc_proj, 2: enc_in[None], 4: dec_proj[0:3], 6: dec_proj[3:6]},
        {1: enc_oproj, 3: enc_out, 5: dec_oproj[0], 7: dec_oproj[1]},
        [src_x, tgt_x, tgt_cot, src_cot],
        [2, 5, 8, 11],
    )
    source, target, target_cot, source_cot = tensors
    enc_qkv_w, enc_o_w, enc_in_w, enc_out_w, dec_qkv_w, dec_o_w, cross_w, cross_o_w = (
        weights[k] for k in range(8)
    )
    dec_in_w, dec_out_w = moves.gather_late(dec_in[None], dec_out, everything)
    table = everything[:, :edge].reshape(2 * dp * seq, n_small, -1).transpose(1, 0, 2).reshape(n_small, width)
    ffb = everything[:, edge:].reshape(2 * dp * seq, 2, -1).transpose(1, 0, 2).reshape(2, -1)
    languages = table[:langs]
    gain_f = table[langs : langs + gains.shape[0]].astype(F32)
    bias_f = table[langs + gains.shape[0] :].astype(F32)
    ffb_own = own_columns(ffb.astype(F32), core)
    bias_own = own_columns(bias_f, core)

    meta = jnp.concatenate([src_seg, tgt_seg, tgt_len[:, None], src_lang, tgt_lang], axis=1)
    rows = jnp.where(place.z // 2 == core, meta, place.over_core(meta))
    row = lax.dynamic_index_in_dim(rows, place.z % 2, 0, keepdims=False)
    count, segs = src_seg.shape[1], src_lang.shape[1]
    s_seg, t_seg, t_len = row[:count], row[count : 2 * count], row[2 * count]
    s_lang, t_lang = row[2 * count + 1 : 2 * count + 1 + segs], row[2 * count + 1 + segs :]

    def onehot(segments, chosen):
        member = segments[:, None] == jnp.arange(segs, dtype=jnp.int32)[None, :]
        token = jnp.sum(jnp.where(member, chosen[None, :], 0), axis=1)
        return (token[:, None] == jnp.arange(langs, dtype=jnp.int32)[None, :]).astype(B16)

    src_hot, tgt_hot = onehot(s_seg, s_lang), onehot(t_seg, t_lang)
    enc_masks = (block_info(False, s_seg, s_seg, t_len), s_seg[None, :], s_seg[:, None])
    dec_masks = (block_info(True, t_seg, t_seg, t_len), t_seg[None, :], t_seg[:, None])
    cross_masks = (block_info(False, t_seg, s_seg, t_len), t_seg[None, :], s_seg[:, None])

    none = jnp.zeros((half,), F32)
    packed = (0, half // GROUP, 2 * half // GROUP)

    enc_h0 = source.astype(F32) + product(src_hot, languages)
    enc_n1 = layer_norm(enc_h0, gain_f[0], bias_f[0])
    enc_qkv_bias = jnp.concatenate([bias_own[1], none, bias_own[2]])
    enc_qkv = (product(enc_n1, enc_qkv_w) + enc_qkv_bias).astype(B16)
    enc_mixed, enc_lse = attend_forward(False, enc_masks, enc_qkv, enc_qkv, enc_qkv, packed, half)
    enc_h1 = enc_h0 + place.both_cores(product(enc_mixed, enc_o_w)) + bias_f[3]
    enc_n2 = layer_norm(enc_h1, gain_f[1], bias_f[4])
    enc_acted, enc_slope = gelu_both(product(enc_n2, enc_in_w) + ffb_own[0])
    encoded = enc_h1 + place.both_cores(product(enc_acted, enc_out_w)) + bias_f[5]
    memory = encoded.astype(B16)

    dec_h0 = target.astype(F32) + product(tgt_hot, languages)
    dec_n1 = layer_norm(dec_h0, gain_f[2], bias_f[6])
    dec_qkv_bias = jnp.concatenate([bias_own[7], none, bias_own[8]])
    dec_qkv = (product(dec_n1, dec_qkv_w) + dec_qkv_bias).astype(B16)
    dec_mixed, dec_lse = attend_forward(True, dec_masks, dec_qkv, dec_qkv, dec_qkv, packed, half)
    dec_h1 = dec_h0 + place.both_cores(product(dec_mixed, dec_o_w)) + bias_f[9]
    dec_n2 = layer_norm(dec_h1, gain_f[3], bias_f[10])
    cross_q = (product(dec_n2, cross_w[:, :half]) + bias_own[11]).astype(B16)
    cross_kv_bias = jnp.concatenate([none, bias_own[12]])
    cross_kv = (product(memory, cross_w[:, half:]) + cross_kv_bias).astype(B16)
    apart = (0, 0, half // GROUP)
    cross_mixed, cross_lse = attend_forward(False, cross_masks, cross_q, cross_kv, cross_kv, apart, half)
    dec_h2 = dec_h1 + place.both_cores(product(cross_mixed, cross_o_w)) + bias_f[13]
    dec_n3 = layer_norm(dec_h2, gain_f[4], bias_f[14])
    dec_acted, dec_slope = gelu_both(product(dec_n3, dec_in_w) + ffb_own[1])
    decoded = dec_h2 + place.both_cores(product(dec_acted, dec_out_w)) + bias_f[15]

    dec_du = (product_nt(target_cot, dec_out_w) * dec_slope.astype(F32)).astype(B16)
    dec_dn3 = place.both_cores(product_nt(dec_du, dec_in_w))
    dec_in_grad = moves.early_columns([(dec_n3, dec_du)], 1)
    dec_out_grad = moves.early_rows(dec_acted, target_cot)
    target_cot_f = target_cot.astype(F32)
    step, gain_four, shift_14 = norm_backward(dec_h2, gain_f[4], dec_dn3)
    grad_h2 = target_cot_f + step

    cross_branch = grad_h2.astype(B16)
    cross_do = product_nt(cross_branch, cross_o_w).astype(B16)
    cross_dq, cross_dkv = attend_backward(
        False, cross_masks, cross_q, cross_kv, cross_kv, apart, half, cross_mixed, cross_lse, cross_do
    )
    grad_memory = place.both_cores(product_nt(cross_dkv, cross_w[:, half:]))
    dec_dn2 = place.both_cores(product_nt(cross_dq, cross_w[:, :half]))

    cross_grad, cross_o_grad = moves.early_both(
        [(dec_n2, cross_dq), (memory, cross_dkv)], 3, cross_mixed, cross_branch
    )

    source_cot_f = source_cot.astype(F32) + grad_memory
    enc_ff_branch = source_cot_f.astype(B16)
    enc_du = (product_nt(enc_ff_branch, enc_out_w) * enc_slope.astype(F32)).astype(B16)
    enc_dn2 = place.both_cores(product_nt(enc_du, enc_in_w))

    step, gain_three, shift_10 = norm_backward(dec_h1, gain_f[3], dec_dn2)
    grad_h1 = grad_h2 + step
    self_branch = grad_h1.astype(B16)
    dec_do = product_nt(self_branch, dec_o_w).astype(B16)
    (dec_dqkv,) = attend_backward(
        True, dec_masks, dec_qkv, dec_qkv, dec_qkv, packed, half, dec_mixed, dec_lse, dec_do
    )
    dec_dn1 = place.both_cores(product_nt(dec_dqkv, dec_qkv_w))
    step, gain_two, shift_6 = norm_backward(dec_h0, gain_f[2], dec_dn1)
    target_grad = grad_h1 + step

    step, gain_one, shift_4 = norm_backward(enc_h1, gain_f[1], enc_dn2)
    grad_e1 = source_cot_f + step
    enc_branch = grad_e1.astype(B16)
    enc_do = product_nt(enc_branch, enc_o_w).astype(B16)
    (enc_dqkv,) = attend_backward(
        False, enc_masks, enc_qkv, enc_qkv, enc_qkv, packed, half, enc_mixed, enc_lse, enc_do
    )
    enc_dn1 = place.both_cores(product_nt(enc_dqkv, enc_qkv_w))
    step, gain_zero, shift_0 = norm_backward(enc_h0, gain_f[0], enc_dn1)
    source_grad = grad_e1 + step

    source_high, target_high = source_grad.astype(B16), target_grad.astype(B16)
    lang_grad = 0.0
    for hot, value, high in ((src_hot, source_grad, source_high), (tgt_hot, target_grad, target_high)):
        low = (value - high.astype(F32)).astype(B16)
        lang_grad = lang_grad + product_tn(hot, high) + product_tn(hot, low)
    own = functools.partial(own_columns, core=core)
    gain_rows = jnp.stack([gain_zero, gain_one, gain_two, gain_three, gain_four])
    enc_qkv_sum, dec_qkv_sum = column_sum(enc_dqkv), column_sum(dec_dqkv)
    bias_rows = jnp.stack(
        [
            own(shift_0),
            enc_qkv_sum[:half],
            enc_qkv_sum[2 * half :],
            own(column_sum(enc_branch)),
            own(shift_4),
            own(column_sum(enc_ff_branch)),
            own(shift_6),
            dec_qkv_sum[:half],
            dec_qkv_sum[2 * half :],
            own(column_sum(self_branch)),
            own(shift_10),
            column_sum(cross_dq),
            column_sum(cross_dkv[:, half:]),
            own(column_sum(cross_branch)),
            own(shift_14),
            own(column_sum(target_cot)),
        ]
    )
    grads, small, ffb_grad, outputs = moves.sums(
        {
            1: (dec_n1, dec_dqkv, 3),
            2: (enc_n2, enc_du, 1),
            4: (enc_n1, enc_dqkv, 3),
        },
        {
            0: (dec_mixed, self_branch),
            3: (enc_acted, enc_ff_branch),
            5: (enc_mixed, enc_branch),
        },
        jnp.concatenate([own(lang_grad), own(gain_rows), bias_rows], axis=0),
        jnp.stack([column_sum(enc_du), column_sum(dec_du)]),
        [memory, decoded.astype(B16), source_high, target_high],
    )
    return (
        outputs[0],
        outputs[1],
        outputs[2].astype(F32),
        outputs[3].astype(F32),
        small[:langs],
        small[langs : langs + 5],
        small[langs + 5 :],
        ffb_grad,
        grads[4],
        grads[5],
        grads[2][0],
        grads[3],
        jnp.concatenate([grads[1], cross_grad], axis=0),
        jnp.stack([grads[0], cross_o_grad]),
        dec_in_grad[0],
        dec_out_grad,
    )


def solution(mesh):
    dp, seq = mesh.shape["dp"] // 2, mesh.shape["seq"]
    pairs = Mesh(mesh.devices.reshape(dp, 2, seq), ("dp", "core", "seq"))
    both, every = ("dp", "core"), ("dp", "core", "seq")
    rows = P(both, "seq", None)
    columns = P(None, every)
    middle = P(None, every, None)
    first = P(every, None)
    weights = (columns, columns, columns, columns, middle, first, first, first, middle, middle, first, first)
    return jax.shard_map(
        functools.partial(on_device, dp, seq),
        mesh=pairs,
        in_specs=(rows, rows, P(both, None), P(both, None), P(both), P(both, None), P(both, None))
        + weights
        + (rows, rows),
        out_specs=(rows, rows, rows, rows) + weights,
        check_vma=False,
    )
```

```python
import functools

import jax
import jax.numpy as jnp
from jax import lax
from jax.experimental import pallas as pl
from jax.experimental.pallas import tpu as pltpu
from jax.sharding import Mesh
from jax.sharding import PartitionSpec as P

HEAD_DIM = 64
EPSILON = 1e-05
MASKED = -1000000000.0
BLOCK = 256
HEADS = 4
GROUP = HEADS * HEAD_DIM
B16 = jnp.bfloat16
F32 = jnp.float32


def product(left, right):
    return jnp.dot(left, right, preferred_element_type=F32)


def product_tn(left, right):
    return lax.dot_general(left, right, (((0,), (0,)), ((), ())), preferred_element_type=F32)


def product_nt(left, right):
    return lax.dot_general(left, right, (((1,), (1,)), ((), ())), preferred_element_type=F32)


def column_sum(values):
    return jnp.sum(values.astype(F32), axis=0)


def norm_parts(hidden):
    centred = hidden - jnp.mean(hidden, axis=-1, keepdims=True)
    spread = jnp.mean(centred * centred, axis=-1, keepdims=True)
    scale = lax.rsqrt(spread + EPSILON)
    return centred * scale, scale


def layer_norm(hidden, gain_row, shift_row):
    return (norm_parts(hidden)[0] * gain_row + shift_row).astype(B16)


def norm_backward_kernel(last, h_ref, mine_ref, other_ref, grad_ref, gain_ref, *rest):
    if last:
        hot_ref, low_ref, sums_ref, lang_ref = rest
    else:
        full_ref, low_ref, sums_ref = rest
    unit, scale = norm_parts(h_ref[...])
    down = mine_ref[...].astype(F32) + other_ref[...].astype(F32)
    weighted = down * gain_ref[...]
    step = scale * (
        weighted
        - jnp.mean(weighted, axis=-1, keepdims=True)
        - unit * jnp.mean(weighted * unit, axis=-1, keepdims=True)
    )
    full = grad_ref[...].astype(F32) + step
    low = full.astype(B16)
    low_ref[...] = low

    @pl.when(pl.program_id(0) == 0)
    def _():
        sums_ref[...] = jnp.zeros_like(sums_ref)
        if last:
            lang_ref[...] = jnp.zeros_like(lang_ref)

    for k, value in enumerate((down * unit, down, low.astype(F32))):
        sums_ref[k : k + 1, :] += jnp.sum(value, axis=0, keepdims=True)
    if last:
        hot = hot_ref[...]
        rest_low = (full - low.astype(F32)).astype(B16)
        lang_ref[...] += product_tn(hot, low) + product_tn(hot, rest_low)
    else:
        full_ref[...] = full


def norm_backward(hidden, gain_row, parts, grad, hot=None):
    count, width = hidden.shape
    last = hot is not None
    block = pl.BlockSpec((BLOCK, width), lambda i: (i, 0))
    still = lambda rows: pl.BlockSpec((rows, width), lambda i: (0, 0))
    inputs = [hidden, parts[0], parts[1], grad, gain_row] + ([hot] if last else [])
    outs = [(count, B16, block), (8, F32, still(8))]
    outs = outs + [(hot.shape[1], F32, still(hot.shape[1]))] if last else [(count, F32, block)] + outs
    return pl.pallas_call(
        functools.partial(norm_backward_kernel, last),
        grid=(count // BLOCK,),
        in_specs=[block] * 4
        + [still(1)]
        + ([pl.BlockSpec((BLOCK, hot.shape[1]), lambda i: (i, 0))] if last else []),
        out_specs=[spec for _, _, spec in outs],
        out_shape=[jax.ShapeDtypeStruct((rows, width), kind) for rows, kind, _ in outs],
        compiler_params=pltpu.CompilerParams(vmem_limit_bytes=28 * 2**20),
        cost_estimate=pl.CostEstimate(flops=30 * count * width, bytes_accessed=18 * count * width, transcendentals=0),
        name="norm_last" if last else "norm_grad",
    )(*inputs)


def gelu_both(values):
    below = 0.5 * (1.0 + lax.erf(values * (0.5**0.5)))
    density = jnp.exp(-0.5 * values * values) * (0.5 / jnp.pi) ** 0.5
    return (values * below).astype(B16), (below + values * density).astype(B16)


def allowed_block(causal, kseg_ref, qseg, length, key_at, query_at):
    allowed = kseg_ref[key_at : key_at + BLOCK, :] == qseg
    if causal:
        keys = key_at + lax.broadcasted_iota(jnp.int32, (BLOCK, BLOCK), 0)
        queries = query_at + lax.broadcasted_iota(jnp.int32, (BLOCK, BLOCK), 1)
        allowed = allowed & (keys <= queries) & ((keys < length) | (keys == queries))
    return allowed


def dot_nt(left, right):
    return lax.dot_general(left, right, (((1,), (1,)), ((), ())), preferred_element_type=F32)


def head_masked(value, axis=1):
    lane = lax.broadcasted_iota(jnp.int32, value.shape, axis) // HEAD_DIM
    zero = jnp.zeros_like(value)
    return [jnp.where(lane == h, value, zero) for h in range(HEADS)]


def dot_nn(left, right):
    return jnp.dot(left, right, preferred_element_type=F32)


def fold_rows(value, combine):
    return combine(value.reshape(value.shape[0] // 8, 8, value.shape[1]), axis=0)


def forward_kernel(
    causal,
    info_ref,
    q_ref,
    k_ref,
    v_ref,
    qseg_ref,
    kseg_ref,
    o_ref,
    lse_ref,
    vt_ref,
    s_ref,
    acc_ref,
    top_ref,
    sum_ref,
    qt_ref,
):
    block = pl.program_id(1)
    blocks = k_ref.shape[0] // BLOCK
    length = info_ref[blocks * blocks]

    @pl.when(block == 0)
    def _():
        vt_ref[...] = v_ref[...].T

    qseg = qseg_ref[...]
    for h, head in enumerate(head_masked((q_ref[...] * jnp.asarray(HEAD_DIM**-0.5, B16)).T, 0)):
        qt_ref[h] = head
    top_ref[...] = jnp.full(top_ref.shape, -1e30, F32)
    sum_ref[...] = jnp.zeros_like(sum_ref)
    acc_ref[...] = jnp.zeros_like(acc_ref)
    for j in range(blocks):

        @pl.when(info_ref[block * blocks + j] > 0)
        def _(j=j):
            keys = k_ref[j * BLOCK : (j + 1) * BLOCK, :]
            allowed = allowed_block(causal, kseg_ref, qseg, length, j * BLOCK, block * BLOCK)
            for h in range(HEADS):
                scores = jnp.where(allowed, dot_nn(keys, qt_ref[h]), MASKED)
                s_ref[h, j * BLOCK : (j + 1) * BLOCK, :] = scores
                top_ref[h] = jnp.maximum(top_ref[h], fold_rows(scores, jnp.max))

    highest = [jnp.max(top_ref[h], axis=0, keepdims=True) for h in range(HEADS)]
    for j in range(blocks):

        @pl.when(info_ref[block * blocks + j] > 0)
        def _(j=j):
            for h in range(HEADS):
                weights = jnp.exp(s_ref[h, j * BLOCK : (j + 1) * BLOCK, :] - highest[h])
                sum_ref[h] += fold_rows(weights, jnp.sum)
                rows = slice(h * HEAD_DIM, (h + 1) * HEAD_DIM)
                acc_ref[rows, :] += jnp.dot(
                    vt_ref[rows, j * BLOCK : (j + 1) * BLOCK],
                    weights.astype(B16),
                    preferred_element_type=F32,
                )

    lse_ref[...] = jnp.zeros_like(lse_ref)
    for h in range(HEADS):
        total = jnp.sum(sum_ref[h], axis=0, keepdims=True)
        rows = slice(h * HEAD_DIM, (h + 1) * HEAD_DIM)
        acc_ref[rows, :] = acc_ref[rows, :] / total
        lse_ref[0, h : h + 1, :] = highest[h] + jnp.log(total)
    o_ref[...] = acc_ref[...].T.astype(B16)


def backward_kernel(
    causal,
    info_ref,
    q_ref,
    k_ref,
    v_ref,
    o_ref,
    do_ref,
    lse_ref,
    qseg_ref,
    kseg_ref,
    *rest,
):
    *outs, kt_ref, dqt_ref, sums_ref, done_ref, qt_ref, dot_ref, sems = rest
    group, block = pl.program_id(0), pl.program_id(1)
    groups = pl.num_programs(0)
    blocks = k_ref.shape[0] // BLOCK
    length = info_ref[blocks * blocks]

    @pl.when(block == 0)
    def _():
        kt_ref[...] = k_ref[...].T
        sums_ref[...] = jnp.zeros_like(sums_ref)

    qseg = qseg_ref[...]
    grads = do_ref[...]
    scaled = q_ref[...] * jnp.asarray(HEAD_DIM**-0.5, B16)
    grads_up = grads.T
    for h, head in enumerate(head_masked(scaled.T, 0)):
        qt_ref[h] = head
    for h, head in enumerate(head_masked(grads_up, 0)):
        dot_ref[h] = head
    queries_down = jnp.concatenate(head_masked(scaled), axis=0)
    grads_down = jnp.concatenate(head_masked(grads), axis=0)
    mixed = grads_up.astype(F32) * o_ref[...].T.astype(F32)
    inner = [
        jnp.sum(fold_rows(mixed[h * HEAD_DIM : (h + 1) * HEAD_DIM], jnp.sum), axis=0, keepdims=True)
        for h in range(HEADS)
    ]
    dqt_ref[...] = jnp.zeros_like(dqt_ref)
    for j in range(blocks):

        @pl.when(info_ref[block * blocks + j] > 0)
        def _(j=j):
            rows = slice(j * BLOCK, (j + 1) * BLOCK)
            keys = k_ref[rows, :]
            values = v_ref[rows, :]
            allowed = allowed_block(causal, kseg_ref, qseg, length, j * BLOCK, block * BLOCK)
            all_chances, all_scores = [], []
            for h in range(HEADS):
                scores = dot_nn(keys, qt_ref[h])
                chances = jnp.where(allowed, jnp.exp(scores - lse_ref[0, h : h + 1, :]), 0.0)
                grad_chances = dot_nn(values, dot_ref[h])
                grad_scores = (chances * (grad_chances - inner[h])).astype(B16)
                all_chances.append(chances.astype(B16))
                all_scores.append(grad_scores)
                part = slice(h * HEAD_DIM, (h + 1) * HEAD_DIM)
                dqt_ref[part, :] += jnp.dot(kt_ref[part, rows], grad_scores, preferred_element_type=F32)
            sums_ref[0, rows, :] += jnp.dot(
                jnp.concatenate(all_scores, axis=1), queries_down, preferred_element_type=F32
            )
            sums_ref[1, rows, :] += jnp.dot(
                jnp.concatenate(all_chances, axis=1), grads_down, preferred_element_type=F32
            )

    here = pl.ds(pl.multiple_of(block * BLOCK, BLOCK), BLOCK)
    done_ref[0, here, :] = (dqt_ref[...].T * HEAD_DIM**-0.5).astype(B16)

    @pl.when(block == blocks - 1)
    def _():
        done_ref[1] = sums_ref[0].astype(B16)
        done_ref[2] = sums_ref[1].astype(B16)
        width = k_ref.shape[1]
        copies = []
        for k in range(3):
            out, place = (outs[0], k) if len(outs) == 1 else (outs[min(k, 1)], max(k - 1, 0))
            lanes = pl.ds(pl.multiple_of((place * groups + group) * width, width), width)
            copies.append(pltpu.make_async_copy(done_ref.at[k], out.at[:, lanes], sems.at[k]))
        for copy in copies:
            copy.start()
        for copy in copies:
            copy.wait()


def block_info(causal, query_seg, key_seg, length):
    blocks = query_seg.shape[0] // BLOCK
    query_low, query_high = query_seg[::BLOCK], query_seg[BLOCK - 1 :: BLOCK]
    key_low, key_high = key_seg[::BLOCK], key_seg[BLOCK - 1 :: BLOCK]
    meets = (key_low[None, :] <= query_high[:, None]) & (key_high[None, :] >= query_low[:, None])
    if causal:
        at = jnp.arange(blocks)
        meets = meets & (at[None, :] <= at[:, None])
    return jnp.concatenate([meets.astype(jnp.int32).reshape(-1), length[None]])


def attention_specs(count, offsets):
    query = pl.BlockSpec((BLOCK, GROUP), lambda p, i, info: (i, p + offsets[0]))
    key = pl.BlockSpec((count, GROUP), lambda p, i, info: (0, p + offsets[1]))
    value = pl.BlockSpec((count, GROUP), lambda p, i, info: (0, p + offsets[2]))
    plain = pl.BlockSpec((BLOCK, GROUP), lambda p, i, info: (i, p))
    whole = pl.BlockSpec((count, GROUP), lambda p, i, info: (0, p))
    stats = pl.BlockSpec((1, 8, BLOCK), lambda p, i, info: (p, 0, i))
    qseg = pl.BlockSpec((1, BLOCK), lambda p, i, info: (0, i))
    kseg = pl.BlockSpec((count, 1), lambda p, i, info: (0, 0))
    return query, key, value, plain, whole, stats, qseg, kseg


def attend_forward(causal, masks, queries, keys, values, offsets, width):
    info, qseg_row, kseg_column = masks
    count = queries.shape[0]
    groups = width // GROUP
    query, key, value, plain, _, stats, qseg, kseg = attention_specs(count, offsets)
    return pl.pallas_call(
        functools.partial(forward_kernel, causal),
        grid_spec=pltpu.PrefetchScalarGridSpec(
            num_scalar_prefetch=1,
            grid=(groups, count // BLOCK),
            in_specs=[query, key, value, qseg, kseg],
            out_specs=[plain, stats],
            scratch_shapes=[pltpu.VMEM((GROUP, count), B16), pltpu.VMEM((HEADS, count, BLOCK), F32), pltpu.VMEM((GROUP, BLOCK), F32)]
            + [pltpu.VMEM((HEADS, 8, BLOCK), F32)] * 2
            + [pltpu.VMEM((HEADS, GROUP, BLOCK), B16)],
        ),
        out_shape=[
            jax.ShapeDtypeStruct((count, width), B16),
            jax.ShapeDtypeStruct((groups, 8, count), F32),
        ],
        compiler_params=pltpu.CompilerParams(vmem_limit_bytes=24 * 2**20),
        cost_estimate=pl.CostEstimate(
            flops=2 * 2 * count * count * width * 2, bytes_accessed=count * width * 8, transcendentals=0
        ),
        name="attend_causal" if causal else "attend",
    )(info, queries, keys, values, qseg_row, kseg_column)


def attend_backward(causal, masks, queries, keys, values, offsets, width, mixed, lse, grad):
    widths = (3 * width,) if queries is keys else (width, 2 * width)
    info, qseg_row, kseg_column = masks
    count = queries.shape[0]
    groups = width // GROUP
    query, key, value, plain, _, stats, qseg, kseg = attention_specs(count, offsets)
    return pl.pallas_call(
        functools.partial(backward_kernel, causal),
        grid_spec=pltpu.PrefetchScalarGridSpec(
            num_scalar_prefetch=1,
            grid=(groups, count // BLOCK),
            in_specs=[query, key, value, plain, plain, stats, qseg, kseg],
            out_specs=[pl.BlockSpec(memory_space=pl.ANY)] * len(widths),
            scratch_shapes=[
                pltpu.VMEM((GROUP, count), B16),
                pltpu.VMEM((GROUP, BLOCK), F32),
                pltpu.VMEM((2, count, GROUP), F32),
                pltpu.VMEM((3, count, GROUP), B16),
                pltpu.VMEM((HEADS, GROUP, BLOCK), B16),
                pltpu.VMEM((HEADS, GROUP, BLOCK), B16),
                pltpu.SemaphoreType.DMA((3,)),
            ],
        ),
        out_shape=[jax.ShapeDtypeStruct((count, w), B16) for w in widths],
        compiler_params=pltpu.CompilerParams(vmem_limit_bytes=24 * 2**20),
        cost_estimate=pl.CostEstimate(
            flops=5 * 2 * count * count * width * 2, bytes_accessed=count * width * 16, transcendentals=0
        ),
        name="attend_grad_causal" if causal else "attend_grad",
    )(info, queries, keys, values, mixed, grad, lse, qseg_row, kseg_column)


MESH = pl.DeviceIdType.MESH
GATHER_LAGS = (0, 1, 2, 3)
ROW_LAG = 4
SUM_CUT = 20
SUM_ROWS = [1, 3, 5, 7]


def own_columns(array, core):
    w = array.shape[-1] // 8
    runs = [array[..., k * w : (k + 1) * w] for k in range(8)]
    return jnp.concatenate([jnp.where(core == 0, runs[k], runs[k + 1]) for k in range(0, 8, 2)], axis=-1)


def lay_side(array):
    return jnp.concatenate([array[i] for i in range(array.shape[0])], axis=1)


def lay_wide(arrays):
    return arrays[0] if len(arrays) == 1 else jnp.concatenate(arrays, axis=1)


def xor_arrange(pieces, place):
    pieces, bit = list(pieces), 0
    while 1 << bit < len(pieces):
        odd = ((place >> bit) & 1) == 1
        pieces = [jnp.where(odd, pieces[k ^ (1 << bit)], pieces[k]) for k in range(len(pieces))]
        bit += 1
    return pieces


class Here:
    def __init__(self):
        self.at = lax.axis_index("dp")
        self.c = lax.axis_index("core")
        self.z = lax.axis_index("seq")
        self.x = self.at % 2
        self.y = self.at // 2
        self.core_peer = (self.at, 1 - self.c, self.z)
        self.x_peer = (self.at + 1 - 2 * self.x, self.c, self.z)
        self.y_peer = (self.at + 2 - 4 * self.y, self.c, self.z)
        self.edge = (self.z % 3) == 0
        self.inner = jnp.logical_not(self.edge)

    def z_flip(self, j):
        return (self.z // 2 + j // 2) % 2 * 2 + (self.z % 2 + j % 2) % 2

    def z_peer(self, j):
        return (self.at, self.c, self.z_flip(j))

    def enter(self):
        barrier = pltpu.get_barrier_semaphore()
        peers = [self.x_peer, self.y_peer, self.core_peer]
        for j in range(1, 4):
            peers += [(self.at, self.c, self.z_flip(j)), (self.at, 1 - self.c, self.z_flip(j))]
        for peer in peers:
            pl.semaphore_signal(barrier, inc=1, device_id=peer, device_id_type=MESH)
        pl.semaphore_wait(barrier, len(peers))


def remote(source, target, send_sem, recv_sem, peer):
    return pltpu.make_async_remote_copy(
        src_ref=source,
        dst_ref=target,
        send_sem=send_sem,
        recv_sem=recv_sem,
        device_id=peer,
        device_id_type=MESH,
    )


class GatherItem:
    def __init__(self, here, source, first, kind, out, start, size, send, recv, local):
        self.here, self.source, self.first, self.kind, self.out = here, source, first, kind, out
        self.send, self.recv, self.local = send, recv, local
        self.start, self.size = start, size
        self.all = pl.ds(start, size)
        self.sides = [pl.ds(start, size // 2), pl.ds(start + size // 2, size // 2)]
        if kind == "small":
            self.sides = [self.all]
        self.core = 0 if kind == "rows" else here.c
        self.copies = {}

    def move(self, slot, region, peer, arrive=None):
        recv = self.recv.at[slot if arrive is None else arrive]
        self.copies[slot] = remote(region, region, self.send.at[slot], recv, peer)
        return self.copies[slot]

    def runs(self, core):
        w = self.source.shape[-1] // 8
        for q in range(self.start // w, (self.start + self.size) // w):
            lanes = pl.ds(pl.multiple_of((q % 4 * 2 + core) * w, 128), w)
            yield self.source.at[self.first + q // 4, :, lanes], pl.ds(q * w, w)

    def begin(self):
        here = self.here
        place = self.out.at[here.y, here.x, self.core, here.z]
        block = self.out.at[here.y, here.x, self.core, here.z, :, self.all]
        self.own = pltpu.make_async_copy(block, block, self.local)
        if self.kind == "columns":
            for source, lanes in self.runs(here.c):
                pltpu.make_async_copy(source, place.at[:, lanes], self.local).start()
            for source, lanes in self.runs(1 - here.c):
                remote(source, place.at[:, lanes], self.send.at[0], self.recv.at[0], here.core_peer).start()
        else:
            source = self.source.at[self.first, :, self.all]
            pltpu.make_async_copy(source, block, self.local).start()
            if self.kind == "small":
                remote(source, block, self.send.at[0], self.recv.at[0], here.core_peer).start()
        if self.kind != "rows":
            self.copies[0] = remote(block, block, self.send.at[0], self.recv.at[0], here.core_peer)

    def stage_z(self):
        here = self.here
        self.own.wait()
        if self.kind != "rows":
            self.copies[0].wait_recv()
        block = self.out.at[here.y, here.x, :, here.z, :, self.all]
        self.move(1, block, here.z_peer(1)).start()
        self.move(2, block, here.z_peer(2)).start()
        pl.when(here.inner)(self.move(3, block, here.z_peer(3)).start)

    def stage_pass(self):
        here = self.here
        self.copies[2].wait_recv()
        block = self.out.at[here.y, here.x, :, here.z_flip(2), :, self.all]
        pl.when(here.inner)(self.move(8, block, here.z_peer(1), arrive=3).start)

    def stage_one(self):
        here = self.here
        self.copies[1].wait_recv()
        self.copies[3].wait_recv()
        for k, peer in list(enumerate((here.x_peer, here.y_peer)))[: len(self.sides)]:
            self.move(4 + k, self.out.at[here.y, here.x, :, :, :, self.sides[k]], peer).start()

    def stage_two(self):
        here = self.here
        self.copies[4].wait_recv()
        self.move(6, self.out.at[here.y, :, :, :, :, self.sides[0]], here.y_peer).start()
        if len(self.sides) == 2:
            self.copies[5].wait_recv()
            self.move(7, self.out.at[:, here.x, :, :, :, self.sides[1]], here.x_peer).start()

    def finish(self):
        for k in range(len(self.sides)):
            self.copies[6 + k].wait_recv()
        for slot, copy in self.copies.items():
            if slot in (3, 8):
                pl.when(self.here.inner)(copy.wait_send)
            else:
                copy.wait_send()


class RowIn:
    def __init__(self, here, source, out, send, recv, local):
        self.here, self.source, self.out = here, source, out
        self.send, self.recv, self.local = send, recv, local
        self.half = source.shape[-1] // 2

    def lanes(self, f):
        return pl.ds(f * self.half, self.half) if isinstance(f, int) else pl.ds(pl.multiple_of(f * self.half, 128), self.half)

    def parts(self):
        here = self.here
        for i in range(2):
            for f in range(2):
                source = self.source.at[i, :, self.lanes(f)]
                target = self.out.at[here.z, :, self.lanes(f)]
                self_sent = (2 * here.c + i == here.z) & (here.c == f)
                peer = (here.at, f, 2 * here.c + i)
                away = remote(source, target, self.send.at[2 * i + f], self.recv.at[here.z], peer)
                stay = pltpu.make_async_copy(source, target, self.local)
                yield self_sent, away, stay

    def begin(self):
        for self_sent, away, stay in self.parts():
            pl.when(self_sent)(stay.start)
            pl.when(jnp.logical_not(self_sent))(away.start)

    def across(self):
        here = self.here
        lanes = self.lanes(here.c)
        for k in range(4):
            target = self.out.at[k, :, lanes]
            from_self = (here.z == k) & (here.z // 2 == here.c)
            stay = pltpu.make_async_copy(target, target, self.local)
            away = remote(target, target, self.send.at[0], self.recv.at[k], here.core_peer)
            pl.when(from_self)(stay.wait)
            pl.when(jnp.logical_not(from_self))(away.wait_recv)
        region = self.out.at[:, :, lanes]
        self.copy = remote(region, region, self.send.at[4], self.recv.at[4], here.core_peer)
        self.copy.start()

    def finish(self):
        self.copy.wait()
        for self_sent, away, _ in self.parts():
            pl.when(jnp.logical_not(self_sent))(away.wait_send)


def gather_kernel(kinds, cuts, rows_at, refs):
    here = Here()
    refs = list(refs)
    take = lambda n: [refs.pop(0) for _ in range(n)]
    count = len(kinds)
    ins = take(count)
    row_ins = take(len(rows_at))
    outs = take(count)
    row_outs = take(len(rows_at))
    send, recv, local, row_send, row_recv, row_local = refs
    items = []
    for k, (first, kind) in enumerate(kinds):
        size = outs[k].shape[-1] // cuts[k]
        for cut in range(cuts[k]):
            n = len(items)
            sems = send.at[n], recv.at[n], local.at[n]
            items.append(GatherItem(here, ins[k], first, kind, outs[k], cut * size, size, *sems))
    count = len(items)
    rows = [
        RowIn(here, row_ins[t], row_outs[t], row_send.at[t], row_recv.at[t], row_local.at[t])
        for t in range(len(rows_at))
    ]
    here.enter()
    for item in items:
        item.begin()
    steps = (GatherItem.stage_z, GatherItem.stage_pass, GatherItem.stage_one, GatherItem.stage_two)
    for step in range(count + GATHER_LAGS[-1] + 1):
        for t, start in enumerate(rows_at):
            if start == step:
                rows[t].begin()
            if min(start + ROW_LAG, count + GATHER_LAGS[-1]) == step:
                rows[t].across()
        for stage, lag in zip(steps, GATHER_LAGS):
            if 0 <= step - lag < count:
                stage(items[step - lag])
    for item in items:
        item.finish()
    for row in rows:
        row.finish()


def gather_all(sources, rows, rows_at):
    kinds = [(first, kind) for _, first, _, kind in sources]
    inputs = [source[0] for source in sources] + list(rows)
    shapes, cuts = [], []
    for array, _, number, kind in sources:
        _, r, n = array.shape
        n = number * n // 2 if kind == "columns" else n
        shapes.append(jax.ShapeDtypeStruct((2, 2, 1 if kind == "rows" else 2, 4, r, n), array.dtype))
        cuts.append(2 if r * n * (2 if kind == "columns" else 1) > 2**16 else 1)
    shapes += [jax.ShapeDtypeStruct((4,) + row.shape[1:], row.dtype) for row in rows]
    count, tensors = sum(cuts), len(rows)
    hbm = pl.BlockSpec(memory_space=pl.ANY)

    def kernel(*refs):
        gather_kernel(kinds, cuts, rows_at, refs)

    dma = pltpu.SemaphoreType.DMA
    return pl.pallas_call(
        kernel,
        in_specs=[hbm] * len(inputs),
        out_specs=[hbm] * len(shapes),
        out_shape=shapes,
        scratch_shapes=[
            dma((count, 9)),
            dma((count, 9)),
            dma((count,)),
            dma((tensors, 5)),
            dma((tensors, 5)),
            dma((tensors,)),
        ],
        compiler_params=pltpu.CompilerParams(collective_id=0, has_side_effects=True),
        name="gather_all",
    )(*inputs)


class SumItem:
    def __init__(self, here, source, out, start, scratch, send, recv, local):
        self.here, self.source, self.out = here, source, out
        self.own, self.b1, self.b2, self.b3, self.met = scratch[:5]
        self.columns = source.shape[2] == 2
        if self.columns:
            self.b4, self.b4s = scratch[5:]
        self.send, self.recv, self.local = send, recv, local
        size = self.own.shape[-1]
        self.half = size // 2
        self.sides = pl.ds(0, self.half), pl.ds(self.half, self.half)
        self.cut = slice(start, start + size)
        self.source_sides = pl.ds(start, self.half), pl.ds(start + self.half, self.half)
        self.copies = {}

    def make(self, slot, source, target, peer):
        self.copies[slot] = remote(source, target, self.send.at[slot], self.recv.at[slot], peer)
        return self.copies[slot]

    def go(self, slot, source, target, peer):
        self.make(slot, source, target, peer).start()

    def blocks(self, body):
        cores = self.b2.shape[0]

        def step(k, carry):
            body(k // 4, k % 4)
            return carry

        lax.fori_loop(0, cores * 4, step, 0)

    def stage_one(self):
        here, (a, b), source = self.here, self.sides, self.source
        first, second = self.source_sides
        self.go(0, source.at[:, 1 - here.x, :, :, :, first], self.b1.at[:, :, :, :, a], here.x_peer)
        self.go(1, source.at[1 - here.y, :, :, :, :, second], self.b1.at[:, :, :, :, b], here.y_peer)
        self.loads = [
            pltpu.make_async_copy(source.at[:, here.x, :, :, :, first], self.own.at[:, :, :, :, a], self.local.at[0]),
            pltpu.make_async_copy(source.at[here.y, :, :, :, :, second], self.own.at[:, :, :, :, b], self.local.at[1]),
        ]
        for load in self.loads:
            load.start()

        @pl.when(here.edge)
        def _():
            self.b3[2] = jnp.zeros(self.b3.shape[1:], self.b3.dtype)

    def stage_two(self):
        here = self.here
        for side, near, peer in ((0, here.y, here.y_peer), (1, here.x, here.x_peer)):
            lanes = self.sides[side]
            away = 1 - near
            self.loads[side].wait()
            self.copies[side].wait_recv()

            def add(c, z, away=away, lanes=lanes):
                total = self.own[away, c, z, :, lanes].astype(F32) + self.b1[away, c, z, :, lanes].astype(F32)
                self.own[away, c, z, :, lanes] = total.astype(self.own.dtype)

            self.blocks(add)
            self.go(2 + side, self.own.at[away, :, :, :, lanes], self.b2.at[:, :, :, lanes], peer)

    def stage_three(self):
        here = self.here
        for side, near in ((0, here.y), (1, here.x)):
            lanes = self.sides[side]
            self.copies[2 + side].wait_recv()

            def add(c, z, near=near, lanes=lanes):
                total = self.own[near, c, z, :, lanes].astype(F32) + self.b1[near, c, z, :, lanes].astype(F32)
                total = total + self.b2[c, z, :, lanes].astype(F32)
                self.b2[c, z, :, lanes] = total.astype(self.b2.dtype)

            self.blocks(add)
        piece = lambda j: self.b2.at[:, here.z_flip(j)]
        self.go(4, piece(1), self.b3.at[0], here.z_peer(1))
        pl.when(here.edge)(self.make(5, piece(2), self.b3.at[1], here.z_peer(2)).start)
        pl.when(here.inner)(self.make(6, piece(3), self.b3.at[2], here.z_peer(3)).start)
        pl.when(here.edge)(self.make(8, piece(3), self.met, here.z_peer(1)).start)

    def stage_meet(self):
        here = self.here

        @pl.when(here.inner)
        def _():
            self.copies[8].wait_recv()
            for c in range(self.b2.shape[0]):
                place = here.z_flip(2)
                total = self.b2[c, place].astype(F32) + self.met[c].astype(F32)
                self.b2[c, place] = total.astype(self.b2.dtype)
            self.copies[5].start()

    def total(self, c):
        total = self.b2[c, self.here.z].astype(F32)
        for j in range(3):
            total = total + self.b3[j, c].astype(F32)
        return total

    def place(self, value, core):
        w = self.out.shape[-1] // 8
        for k in range(value.shape[1] // w):
            q = self.cut.start // w + k
            lanes = pl.ds(pl.multiple_of((q % 4 * 2 + core) * w, 128), w)
            self.out[q // 4, :, lanes] = value[:, k * w : (k + 1) * w]

    def stage_four(self):
        here = self.here
        self.copies[4].wait_recv()
        self.copies[5].wait_recv()
        pl.when(here.inner)(self.copies[6].wait_recv)
        if self.columns:
            self.b4s[...] = self.total(1 - here.c).astype(self.b4s.dtype)
            self.go(7, self.b4s, self.b4, here.core_peer)
            self.place(self.total(here.c), here.c)
        else:
            self.out[:, self.cut] = self.total(0)

    def finish(self):
        if self.columns:
            self.copies[7].wait_recv()
            self.place(self.b4[...].astype(F32), 1 - self.here.c)
        for slot, copy in self.copies.items():
            if slot == 6:
                pl.when(self.here.inner)(copy.wait_send)
            elif slot == 8:
                pl.when(self.here.edge)(copy.wait_send)
            else:
                copy.wait_send()


class RowOut:
    def __init__(self, here, source, out, send, recv, local):
        self.here, self.source, self.out = here, source, out
        self.send, self.recv, self.local = send, recv, local
        self.half = source.shape[-1] // 2

    def parts(self):
        here = self.here
        lanes = pl.ds(pl.multiple_of(here.c * self.half, 128), self.half)
        for k in range(4):
            source = self.source.at[k, :, lanes]
            target = self.out.at[here.z % 2, :, lanes]
            self_sent = (here.z == k) & (here.z // 2 == here.c)
            peer = (here.at, here.z // 2, k)
            away = remote(source, target, self.send.at[k], self.recv.at[here.z % 2 * 2 + here.c], peer)
            yield self_sent, away, pltpu.make_async_copy(source, target, self.local)

    def begin(self):
        for self_sent, away, stay in self.parts():
            pl.when(self_sent)(stay.start)
            pl.when(jnp.logical_not(self_sent))(away.start)

    def finish(self):
        here = self.here
        for i in range(2):
            for f in range(2):
                target = self.out.at[i, :, pl.ds(f * self.half, self.half)]
                from_self = (2 * here.c + i == here.z) & (here.c == f)
                away = remote(target, target, self.send.at[0], self.recv.at[2 * i + f], here.core_peer)
                stay = pltpu.make_async_copy(target, target, self.local)
                pl.when(from_self)(stay.wait)
                pl.when(jnp.logical_not(from_self))(away.wait_recv)
        for self_sent, away, _ in self.parts():
            pl.when(jnp.logical_not(self_sent))(away.wait_send)


def sum_kernel(column_flags, cuts, rows_at, refs):
    here = Here()
    refs = list(refs)
    take = lambda n: [refs.pop(0) for _ in range(n)]
    grads, tensors = len(column_flags), len(rows_at)
    sources, row_sources = take(grads), take(tensors)
    outs, row_outs = take(grads), take(tensors)
    scratch = [[take(7 if columns else 5) for _ in range(cut)] for columns, cut in zip(column_flags, cuts)]
    send, recv, local, row_send, row_recv, row_local = refs
    items = []
    for k in range(grads):
        for cut in range(cuts[k]):
            n, start = len(items), cut * (sources[k].shape[-1] // cuts[k])
            items.append(
                SumItem(here, sources[k], outs[k], start, scratch[k][cut], send.at[n], recv.at[n], local.at[n])
            )
    count = len(items)
    rows = [
        RowOut(here, row_sources[t], row_outs[t], row_send.at[t], row_recv.at[t], row_local.at[t])
        for t in range(tensors)
    ]
    here.enter()
    for step in range(count + 5):
        if step < count:
            items[step].stage_one()
        if 0 <= step - 1 < count:
            items[step - 1].stage_two()
        if 0 <= step - 2 < count:
            items[step - 2].stage_three()
        if 0 <= step - 3 < count:
            items[step - 3].stage_meet()
        if 0 <= step - 4 < count:
            items[step - 4].stage_four()
        if 0 <= step - 5 < count:
            items[step - 5].finish()
        for t, start in enumerate(rows_at):
            if start == step:
                rows[t].begin()
    for row in rows:
        row.finish()


def sum_all(grads, parts, rows, rows_at):
    flags = [grad.shape[2] == 2 for grad in grads]
    hbm = pl.BlockSpec(memory_space=pl.ANY)
    vmem = pl.BlockSpec(memory_space=pltpu.VMEM)
    shapes, scratch, cuts = [], [], []
    for grad, columns, number in zip(grads, flags, parts):
        _, _, cores, places, r, n = grad.shape
        shapes.append(jax.ShapeDtypeStruct((number, r, 2 * n // number) if columns else (r, n), F32))
        cuts.append(2 if grad.size > 2**SUM_CUT else 1)
        n = n // cuts[-1]
        sizes = [(2, cores, places, r, n)] * 2 + [(cores, places, r, n), (3, cores, r, n), (cores, r, n)]
        sizes += [(r, n)] * 2 if columns else []
        scratch += [pltpu.VMEM(size, grad.dtype) for size in sizes] * cuts[-1]
    count, tensors = sum(cuts), len(rows)
    row_shapes = [jax.ShapeDtypeStruct((2,) + row.shape[1:], row.dtype) for row in rows]

    def kernel(*refs):
        sum_kernel(flags, cuts, rows_at, refs)

    dma = pltpu.SemaphoreType.DMA
    return pl.pallas_call(
        kernel,
        in_specs=[hbm] * (len(grads) + tensors),
        out_specs=[vmem] * len(grads) + [hbm] * tensors,
        out_shape=shapes + row_shapes,
        scratch_shapes=scratch
        + [
            dma((count, 9)),
            dma((count, 9)),
            dma((count, 2)),
            dma((tensors, 4)),
            dma((tensors, 4)),
            dma((tensors,)),
        ],
        compiler_params=pltpu.CompilerParams(
            collective_id=1, has_side_effects=True, vmem_limit_bytes=60 * 2**20
        ),
        name="sum_all",
    )(*grads, *rows)


class Place:
    def __init__(self):
        self.core = lax.axis_index("core")
        self.z = lax.axis_index("seq")

    def over_core(self, value):
        return lax.ppermute(value, "core", [(0, 1), (1, 0)])

    def both_parts(self, part):
        part = part.astype(B16)
        return part, self.over_core(part)

    def both_cores(self, part):
        mine, other = self.both_parts(part)
        return mine.astype(F32) + other.astype(F32)


class Tree:
    def __init__(self, place):
        self.place = place

    def gather(self, table, ffb, columns, rows, tensors, tensors_at):
        n, r = table.shape
        small = jnp.pad(table, ((0, 128 - n), (0, 0))).T
        small = jnp.concatenate([small, jnp.pad(ffb, ((0, 16 - ffb.shape[0]), (0, 0)))], axis=0)
        sources = {-1: (small[None], 0, 1, "small")}
        for key, value in columns.items():
            sources[key] = value + ("columns",)
        for key, value in rows.items():
            sources[key] = value + ("rows",)
        keys = sorted(sources)
        outs = gather_all([sources[key] for key in keys], tensors, tensors_at)
        whole = {key: out for key, out in zip(keys, outs)}
        small = whole.pop(-1)
        table = small[..., :r, :].reshape(-1, 128).astype(F32).T
        ffb = small[..., r : r + ffb.shape[0], :].reshape(32, ffb.shape[0], -1).transpose(1, 0, 2)
        weights = {key: value.reshape(-1, value.shape[-1]) for key, value in whole.items()}
        return table, ffb.reshape(ffb.shape[0], -1), weights, [out.reshape(-1, out.shape[-1]) for out in outs[len(keys) :]]

    def gather_late(self, columns, rows, after):
        core = self.place.core
        mine, other = lay_side(own_columns(columns, core)), lay_side(own_columns(columns, 1 - core))
        both = jnp.stack(xor_arrange([mine, self.place.over_core(other)], core))
        width = rows.shape[1]
        wide = both.shape[2] // width
        parts = [both[:, :, k * width : (k + 1) * width].reshape(-1, width) for k in range(wide)]
        local = jnp.concatenate(parts + [rows], axis=0)
        local, _ = lax.optimization_barrier((local, after))
        full = lax.all_gather(local, ("dp", "seq"), axis=0, tiled=False)
        r = parts[0].shape[0]
        first = [full[:, k * r : (k + 1) * r].reshape(4, 4, 2, -1, width) for k in range(wide)]
        first = [part.transpose(0, 2, 1, 3, 4).reshape(-1, width) for part in first]
        return lay_wide(first), full[:, wide * r :].reshape(-1, width)

    def full_columns(self, pairs):
        return lay_wide([product_tn(features, grad).astype(B16) for features, grad in pairs])

    def full_rows(self, features, grad):
        return product_tn(features, grad).astype(B16)

    def early_columns(self, value, parts):
        core = self.place.core
        value = value.reshape(4, 2, 4, -1, value.shape[1]).transpose(0, 2, 1, 3, 4)
        value = value.reshape(16, -1, value.shape[-1])
        total = lax.psum_scatter(value, ("dp", "seq"), scatter_dimension=0, tiled=True)
        total = total.reshape(2, -1, total.shape[-1])
        mine = lax.dynamic_index_in_dim(total, core, 0, keepdims=False)
        other = lax.dynamic_index_in_dim(total, 1 - core, 0, keepdims=False)
        both = jnp.stack(xor_arrange([mine, self.place.over_core(other)], core))
        return self.weave(both, parts)

    def early_both(self, pairs, parts, features, grad):
        core = self.place.core
        values = [product_tn(f, g).astype(B16) for f, g in pairs]
        width = min([v.shape[1] for v in values] + [grad.shape[1]])
        cut = [v[:, k : k + width] for v in values for k in range(0, v.shape[1], width)]
        cut = [v.reshape(4, 2, 4, -1, width).transpose(0, 2, 1, 3, 4).reshape(16, -1, width) for v in cut]
        rows = product_tn(features, grad).astype(B16)
        rows = rows.reshape(16, -1, rows.shape[1])
        r = rows.shape[1]
        cut += [rows[:, :, k : k + width] for k in range(0, rows.shape[2], width)]
        total = lax.psum_scatter(jnp.concatenate(cut, axis=1), ("dp", "seq"), scatter_dimension=0, tiled=True)[0]
        pieces, small = len(cut) - rows.shape[2] // width, cut[0].shape[1]
        columns, rest = total[: small * pieces].reshape(pieces, 2, small // 2, width), total[small * pieces :]
        mine = lax.dynamic_index_in_dim(columns, core, 1, keepdims=False)
        other = lax.dynamic_index_in_dim(columns, 1 - core, 1, keepdims=False)
        both = jnp.stack(xor_arrange([mine, self.place.over_core(other)], core))
        both = both.astype(F32).reshape(2, parts, pieces // parts, small // 2, width)
        both = both.transpose(0, 1, 3, 2, 4).reshape(2, parts, small // 2, 4, -1)
        both = both.transpose(1, 2, 3, 0, 4).reshape(parts, small // 2, -1)
        return both, rest.astype(F32).reshape(-1, r, width).transpose(1, 0, 2).reshape(r, -1)

    def early_rows(self, value):
        return lax.psum_scatter(value, ("dp", "seq"), scatter_dimension=0, tiled=True).astype(F32)

    def weave(self, both, parts):
        r = both.shape[1]
        both = both.astype(F32).reshape(2, r, parts, 4, -1)
        return both.transpose(2, 1, 3, 0, 4).reshape(parts, r, -1)

    def sums(self, columns, rows, table, hidden, tensors):
        n, m = table.shape[0], hidden.shape[0]
        both = jnp.concatenate(
            [
                table.reshape(n, 2, 2, 4, -1).transpose(1, 2, 3, 0, 4).reshape(2, 2, 4, -1),
                hidden.reshape(m, 2, 2, 4, -1).transpose(1, 2, 3, 0, 4).reshape(2, 2, 4, -1),
            ],
            axis=-1,
        )
        size = both.shape[-1]
        both = jnp.pad(both, ((0, 0), (0, 0), (0, 0), (0, -size % 2048))).reshape(2, 2, 1, 4, 8, -1)
        grads, keys = [], []
        for key, (features, grad, _) in columns.items():
            value = product_tn(features, grad).astype(B16)
            grads.append(value.reshape(2, 2, 2, 4, value.shape[0] // 32, value.shape[1]))
            keys.append(key)
        for key, (features, grad) in rows.items():
            value = product_tn(features, grad).astype(B16)
            grads.append(value.reshape(2, 2, 1, 4, value.shape[0] // 16, value.shape[1]))
            keys.append(key)
        order = sorted(range(len(keys)), key=lambda k: keys[k])
        parts = [columns[keys[k]][2] if keys[k] in columns else 1 for k in order] + [1]
        outs = sum_all([grads[k] for k in order] + [both], parts, [t.reshape(4, -1, t.shape[-1]) for t in tensors], SUM_ROWS)
        result = {}
        for k, out in zip(order, outs):
            result[keys[k]] = out
        flat = outs[len(keys)].reshape(-1)[:size]
        edge = table.shape[1] // 16 * n
        return result, flat[:edge].reshape(n, -1), flat[edge:].reshape(m, -1), outs[len(keys) + 1 :]


class Plain:
    def __init__(self, place):
        self.place = place
        self.axes = ("dp", "core", "seq")

    def row_in(self, array):
        place = self.place
        parts = array.reshape(2, array.shape[1], 2, -1)
        got = []
        for m in range(4):
            code = place.z ^ m
            piece = lax.dynamic_index_in_dim(parts, code // 2, 0, keepdims=False)
            piece = lax.dynamic_index_in_dim(piece, code % 2, 1, keepdims=False)
            moves = []
            for c in range(2):
                for z in range(4):
                    q = m ^ z
                    moves.append((c * 4 + z, q % 2 * 4 + 2 * c + q // 2))
            got.append(lax.ppermute(piece, ("core", "seq"), moves))
        half = jnp.concatenate(xor_arrange(got, (place.z % 2) * 2 + place.core), axis=0)
        return jnp.concatenate(xor_arrange([half, place.over_core(half)], place.core), axis=1)

    def row_out(self, row):
        place = self.place
        parts = row.reshape(4, -1, 2, row.shape[1] // 2)
        mine = lax.dynamic_index_in_dim(parts, place.core, 2, keepdims=False)
        q_here = (place.z % 2) * 2 + place.core
        got = []
        for m in range(4):
            piece = lax.dynamic_index_in_dim(mine, q_here ^ m, 0, keepdims=False)
            moves = []
            for c in range(2):
                for z in range(4):
                    q = (z % 2) * 2 + c
                    moves.append((c * 4 + z, z // 2 * 4 + (m ^ q)))
            got.append(lax.ppermute(piece, ("core", "seq"), moves))
        placed = xor_arrange(got, place.z)
        return jnp.stack([jnp.concatenate(placed[2 * i : 2 * i + 2], axis=1) for i in range(2)])

    def gather(self, table, ffb, columns, rows, tensors, tensors_at):
        table = lax.all_gather(table, self.axes, axis=1, tiled=True).astype(F32)
        ffb = lax.all_gather(ffb, self.axes, axis=1, tiled=True)
        weights = {}
        for key, (value, first, number) in columns.items():
            weights[key] = self.whole_columns(value[first : first + number])
        for key, (value, first, _) in rows.items():
            weights[key] = self.whole_rows(value[first])
        return table, ffb, weights, [self.row_in(tensor) for tensor in tensors]

    def whole_columns(self, value):
        full = lax.all_gather(value, self.axes, axis=1, tiled=True)
        return lay_side(own_columns(full, self.place.core))

    def whole_rows(self, value):
        full = lax.all_gather(value, self.axes, axis=0, tiled=True)
        split = full.reshape(4, 2, full.shape[0] // 8, full.shape[1])
        mine = lax.dynamic_index_in_dim(split, self.place.core, 1, keepdims=False)
        return mine.reshape(-1, full.shape[1])

    def gather_late(self, columns, rows, after):
        return self.whole_columns(columns), self.whole_rows(rows)

    def full_columns(self, pairs):
        return lay_wide([product_tn(features, grad).astype(B16) for features, grad in pairs])

    def full_rows(self, features, grad):
        return product_tn(features, grad).astype(B16)

    def early_columns(self, full, parts):
        full = full.reshape(full.shape[0], parts, -1).transpose(1, 0, 2).astype(B16)
        return self.scatter(self.spread(full, 2), 1)

    def early_both(self, pairs, parts, features, grad):
        return self.early_columns(self.full_columns(pairs), parts), self.early_rows(self.full_rows(features, grad))

    def early_rows(self, full):
        return self.scatter(self.spread(full, 0), 0)

    def spread(self, half, axis):
        shape = half.shape[:axis] + (4, 1, half.shape[axis] // 4) + half.shape[axis + 1 :]
        half = half.reshape(shape)
        empty = jnp.zeros_like(half)
        first = jnp.where(self.place.core == 0, half, empty)
        second = jnp.where(self.place.core == 1, half, empty)
        both = jnp.concatenate([first, second], axis=axis + 1)
        return both.reshape(shape[:axis] + (-1,) + shape[axis + 3 :])

    def scatter(self, value, axis):
        return lax.psum_scatter(value, self.axes, scatter_dimension=axis, tiled=True).astype(F32)

    def sums(self, columns, rows, table, hidden, tensors):
        result = {}
        for key, (features, grad, parts) in columns.items():
            result[key] = self.early_columns(self.full_columns([(features, grad)]), parts)
        for key, (features, grad) in rows.items():
            result[key] = self.early_rows(self.full_rows(features, grad))
        small = [self.scatter(self.spread(v, 1), 1) for v in (table, hidden)]
        return result, small[0], small[1], [self.row_out(tensor) for tensor in tensors]


def on_device(
    dp,
    seq,
    src_x,
    tgt_x,
    src_seg,
    tgt_seg,
    tgt_len,
    src_lang,
    tgt_lang,
    lang_table,
    gains,
    biases,
    ff_biases,
    enc_proj,
    enc_oproj,
    enc_in,
    enc_out,
    dec_proj,
    dec_oproj,
    dec_in,
    dec_out,
    src_cot,
    tgt_cot,
):
    place = Place()
    core = place.core
    moves = Tree(place) if (dp, seq) == (4, 4) else Plain(place)
    width = enc_oproj.shape[1]
    half = width // 2
    langs = lang_table.shape[0]

    table = jnp.concatenate([lang_table, gains, biases], axis=0)
    table, ffb, weights, tensors = moves.gather(
        table,
        ff_biases,
        {0: (enc_proj, 0, 3), 2: (enc_in[None], 0, 1), 4: (dec_proj, 0, 3), 6: (dec_proj, 3, 3)},
        {1: (enc_oproj[None], 0, 1), 3: (enc_out[None], 0, 1), 5: (dec_oproj, 0, 1), 7: (dec_oproj, 1, 1)},
        [src_x, tgt_x, tgt_cot, src_cot],
        [2, 5, 8, 11],
    )
    source, target, target_cot, source_cot = tensors
    enc_qkv_w, enc_o_w, enc_in_w, enc_out_w, dec_qkv_w, dec_o_w, cross_w, cross_o_w = (
        weights[k] for k in range(8)
    )
    dec_in_w, dec_out_w = moves.gather_late(dec_in[None], dec_out, ffb)
    table, ffb_own = lax.optimization_barrier((table, own_columns(ffb, core).astype(F32)))
    languages = table[: langs + -langs % 16].astype(B16)
    gain_f = [table[langs + k : langs + k + 1] for k in range(5)]
    bias_f = [table[langs + 5 + k : langs + 6 + k] for k in range(16)]
    table_own = own_columns(table, core)
    bias_own = [table_own[langs + 5 + k : langs + 6 + k] for k in range(16)]

    meta = jnp.concatenate([src_seg, tgt_seg, tgt_len[:, None], src_lang, tgt_lang], axis=1)
    rows = jnp.where(place.z // 2 == core, meta, place.over_core(meta))
    row = lax.dynamic_index_in_dim(rows, place.z % 2, 0, keepdims=False)
    count, segs = src_seg.shape[1], src_lang.shape[1]
    s_seg, t_seg, t_len = row[:count], row[count : 2 * count], row[2 * count]
    s_lang, t_lang = row[2 * count + 1 : 2 * count + 1 + segs], row[2 * count + 1 + segs :]

    def onehot(segments, chosen):
        member = segments[:, None] == jnp.arange(segs, dtype=jnp.int32)[None, :]
        token = jnp.sum(jnp.where(member, chosen[None, :], 0), axis=1)
        return (token[:, None] == jnp.arange(langs + -langs % 16, dtype=jnp.int32)[None, :]).astype(B16)

    src_hot, tgt_hot = onehot(s_seg, s_lang), onehot(t_seg, t_lang)
    enc_masks = (block_info(False, s_seg, s_seg, t_len), s_seg[None, :], s_seg[:, None])
    dec_masks = (block_info(True, t_seg, t_seg, t_len), t_seg[None, :], t_seg[:, None])
    cross_masks = (block_info(False, t_seg, s_seg, t_len), t_seg[None, :], s_seg[:, None])

    none = jnp.zeros((1, half), F32)
    packed = (0, half // GROUP, 2 * half // GROUP)

    enc_h0 = source.astype(F32) + product(src_hot, languages)
    enc_n1 = layer_norm(enc_h0, gain_f[0], bias_f[0])
    enc_qkv_bias = jnp.concatenate([bias_own[1], none, bias_own[2]], axis=1)
    enc_qkv = (product(enc_n1, enc_qkv_w) + enc_qkv_bias).astype(B16)
    enc_mixed, enc_lse = attend_forward(False, enc_masks, enc_qkv, enc_qkv, enc_qkv, packed, half)
    enc_h1 = enc_h0 + place.both_cores(product(enc_mixed, enc_o_w)) + bias_f[3]
    enc_n2 = layer_norm(enc_h1, gain_f[1], bias_f[4])
    enc_acted, enc_slope = gelu_both(product(enc_n2, enc_in_w) + ffb_own[0:1])
    encoded = enc_h1 + place.both_cores(product(enc_acted, enc_out_w)) + bias_f[5]
    memory = encoded.astype(B16)

    dec_h0 = target.astype(F32) + product(tgt_hot, languages)
    dec_n1 = layer_norm(dec_h0, gain_f[2], bias_f[6])
    dec_qkv_bias = jnp.concatenate([bias_own[7], none, bias_own[8]], axis=1)
    dec_qkv = (product(dec_n1, dec_qkv_w) + dec_qkv_bias).astype(B16)
    dec_mixed, dec_lse = attend_forward(True, dec_masks, dec_qkv, dec_qkv, dec_qkv, packed, half)
    dec_h1 = dec_h0 + place.both_cores(product(dec_mixed, dec_o_w)) + bias_f[9]
    dec_n2 = layer_norm(dec_h1, gain_f[3], bias_f[10])
    cross_q = (product(dec_n2, cross_w[:, :half]) + bias_own[11]).astype(B16)
    cross_kv_bias = jnp.concatenate([none, bias_own[12]], axis=1)
    cross_kv = (product(memory, cross_w[:, half:]) + cross_kv_bias).astype(B16)
    apart = (0, 0, half // GROUP)
    cross_mixed, cross_lse = attend_forward(False, cross_masks, cross_q, cross_kv, cross_kv, apart, half)
    dec_h2 = dec_h1 + place.both_cores(product(cross_mixed, cross_o_w)) + bias_f[13]
    dec_n3 = layer_norm(dec_h2, gain_f[4], bias_f[14])
    dec_acted, dec_slope = gelu_both(product(dec_n3, dec_in_w) + ffb_own[1:2])
    decoded = dec_h2 + place.both_cores(product(dec_acted, dec_out_w)) + bias_f[15]

    dec_du = (product_nt(target_cot, dec_out_w) * dec_slope.astype(F32)).astype(B16)
    dec_dn3 = place.both_parts(product_nt(dec_du, dec_in_w))
    dec_out_full = moves.full_rows(dec_acted, target_cot)
    dec_in_full = moves.full_columns([(dec_n3, dec_du)])
    dec_out_grad = moves.early_rows(dec_out_full)
    dec_in_grad = moves.early_columns(dec_in_full, 1)
    grad_h2, cross_branch, cross_rows = norm_backward(dec_h2, gain_f[4], dec_dn3, target_cot)
    cross_branch, _, _ = lax.optimization_barrier((cross_branch, dec_out_full, dec_in_full))

    cross_do = product_nt(cross_branch, cross_o_w).astype(B16)
    cross_dq, cross_dkv = attend_backward(
        False, cross_masks, cross_q, cross_kv, cross_kv, apart, half, cross_mixed, cross_lse, cross_do
    )
    grad_memory = place.both_cores(product_nt(cross_dkv, cross_w[:, half:]))
    dec_dn2 = place.both_parts(product_nt(cross_dq, cross_w[:, :half]))

    cross_grad, cross_o_grad = moves.early_both(
        [(dec_n2, cross_dq), (memory, cross_dkv)], 3, cross_mixed, cross_branch
    )

    source_cot_f = source_cot.astype(F32) + grad_memory
    enc_ff_branch = source_cot_f.astype(B16)
    enc_du = (product_nt(enc_ff_branch, enc_out_w) * enc_slope.astype(F32)).astype(B16)
    enc_dn2 = place.both_parts(product_nt(enc_du, enc_in_w))

    grad_h1, self_branch, self_rows = norm_backward(dec_h1, gain_f[3], dec_dn2, grad_h2)
    dec_do = product_nt(self_branch, dec_o_w).astype(B16)
    (dec_dqkv,) = attend_backward(
        True, dec_masks, dec_qkv, dec_qkv, dec_qkv, packed, half, dec_mixed, dec_lse, dec_do
    )
    dec_dn1 = place.both_parts(product_nt(dec_dqkv, dec_qkv_w))
    target_high, target_rows, target_lang = norm_backward(dec_h0, gain_f[2], dec_dn1, grad_h1, tgt_hot)

    grad_e1, enc_branch, enc_rows = norm_backward(enc_h1, gain_f[1], enc_dn2, source_cot_f)
    enc_do = product_nt(enc_branch, enc_o_w).astype(B16)
    (enc_dqkv,) = attend_backward(
        False, enc_masks, enc_qkv, enc_qkv, enc_qkv, packed, half, enc_mixed, enc_lse, enc_do
    )
    enc_dn1 = place.both_parts(product_nt(enc_dqkv, enc_qkv_w))
    source_high, source_rows, source_lang = norm_backward(enc_h0, gain_f[0], enc_dn1, grad_e1, src_hot)

    ff_sums = jnp.stack([column_sum(enc_ff_branch), column_sum(target_cot)])
    wide = [rows[:3] for rows in (source_rows, enc_rows, target_rows, self_rows, cross_rows)]
    wide = own_columns(jnp.concatenate([source_lang + target_lang] + wide + [ff_sums], axis=0), core)
    enc_sum, dec_sum = column_sum(enc_dqkv)[None], column_sum(dec_dqkv)[None]
    narrow = [enc_sum[:, :half], enc_sum[:, 2 * half :], dec_sum[:, :half], dec_sum[:, 2 * half :]]
    narrow += [column_sum(cross_dq)[None], column_sum(cross_dkv)[None, half:]]
    small_table = jnp.concatenate([wide] + narrow, axis=0)
    at = src_hot.shape[1]
    gain_places = [at, at + 3, at + 6, at + 9, at + 12]
    bias_places = [at + k for k in (1, 17, 18, 5, 4, 15, 7, 19, 20, 11, 10, 21, 22, 14, 13, 16)]

    grads, small, ffb_grad, outputs = moves.sums(
        {
            1: (dec_n1, dec_dqkv, 3),
            2: (enc_n2, enc_du, 1),
            4: (enc_n1, enc_dqkv, 3),
        },
        {
            0: (dec_mixed, self_branch),
            3: (enc_acted, enc_ff_branch),
            5: (enc_mixed, enc_branch),
        },
        small_table,
        jnp.stack([column_sum(enc_du), column_sum(dec_du)]),
        [memory, decoded.astype(B16), source_high, target_high],
    )
    picked = lambda places: jnp.concatenate([small[k : k + 1] for k in places], axis=0)
    return (
        outputs[0],
        outputs[1],
        outputs[2].astype(F32),
        outputs[3].astype(F32),
        small[:langs],
        picked(gain_places),
        picked(bias_places),
        ffb_grad,
        grads[4],
        grads[5],
        grads[2][0],
        grads[3],
        jnp.concatenate([grads[1], cross_grad], axis=0),
        jnp.stack([grads[0], cross_o_grad]),
        dec_in_grad[0],
        dec_out_grad,
    )


def solution(mesh):
    dp, seq = mesh.shape["dp"] // 2, mesh.shape["seq"]
    pairs = Mesh(mesh.devices.reshape(dp, 2, seq), ("dp", "core", "seq"))
    both, every = ("dp", "core"), ("dp", "core", "seq")
    rows = P(both, "seq", None)
    columns = P(None, every)
    middle = P(None, every, None)
    first = P(every, None)
    weights = (columns, columns, columns, columns, middle, first, first, first, middle, middle, first, first)
    return jax.shard_map(
        functools.partial(on_device, dp, seq),
        mesh=pairs,
        in_specs=(rows, rows, P(both, None), P(both, None), P(both), P(both, None), P(both, None))
        + weights
        + (rows, rows),
        out_specs=(rows, rows, rows, rows) + weights,
        check_vma=False,
    )
```

```python
import functools

import jax
import jax.numpy as jnp
from jax import lax
from jax.experimental import pallas as pl
from jax.experimental.pallas import tpu as pltpu
from jax.sharding import Mesh
from jax.sharding import PartitionSpec as P

HEAD_DIM = 64
EPSILON = 1e-05
MASKED = -1000000000.0
BLOCK = 256
ROWS = 32
HEADS = 4
GROUP = HEADS * HEAD_DIM
B16 = jnp.bfloat16
F32 = jnp.float32


def product(left, right):
    return jnp.dot(left, right, preferred_element_type=F32)


def product_tn(left, right):
    return lax.dot_general(left, right, (((0,), (0,)), ((), ())), preferred_element_type=F32)


def product_nt(left, right):
    return lax.dot_general(left, right, (((1,), (1,)), ((), ())), preferred_element_type=F32)


def column_sum(values):
    return jnp.sum(values.astype(F32), axis=0)


def norm_parts(hidden):
    centred = hidden - jnp.mean(hidden, axis=-1, keepdims=True)
    spread = jnp.mean(centred * centred, axis=-1, keepdims=True)
    scale = lax.rsqrt(spread + EPSILON)
    return centred * scale, scale


def layer_norm(hidden, gain_row, shift_row):
    return lax.optimization_barrier((norm_parts(hidden)[0] * gain_row + shift_row).astype(B16))


def norm_backward_kernel(last, h_ref, mine_ref, other_ref, grad_ref, gain_ref, *rest):
    if last:
        hot_ref, low_ref, sums_ref, lang_ref = rest
    else:
        full_ref, low_ref, sums_ref = rest
    unit, scale = norm_parts(h_ref[...])
    down = mine_ref[...].astype(F32) + other_ref[...].astype(F32)
    weighted = down * gain_ref[...]
    step = scale * (
        weighted
        - jnp.mean(weighted, axis=-1, keepdims=True)
        - unit * jnp.mean(weighted * unit, axis=-1, keepdims=True)
    )
    full = grad_ref[...].astype(F32) + step
    low = full.astype(B16)
    low_ref[...] = low

    @pl.when(pl.program_id(0) == 0)
    def _():
        sums_ref[...] = jnp.zeros_like(sums_ref)
        if last:
            lang_ref[...] = jnp.zeros_like(lang_ref)

    for k, value in enumerate((down * unit, down, low.astype(F32))):
        sums_ref[k : k + 1, :] += jnp.sum(value, axis=0, keepdims=True)
    if last:
        hot = hot_ref[...]
        rest_low = (full - low.astype(F32)).astype(B16)
        lang_ref[...] += product_tn(hot, low) + product_tn(hot, rest_low)
    else:
        full_ref[...] = full


def norm_backward(hidden, gain_row, parts, grad, hot=None):
    count, width = hidden.shape
    last = hot is not None
    block = pl.BlockSpec((BLOCK, width), lambda i: (i, 0))
    still = lambda rows: pl.BlockSpec((rows, width), lambda i: (0, 0))
    inputs = [hidden, parts[0], parts[1], grad, gain_row] + ([hot] if last else [])
    outs = [(count, B16, block), (8, F32, still(8))]
    outs = outs + [(hot.shape[1], F32, still(hot.shape[1]))] if last else [(count, F32, block)] + outs
    return pl.pallas_call(
        functools.partial(norm_backward_kernel, last),
        grid=(count // BLOCK,),
        in_specs=[block] * 4
        + [still(1)]
        + ([pl.BlockSpec((BLOCK, hot.shape[1]), lambda i: (i, 0))] if last else []),
        out_specs=[spec for _, _, spec in outs],
        out_shape=[jax.ShapeDtypeStruct((rows, width), kind) for rows, kind, _ in outs],
        compiler_params=pltpu.CompilerParams(vmem_limit_bytes=20 * 2**20),
        cost_estimate=pl.CostEstimate(flops=30 * count * width, bytes_accessed=18 * count * width, transcendentals=0),
        name="norm_last" if last else "norm_grad",
    )(*inputs)


def gelu_both(values):
    below = 0.5 * (1.0 + lax.erf(values * (0.5**0.5)))
    density = jnp.exp(-0.5 * values * values) * (0.5 / jnp.pi) ** 0.5
    return (values * below).astype(B16), (below + values * density).astype(B16)


def allowed_rows(causal, kseg_ref, qseg, length, key_at, query_at):
    allowed = kseg_ref[key_at : key_at + ROWS, :] == qseg
    if causal:
        keys = key_at + lax.broadcasted_iota(jnp.int32, (ROWS, BLOCK), 0)
        queries = query_at + lax.broadcasted_iota(jnp.int32, (ROWS, BLOCK), 1)
        allowed = allowed & (keys <= queries) & ((keys < length) | (keys == queries))
    return allowed


def dot_nt(left, right):
    return lax.dot_general(left, right, (((1,), (1,)), ((), ())), preferred_element_type=F32)


def head_masked(value, axis=1):
    lane = lax.broadcasted_iota(jnp.int32, value.shape, axis) // HEAD_DIM
    zero = jnp.zeros_like(value)
    return [jnp.where(lane == h, value, zero) for h in range(HEADS)]


def dot_nn(left, right):
    return jnp.dot(left, right, preferred_element_type=F32)


def fold_rows(value, combine):
    return combine(value.reshape(value.shape[0] // 8, 8, value.shape[1]), axis=0)


def forward_kernel(
    causal,
    info_ref,
    q_ref,
    k_ref,
    v_ref,
    qseg_ref,
    kseg_ref,
    o_ref,
    lse_ref,
    vt_ref,
    s_ref,
    acc_ref,
    top_ref,
    sum_ref,
    qt_ref,
    e_ref,
):
    block = pl.program_id(1)
    blocks = k_ref.shape[0] // BLOCK
    length = info_ref[blocks * blocks]

    @pl.when(block == 0)
    def _():
        vt_ref[...] = v_ref[...].T

    qseg = qseg_ref[...]
    for h, head in enumerate(head_masked((q_ref[...] * jnp.asarray(HEAD_DIM**-0.5, B16)).T, 0)):
        qt_ref[h] = head
    top_ref[...] = jnp.full(top_ref.shape, -1e30, F32)
    sum_ref[...] = jnp.zeros_like(sum_ref)
    acc_ref[...] = jnp.zeros_like(acc_ref)
    for j in range(blocks):

        @pl.when(info_ref[block * blocks + j] > 0)
        def _(j=j):
            keys = k_ref[j * BLOCK : (j + 1) * BLOCK, :]
            for h in range(HEADS):
                s_ref[h, j * BLOCK : (j + 1) * BLOCK, :] = dot_nn(keys, qt_ref[h])
            top = [top_ref[h] for h in range(HEADS)]
            for at in range(j * BLOCK, (j + 1) * BLOCK, ROWS):
                allowed = allowed_rows(causal, kseg_ref, qseg, length, at, block * BLOCK)
                for h in range(HEADS):
                    scores = jnp.where(allowed, s_ref[h, at : at + ROWS, :], MASKED)
                    s_ref[h, at : at + ROWS, :] = scores
                    top[h] = jnp.maximum(top[h], fold_rows(scores, jnp.max))
            for h in range(HEADS):
                top_ref[h] = top[h]

    highest = [jnp.max(top_ref[h], axis=0, keepdims=True) for h in range(HEADS)]
    for j in range(blocks):

        @pl.when(info_ref[block * blocks + j] > 0)
        def _(j=j):
            for h in range(HEADS):
                total = sum_ref[h]
                for at in range(0, BLOCK, ROWS):
                    weights = jnp.exp(s_ref[h, j * BLOCK + at : j * BLOCK + at + ROWS, :] - highest[h])
                    total = total + fold_rows(weights, jnp.sum)
                    e_ref[h, at : at + ROWS, :] = weights.astype(B16)
                sum_ref[h] = total
                rows = slice(h * HEAD_DIM, (h + 1) * HEAD_DIM)
                acc_ref[rows, :] += dot_nn(vt_ref[rows, j * BLOCK : (j + 1) * BLOCK], e_ref[h])

    lse_ref[...] = jnp.zeros_like(lse_ref)
    for h in range(HEADS):
        total = jnp.sum(sum_ref[h], axis=0, keepdims=True)
        rows = slice(h * HEAD_DIM, (h + 1) * HEAD_DIM)
        acc_ref[rows, :] = acc_ref[rows, :] / total
        lse_ref[0, h : h + 1, :] = highest[h] + jnp.log(total)
    o_ref[...] = acc_ref[...].T.astype(B16)


def backward_kernel(
    causal,
    info_ref,
    q_ref,
    k_ref,
    v_ref,
    o_ref,
    do_ref,
    lse_ref,
    qseg_ref,
    kseg_ref,
    *rest,
):
    *outs, kt_ref, dqt_ref, sums_ref, done_ref, qt_ref, dot_ref, s_ref, dp_ref, p_ref, ds_ref, sems = rest
    group, block = pl.program_id(0), pl.program_id(1)
    groups = pl.num_programs(0)
    blocks = k_ref.shape[0] // BLOCK
    length = info_ref[blocks * blocks]

    @pl.when(block == 0)
    def _():
        kt_ref[...] = k_ref[...].T
        sums_ref[...] = jnp.zeros_like(sums_ref)

    qseg = qseg_ref[...]
    grads = do_ref[...]
    scaled = q_ref[...] * jnp.asarray(HEAD_DIM**-0.5, B16)
    grads_up = grads.T
    for h, head in enumerate(head_masked(scaled.T, 0)):
        qt_ref[h] = head
    for h, head in enumerate(head_masked(grads_up, 0)):
        dot_ref[h] = head
    queries_down = jnp.concatenate(head_masked(scaled), axis=0)
    grads_down = jnp.concatenate(head_masked(grads), axis=0)
    mixed = grads_up.astype(F32) * o_ref[...].T.astype(F32)
    inner = [
        jnp.sum(fold_rows(mixed[h * HEAD_DIM : (h + 1) * HEAD_DIM], jnp.sum), axis=0, keepdims=True)
        for h in range(HEADS)
    ]
    dqt_ref[...] = jnp.zeros_like(dqt_ref)
    for j in range(blocks):

        @pl.when(info_ref[block * blocks + j] > 0)
        def _(j=j):
            rows = slice(j * BLOCK, (j + 1) * BLOCK)
            keys = k_ref[rows, :]
            values = v_ref[rows, :]
            for h in range(HEADS):
                s_ref[h] = dot_nn(keys, qt_ref[h])
                dp_ref[h] = dot_nn(values, dot_ref[h])
            for at in range(0, BLOCK, ROWS):
                here = slice(at, at + ROWS)
                allowed = allowed_rows(causal, kseg_ref, qseg, length, j * BLOCK + at, block * BLOCK)
                for h in range(HEADS):
                    lanes = slice(h * BLOCK, (h + 1) * BLOCK)
                    chances = jnp.where(allowed, jnp.exp(s_ref[h, here, :] - lse_ref[0, h : h + 1, :]), 0.0)
                    p_ref[here, lanes] = chances.astype(B16)
                    ds_ref[here, lanes] = (chances * (dp_ref[h, here, :] - inner[h])).astype(B16)
            for h in range(HEADS):
                part = slice(h * HEAD_DIM, (h + 1) * HEAD_DIM)
                dqt_ref[part, :] += dot_nn(kt_ref[part, rows], ds_ref[:, h * BLOCK : (h + 1) * BLOCK])
            sums_ref[0, rows, :] += dot_nn(ds_ref[...], queries_down)
            sums_ref[1, rows, :] += dot_nn(p_ref[...], grads_down)

    here = pl.ds(pl.multiple_of(block * BLOCK, BLOCK), BLOCK)
    done_ref[0, here, :] = (dqt_ref[...].T * HEAD_DIM**-0.5).astype(B16)

    @pl.when(block == blocks - 1)
    def _():
        done_ref[1] = sums_ref[0].astype(B16)
        done_ref[2] = sums_ref[1].astype(B16)
        width = k_ref.shape[1]
        copies = []
        for k in range(3):
            out, place = (outs[0], k) if len(outs) == 1 else (outs[min(k, 1)], max(k - 1, 0))
            lanes = pl.ds(pl.multiple_of((place * groups + group) * width, width), width)
            copies.append(pltpu.make_async_copy(done_ref.at[k], out.at[:, lanes], sems.at[k]))
        for copy in copies:
            copy.start()
        for copy in copies:
            copy.wait()


def block_info(causal, query_seg, key_seg, length):
    blocks = query_seg.shape[0] // BLOCK
    query_low, query_high = query_seg[::BLOCK], query_seg[BLOCK - 1 :: BLOCK]
    key_low, key_high = key_seg[::BLOCK], key_seg[BLOCK - 1 :: BLOCK]
    meets = (key_low[None, :] <= query_high[:, None]) & (key_high[None, :] >= query_low[:, None])
    if causal:
        at = jnp.arange(blocks)
        meets = meets & (at[None, :] <= at[:, None])
    return jnp.concatenate([meets.astype(jnp.int32).reshape(-1), length[None]])


def attention_specs(count, offsets):
    query = pl.BlockSpec((BLOCK, GROUP), lambda p, i, info: (i, p + offsets[0]))
    key = pl.BlockSpec((count, GROUP), lambda p, i, info: (0, p + offsets[1]))
    value = pl.BlockSpec((count, GROUP), lambda p, i, info: (0, p + offsets[2]))
    plain = pl.BlockSpec((BLOCK, GROUP), lambda p, i, info: (i, p))
    whole = pl.BlockSpec((count, GROUP), lambda p, i, info: (0, p))
    stats = pl.BlockSpec((1, 8, BLOCK), lambda p, i, info: (p, 0, i))
    qseg = pl.BlockSpec((1, BLOCK), lambda p, i, info: (0, i))
    kseg = pl.BlockSpec((count, 1), lambda p, i, info: (0, 0))
    return query, key, value, plain, whole, stats, qseg, kseg


def attend_forward(causal, masks, queries, keys, values, offsets, width):
    info, qseg_row, kseg_column = masks
    count = queries.shape[0]
    groups = width // GROUP
    query, key, value, plain, _, stats, qseg, kseg = attention_specs(count, offsets)
    return pl.pallas_call(
        functools.partial(forward_kernel, causal),
        grid_spec=pltpu.PrefetchScalarGridSpec(
            num_scalar_prefetch=1,
            grid=(groups, count // BLOCK),
            in_specs=[query, key, value, qseg, kseg],
            out_specs=[plain, stats],
            scratch_shapes=[pltpu.VMEM((GROUP, count), B16), pltpu.VMEM((HEADS, count, BLOCK), F32), pltpu.VMEM((GROUP, BLOCK), F32)]
            + [pltpu.VMEM((HEADS, 8, BLOCK), F32)] * 2
            + [pltpu.VMEM((HEADS, GROUP, BLOCK), B16), pltpu.VMEM((HEADS, BLOCK, BLOCK), B16)],
        ),
        out_shape=[
            jax.ShapeDtypeStruct((count, width), B16),
            jax.ShapeDtypeStruct((groups, 8, count), F32),
        ],
        compiler_params=pltpu.CompilerParams(vmem_limit_bytes=20 * 2**20),
        cost_estimate=pl.CostEstimate(
            flops=2 * 2 * count * count * width * 2, bytes_accessed=count * width * 8, transcendentals=0
        ),
        name="attend_causal" if causal else "attend",
    )(info, queries, keys, values, qseg_row, kseg_column)


def attend_backward(causal, masks, queries, keys, values, offsets, width, mixed, lse, grad):
    widths = (3 * width,) if queries is keys else (width, 2 * width)
    info, qseg_row, kseg_column = masks
    count = queries.shape[0]
    groups = width // GROUP
    query, key, value, plain, _, stats, qseg, kseg = attention_specs(count, offsets)
    return pl.pallas_call(
        functools.partial(backward_kernel, causal),
        grid_spec=pltpu.PrefetchScalarGridSpec(
            num_scalar_prefetch=1,
            grid=(groups, count // BLOCK),
            in_specs=[query, key, value, plain, plain, stats, qseg, kseg],
            out_specs=[pl.BlockSpec(memory_space=pl.ANY)] * len(widths),
            scratch_shapes=[
                pltpu.VMEM((GROUP, count), B16),
                pltpu.VMEM((GROUP, BLOCK), F32),
                pltpu.VMEM((2, count, GROUP), F32),
                pltpu.VMEM((3, count, GROUP), B16),
                pltpu.VMEM((HEADS, GROUP, BLOCK), B16),
                pltpu.VMEM((HEADS, GROUP, BLOCK), B16),
                pltpu.VMEM((HEADS, BLOCK, BLOCK), F32),
                pltpu.VMEM((HEADS, BLOCK, BLOCK), F32),
                pltpu.VMEM((BLOCK, HEADS * BLOCK), B16),
                pltpu.VMEM((BLOCK, HEADS * BLOCK), B16),
                pltpu.SemaphoreType.DMA((3,)),
            ],
        ),
        out_shape=[jax.ShapeDtypeStruct((count, w), B16) for w in widths],
        compiler_params=pltpu.CompilerParams(vmem_limit_bytes=20 * 2**20),
        cost_estimate=pl.CostEstimate(
            flops=5 * 2 * count * count * width * 2, bytes_accessed=count * width * 16, transcendentals=0
        ),
        name="attend_grad_causal" if causal else "attend_grad",
    )(info, queries, keys, values, mixed, grad, lse, qseg_row, kseg_column)


MESH = pl.DeviceIdType.MESH
GATHER_LAGS = (0, 1, 2, 3)
ROW_LAG = 4
SUM_CUT = 20
SUM_ROWS = [1, 3, 5, 7]


def own_columns(array, core):
    w = array.shape[-1] // 8
    runs = [array[..., k * w : (k + 1) * w] for k in range(8)]
    return jnp.concatenate([jnp.where(core == 0, runs[k], runs[k + 1]) for k in range(0, 8, 2)], axis=-1)


def lay_side(array):
    return jnp.concatenate([array[i] for i in range(array.shape[0])], axis=1)


def lay_wide(arrays):
    return arrays[0] if len(arrays) == 1 else jnp.concatenate(arrays, axis=1)


def xor_arrange(pieces, place):
    pieces, bit = list(pieces), 0
    while 1 << bit < len(pieces):
        odd = ((place >> bit) & 1) == 1
        pieces = [jnp.where(odd, pieces[k ^ (1 << bit)], pieces[k]) for k in range(len(pieces))]
        bit += 1
    return pieces


class Here:
    def __init__(self):
        self.at = lax.axis_index("dp")
        self.c = lax.axis_index("core")
        self.z = lax.axis_index("seq")
        self.x = self.at % 2
        self.y = self.at // 2
        self.core_peer = (self.at, 1 - self.c, self.z)
        self.x_peer = (self.at + 1 - 2 * self.x, self.c, self.z)
        self.y_peer = (self.at + 2 - 4 * self.y, self.c, self.z)
        self.edge = (self.z % 3) == 0
        self.inner = jnp.logical_not(self.edge)

    def z_flip(self, j):
        return (self.z // 2 + j // 2) % 2 * 2 + (self.z % 2 + j % 2) % 2

    def z_peer(self, j):
        return (self.at, self.c, self.z_flip(j))

    def enter(self):
        barrier = pltpu.get_barrier_semaphore()
        peers = [self.x_peer, self.y_peer, self.core_peer]
        for j in range(1, 4):
            peers += [(self.at, self.c, self.z_flip(j)), (self.at, 1 - self.c, self.z_flip(j))]
        for peer in peers:
            pl.semaphore_signal(barrier, inc=1, device_id=peer, device_id_type=MESH)
        pl.semaphore_wait(barrier, len(peers))


def remote(source, target, send_sem, recv_sem, peer):
    return pltpu.make_async_remote_copy(
        src_ref=source,
        dst_ref=target,
        send_sem=send_sem,
        recv_sem=recv_sem,
        device_id=peer,
        device_id_type=MESH,
    )


class GatherItem:
    def __init__(self, here, source, first, kind, out, start, size, send, recv, local):
        self.here, self.source, self.first, self.kind, self.out = here, source, first, kind, out
        self.send, self.recv, self.local = send, recv, local
        self.start, self.size = start, size
        self.all = pl.ds(start, size)
        self.sides = [pl.ds(start, size // 2), pl.ds(start + size // 2, size // 2)]
        if kind == "small":
            self.sides = [self.all]
        self.core = 0 if kind == "rows" else here.c
        self.copies = {}

    def move(self, slot, region, peer, arrive=None):
        recv = self.recv.at[slot if arrive is None else arrive]
        self.copies[slot] = remote(region, region, self.send.at[slot], recv, peer)
        return self.copies[slot]

    def runs(self, core):
        w = self.source.shape[-1] // 8
        for q in range(self.start // w, (self.start + self.size) // w):
            lanes = pl.ds(pl.multiple_of((q % 4 * 2 + core) * w, 128), w)
            yield self.source.at[self.first + q // 4, :, lanes], pl.ds(q * w, w)

    def begin(self):
        here = self.here
        place = self.out.at[here.y, here.x, self.core, here.z]
        block = self.out.at[here.y, here.x, self.core, here.z, :, self.all]
        self.own = pltpu.make_async_copy(block, block, self.local)
        if self.kind == "columns":
            for source, lanes in self.runs(here.c):
                pltpu.make_async_copy(source, place.at[:, lanes], self.local).start()
            for source, lanes in self.runs(1 - here.c):
                remote(source, place.at[:, lanes], self.send.at[0], self.recv.at[0], here.core_peer).start()
        else:
            source = self.source.at[self.first, :, self.all]
            pltpu.make_async_copy(source, block, self.local).start()
            if self.kind == "small":
                remote(source, block, self.send.at[0], self.recv.at[0], here.core_peer).start()
        if self.kind != "rows":
            self.copies[0] = remote(block, block, self.send.at[0], self.recv.at[0], here.core_peer)

    def stage_z(self):
        here = self.here
        self.own.wait()
        if self.kind != "rows":
            self.copies[0].wait_recv()
        block = self.out.at[here.y, here.x, :, here.z, :, self.all]
        self.move(1, block, here.z_peer(1)).start()
        self.move(2, block, here.z_peer(2)).start()
        pl.when(here.inner)(self.move(3, block, here.z_peer(3)).start)

    def stage_pass(self):
        here = self.here
        self.copies[2].wait_recv()
        block = self.out.at[here.y, here.x, :, here.z_flip(2), :, self.all]
        pl.when(here.inner)(self.move(8, block, here.z_peer(1), arrive=3).start)

    def stage_one(self):
        here = self.here
        self.copies[1].wait_recv()
        self.copies[3].wait_recv()
        for k, peer in list(enumerate((here.x_peer, here.y_peer)))[: len(self.sides)]:
            self.move(4 + k, self.out.at[here.y, here.x, :, :, :, self.sides[k]], peer).start()

    def stage_two(self):
        here = self.here
        self.copies[4].wait_recv()
        self.move(6, self.out.at[here.y, :, :, :, :, self.sides[0]], here.y_peer).start()
        if len(self.sides) == 2:
            self.copies[5].wait_recv()
            self.move(7, self.out.at[:, here.x, :, :, :, self.sides[1]], here.x_peer).start()

    def finish(self):
        for k in range(len(self.sides)):
            self.copies[6 + k].wait_recv()
        for slot, copy in self.copies.items():
            if slot in (3, 8):
                pl.when(self.here.inner)(copy.wait_send)
            else:
                copy.wait_send()


class RowIn:
    def __init__(self, here, source, out, send, recv, local):
        self.here, self.source, self.out = here, source, out
        self.send, self.recv, self.local = send, recv, local
        self.half = source.shape[-1] // 2

    def lanes(self, f):
        return pl.ds(f * self.half, self.half) if isinstance(f, int) else pl.ds(pl.multiple_of(f * self.half, 128), self.half)

    def parts(self):
        here = self.here
        for i in range(2):
            for f in range(2):
                source = self.source.at[i, :, self.lanes(f)]
                target = self.out.at[here.z, :, self.lanes(f)]
                self_sent = (2 * here.c + i == here.z) & (here.c == f)
                peer = (here.at, f, 2 * here.c + i)
                away = remote(source, target, self.send.at[2 * i + f], self.recv.at[here.z], peer)
                stay = pltpu.make_async_copy(source, target, self.local)
                yield self_sent, away, stay

    def begin(self):
        for self_sent, away, stay in self.parts():
            pl.when(self_sent)(stay.start)
            pl.when(jnp.logical_not(self_sent))(away.start)

    def across(self):
        here = self.here
        lanes = self.lanes(here.c)
        for k in range(4):
            target = self.out.at[k, :, lanes]
            from_self = (here.z == k) & (here.z // 2 == here.c)
            stay = pltpu.make_async_copy(target, target, self.local)
            away = remote(target, target, self.send.at[0], self.recv.at[k], here.core_peer)
            pl.when(from_self)(stay.wait)
            pl.when(jnp.logical_not(from_self))(away.wait_recv)
        region = self.out.at[:, :, lanes]
        self.copy = remote(region, region, self.send.at[4], self.recv.at[4], here.core_peer)
        self.copy.start()

    def finish(self):
        self.copy.wait()
        for self_sent, away, _ in self.parts():
            pl.when(jnp.logical_not(self_sent))(away.wait_send)


def gather_kernel(kinds, cuts, rows_at, refs):
    here = Here()
    refs = list(refs)
    take = lambda n: [refs.pop(0) for _ in range(n)]
    count = len(kinds)
    ins = take(count)
    row_ins = take(len(rows_at))
    outs = take(count)
    row_outs = take(len(rows_at))
    send, recv, local, row_send, row_recv, row_local = refs
    items = []
    for k, (first, kind) in enumerate(kinds):
        size = outs[k].shape[-1] // cuts[k]
        for cut in range(cuts[k]):
            n = len(items)
            sems = send.at[n], recv.at[n], local.at[n]
            items.append(GatherItem(here, ins[k], first, kind, outs[k], cut * size, size, *sems))
    count = len(items)
    rows = [
        RowIn(here, row_ins[t], row_outs[t], row_send.at[t], row_recv.at[t], row_local.at[t])
        for t in range(len(rows_at))
    ]
    here.enter()
    for item in items:
        item.begin()
    steps = (GatherItem.stage_z, GatherItem.stage_pass, GatherItem.stage_one, GatherItem.stage_two)
    for step in range(count + GATHER_LAGS[-1] + 1):
        for t, start in enumerate(rows_at):
            if start == step:
                rows[t].begin()
            if min(start + ROW_LAG, count + GATHER_LAGS[-1]) == step:
                rows[t].across()
        for stage, lag in zip(steps, GATHER_LAGS):
            if 0 <= step - lag < count:
                stage(items[step - lag])
    for item in items:
        item.finish()
    for row in rows:
        row.finish()


def gather_all(sources, rows, rows_at):
    kinds = [(first, kind) for _, first, _, kind in sources]
    inputs = [source[0] for source in sources] + list(rows)
    shapes, cuts = [], []
    for array, _, number, kind in sources:
        _, r, n = array.shape
        n = number * n // 2 if kind == "columns" else n
        shapes.append(jax.ShapeDtypeStruct((2, 2, 1 if kind == "rows" else 2, 4, r, n), array.dtype))
        cuts.append(2 if r * n * (2 if kind == "columns" else 1) > 2**16 else 1)
    shapes += [jax.ShapeDtypeStruct((4,) + row.shape[1:], row.dtype) for row in rows]
    count, tensors = sum(cuts), len(rows)
    hbm = pl.BlockSpec(memory_space=pl.ANY)

    def kernel(*refs):
        gather_kernel(kinds, cuts, rows_at, refs)

    dma = pltpu.SemaphoreType.DMA
    return pl.pallas_call(
        kernel,
        in_specs=[hbm] * len(inputs),
        out_specs=[hbm] * len(shapes),
        out_shape=shapes,
        scratch_shapes=[
            dma((count, 9)),
            dma((count, 9)),
            dma((count,)),
            dma((tensors, 5)),
            dma((tensors, 5)),
            dma((tensors,)),
        ],
        compiler_params=pltpu.CompilerParams(collective_id=0, has_side_effects=True),
        name="gather_all",
    )(*inputs)


class SumItem:
    def __init__(self, here, source, out, start, scratch, send, recv, local):
        self.here, self.source, self.out = here, source, out
        self.own, self.b1, self.b2, self.b3, self.met = scratch[:5]
        self.columns = source.shape[2] == 2
        if self.columns:
            self.b4, self.b4s = scratch[5:]
        self.send, self.recv, self.local = send, recv, local
        size = self.own.shape[-1]
        self.half = size // 2
        self.sides = pl.ds(0, self.half), pl.ds(self.half, self.half)
        self.cut = slice(start, start + size)
        self.source_sides = pl.ds(start, self.half), pl.ds(start + self.half, self.half)
        self.copies = {}

    def make(self, slot, source, target, peer):
        self.copies[slot] = remote(source, target, self.send.at[slot], self.recv.at[slot], peer)
        return self.copies[slot]

    def go(self, slot, source, target, peer):
        self.make(slot, source, target, peer).start()

    def blocks(self, body):
        cores = self.b2.shape[0]

        def step(k, carry):
            body(k // 4, k % 4)
            return carry

        lax.fori_loop(0, cores * 4, step, 0)

    def stage_one(self):
        here, (a, b), source = self.here, self.sides, self.source
        first, second = self.source_sides
        self.go(0, source.at[:, 1 - here.x, :, :, :, first], self.b1.at[:, :, :, :, a], here.x_peer)
        self.go(1, source.at[1 - here.y, :, :, :, :, second], self.b1.at[:, :, :, :, b], here.y_peer)
        self.loads = [
            pltpu.make_async_copy(source.at[:, here.x, :, :, :, first], self.own.at[:, :, :, :, a], self.local.at[0]),
            pltpu.make_async_copy(source.at[here.y, :, :, :, :, second], self.own.at[:, :, :, :, b], self.local.at[1]),
        ]
        for load in self.loads:
            load.start()

        @pl.when(here.edge)
        def _():
            self.b3[2] = jnp.zeros(self.b3.shape[1:], self.b3.dtype)

    def stage_two(self):
        here = self.here
        for side, near, peer in ((0, here.y, here.y_peer), (1, here.x, here.x_peer)):
            lanes = self.sides[side]
            away = 1 - near
            self.loads[side].wait()
            self.copies[side].wait_recv()

            def add(c, z, away=away, lanes=lanes):
                total = self.own[away, c, z, :, lanes].astype(F32) + self.b1[away, c, z, :, lanes].astype(F32)
                self.own[away, c, z, :, lanes] = total.astype(self.own.dtype)

            self.blocks(add)
            self.go(2 + side, self.own.at[away, :, :, :, lanes], self.b2.at[:, :, :, lanes], peer)

    def stage_three(self):
        here = self.here
        for side, near in ((0, here.y), (1, here.x)):
            lanes = self.sides[side]
            self.copies[2 + side].wait_recv()

            def add(c, z, near=near, lanes=lanes):
                total = self.own[near, c, z, :, lanes].astype(F32) + self.b1[near, c, z, :, lanes].astype(F32)
                total = total + self.b2[c, z, :, lanes].astype(F32)
                self.b2[c, z, :, lanes] = total.astype(self.b2.dtype)

            self.blocks(add)
        piece = lambda j: self.b2.at[:, here.z_flip(j)]
        self.go(4, piece(1), self.b3.at[0], here.z_peer(1))
        pl.when(here.edge)(self.make(5, piece(2), self.b3.at[1], here.z_peer(2)).start)
        pl.when(here.inner)(self.make(6, piece(3), self.b3.at[2], here.z_peer(3)).start)
        pl.when(here.edge)(self.make(8, piece(3), self.met, here.z_peer(1)).start)

    def stage_meet(self):
        here = self.here

        @pl.when(here.inner)
        def _():
            self.copies[8].wait_recv()
            for c in range(self.b2.shape[0]):
                place = here.z_flip(2)
                total = self.b2[c, place].astype(F32) + self.met[c].astype(F32)
                self.b2[c, place] = total.astype(self.b2.dtype)
            self.copies[5].start()

    def total(self, c):
        total = self.b2[c, self.here.z].astype(F32)
        for j in range(3):
            total = total + self.b3[j, c].astype(F32)
        return total

    def place(self, value, core):
        w = self.out.shape[-1] // 8
        for k in range(value.shape[1] // w):
            q = self.cut.start // w + k
            lanes = pl.ds(pl.multiple_of((q % 4 * 2 + core) * w, 128), w)
            self.out[q // 4, :, lanes] = value[:, k * w : (k + 1) * w]

    def stage_four(self):
        here = self.here
        self.copies[4].wait_recv()
        self.copies[5].wait_recv()
        pl.when(here.inner)(self.copies[6].wait_recv)
        if self.columns:
            self.b4s[...] = self.total(1 - here.c).astype(self.b4s.dtype)
            self.go(7, self.b4s, self.b4, here.core_peer)
            self.place(self.total(here.c), here.c)
        else:
            self.out[:, self.cut] = self.total(0)

    def finish(self):
        if self.columns:
            self.copies[7].wait_recv()
            self.place(self.b4[...].astype(F32), 1 - self.here.c)
        for slot, copy in self.copies.items():
            if slot == 6:
                pl.when(self.here.inner)(copy.wait_send)
            elif slot == 8:
                pl.when(self.here.edge)(copy.wait_send)
            else:
                copy.wait_send()


class RowOut:
    def __init__(self, here, source, out, send, recv, local):
        self.here, self.source, self.out = here, source, out
        self.send, self.recv, self.local = send, recv, local
        self.half = source.shape[-1] // 2

    def parts(self):
        here = self.here
        lanes = pl.ds(pl.multiple_of(here.c * self.half, 128), self.half)
        for k in range(4):
            source = self.source.at[k, :, lanes]
            target = self.out.at[here.z % 2, :, lanes]
            self_sent = (here.z == k) & (here.z // 2 == here.c)
            peer = (here.at, here.z // 2, k)
            away = remote(source, target, self.send.at[k], self.recv.at[here.z % 2 * 2 + here.c], peer)
            yield self_sent, away, pltpu.make_async_copy(source, target, self.local)

    def begin(self):
        for self_sent, away, stay in self.parts():
            pl.when(self_sent)(stay.start)
            pl.when(jnp.logical_not(self_sent))(away.start)

    def finish(self):
        here = self.here
        for i in range(2):
            for f in range(2):
                target = self.out.at[i, :, pl.ds(f * self.half, self.half)]
                from_self = (2 * here.c + i == here.z) & (here.c == f)
                away = remote(target, target, self.send.at[0], self.recv.at[2 * i + f], here.core_peer)
                stay = pltpu.make_async_copy(target, target, self.local)
                pl.when(from_self)(stay.wait)
                pl.when(jnp.logical_not(from_self))(away.wait_recv)
        for self_sent, away, _ in self.parts():
            pl.when(jnp.logical_not(self_sent))(away.wait_send)


def sum_kernel(column_flags, cuts, rows_at, refs):
    here = Here()
    refs = list(refs)
    take = lambda n: [refs.pop(0) for _ in range(n)]
    grads, tensors = len(column_flags), len(rows_at)
    sources, row_sources = take(grads), take(tensors)
    outs, row_outs = take(grads), take(tensors)
    scratch = [[take(7 if columns else 5) for _ in range(cut)] for columns, cut in zip(column_flags, cuts)]
    send, recv, local, row_send, row_recv, row_local = refs
    items = []
    for k in range(grads):
        for cut in range(cuts[k]):
            n, start = len(items), cut * (sources[k].shape[-1] // cuts[k])
            items.append(
                SumItem(here, sources[k], outs[k], start, scratch[k][cut], send.at[n], recv.at[n], local.at[n])
            )
    count = len(items)
    rows = [
        RowOut(here, row_sources[t], row_outs[t], row_send.at[t], row_recv.at[t], row_local.at[t])
        for t in range(tensors)
    ]
    here.enter()
    for step in range(count + 5):
        if step < count:
            items[step].stage_one()
        if 0 <= step - 1 < count:
            items[step - 1].stage_two()
        if 0 <= step - 2 < count:
            items[step - 2].stage_three()
        if 0 <= step - 3 < count:
            items[step - 3].stage_meet()
        if 0 <= step - 4 < count:
            items[step - 4].stage_four()
        if 0 <= step - 5 < count:
            items[step - 5].finish()
        for t, start in enumerate(rows_at):
            if start == step:
                rows[t].begin()
    for row in rows:
        row.finish()


def sum_all(grads, parts, rows, rows_at):
    flags = [grad.shape[2] == 2 for grad in grads]
    hbm = pl.BlockSpec(memory_space=pl.ANY)
    vmem = pl.BlockSpec(memory_space=pltpu.VMEM)
    shapes, scratch, cuts = [], [], []
    for grad, columns, number in zip(grads, flags, parts):
        _, _, cores, places, r, n = grad.shape
        shapes.append(jax.ShapeDtypeStruct((number, r, 2 * n // number) if columns else (r, n), F32))
        cuts.append(2 if grad.size > 2**SUM_CUT else 1)
        n = n // cuts[-1]
        sizes = [(2, cores, places, r, n)] * 2 + [(cores, places, r, n), (3, cores, r, n), (cores, r, n)]
        sizes += [(r, n)] * 2 if columns else []
        scratch += [pltpu.VMEM(size, grad.dtype) for size in sizes] * cuts[-1]
    count, tensors = sum(cuts), len(rows)
    row_shapes = [jax.ShapeDtypeStruct((2,) + row.shape[1:], row.dtype) for row in rows]

    def kernel(*refs):
        sum_kernel(flags, cuts, rows_at, refs)

    dma = pltpu.SemaphoreType.DMA
    return pl.pallas_call(
        kernel,
        in_specs=[hbm] * (len(grads) + tensors),
        out_specs=[vmem] * len(grads) + [hbm] * tensors,
        out_shape=shapes + row_shapes,
        scratch_shapes=scratch
        + [
            dma((count, 9)),
            dma((count, 9)),
            dma((count, 2)),
            dma((tensors, 4)),
            dma((tensors, 4)),
            dma((tensors,)),
        ],
        compiler_params=pltpu.CompilerParams(
            collective_id=1, has_side_effects=True, vmem_limit_bytes=60 * 2**20
        ),
        name="sum_all",
    )(*grads, *rows)


class Place:
    def __init__(self):
        self.core = lax.axis_index("core")
        self.z = lax.axis_index("seq")

    def over_core(self, value):
        return lax.ppermute(value, "core", [(0, 1), (1, 0)])

    def both_parts(self, part):
        part = part.astype(B16)
        return part, self.over_core(part)

    def both_cores(self, part):
        mine, other = self.both_parts(part)
        return mine.astype(F32) + other.astype(F32)


class Tree:
    def __init__(self, place):
        self.place = place

    def gather(self, table, ffb, columns, rows, tensors, tensors_at):
        n, r = table.shape
        small = jnp.pad(table, ((0, 128 - n), (0, 0))).T
        small = jnp.concatenate([small, jnp.pad(ffb, ((0, 16 - ffb.shape[0]), (0, 0)))], axis=0)
        sources = {-1: (small[None], 0, 1, "small")}
        for key, value in columns.items():
            sources[key] = value + ("columns",)
        for key, value in rows.items():
            sources[key] = value + ("rows",)
        keys = sorted(sources)
        outs = gather_all([sources[key] for key in keys], tensors, tensors_at)
        whole = {key: out for key, out in zip(keys, outs)}
        small = whole.pop(-1)
        table = small[..., :r, :].reshape(-1, 128).astype(F32).T
        ffb = small[..., r : r + ffb.shape[0], :].reshape(32, ffb.shape[0], -1).transpose(1, 0, 2)
        weights = {key: value.reshape(-1, value.shape[-1]) for key, value in whole.items()}
        return table, ffb.reshape(ffb.shape[0], -1), weights, [out.reshape(-1, out.shape[-1]) for out in outs[len(keys) :]]

    def gather_late(self, columns, rows, after):
        core = self.place.core
        mine, other = lay_side(own_columns(columns, core)), lay_side(own_columns(columns, 1 - core))
        both = jnp.stack(xor_arrange([mine, self.place.over_core(other)], core))
        width = rows.shape[1]
        wide = both.shape[2] // width
        parts = [both[:, :, k * width : (k + 1) * width].reshape(-1, width) for k in range(wide)]
        local = jnp.concatenate(parts + [rows], axis=0)
        local, _ = lax.optimization_barrier((local, after))
        full = lax.all_gather(local, ("dp", "seq"), axis=0, tiled=False)
        r = parts[0].shape[0]
        first = [full[:, k * r : (k + 1) * r].reshape(4, 4, 2, -1, width) for k in range(wide)]
        first = [part.transpose(0, 2, 1, 3, 4).reshape(-1, width) for part in first]
        return lay_wide(first), full[:, wide * r :].reshape(-1, width)

    def full_columns(self, pairs):
        return lay_wide([product_tn(features, grad).astype(B16) for features, grad in pairs])

    def full_rows(self, features, grad):
        return product_tn(features, grad).astype(B16)

    def early_columns(self, value, parts):
        core = self.place.core
        value = value.reshape(4, 2, 4, -1, value.shape[1]).transpose(0, 2, 1, 3, 4)
        value = value.reshape(16, -1, value.shape[-1])
        total = lax.psum_scatter(value, ("dp", "seq"), scatter_dimension=0, tiled=True)
        total = total.reshape(2, -1, total.shape[-1])
        mine = lax.dynamic_index_in_dim(total, core, 0, keepdims=False)
        other = lax.dynamic_index_in_dim(total, 1 - core, 0, keepdims=False)
        both = jnp.stack(xor_arrange([mine, self.place.over_core(other)], core))
        return self.weave(both, parts)

    def early_both(self, pairs, parts, features, grad):
        core = self.place.core
        values = [product_tn(f, g).astype(B16) for f, g in pairs]
        width = min([v.shape[1] for v in values] + [grad.shape[1]])
        cut = [v[:, k : k + width] for v in values for k in range(0, v.shape[1], width)]
        cut = [v.reshape(4, 2, 4, -1, width).transpose(0, 2, 1, 3, 4).reshape(16, -1, width) for v in cut]
        rows = product_tn(features, grad).astype(B16)
        rows = rows.reshape(16, -1, rows.shape[1])
        r = rows.shape[1]
        cut += [rows[:, :, k : k + width] for k in range(0, rows.shape[2], width)]
        total = lax.psum_scatter(jnp.concatenate(cut, axis=1), ("dp", "seq"), scatter_dimension=0, tiled=True)[0]
        pieces, small = len(cut) - rows.shape[2] // width, cut[0].shape[1]
        columns, rest = total[: small * pieces].reshape(pieces, 2, small // 2, width), total[small * pieces :]
        mine = lax.dynamic_index_in_dim(columns, core, 1, keepdims=False)
        other = lax.dynamic_index_in_dim(columns, 1 - core, 1, keepdims=False)
        both = jnp.stack(xor_arrange([mine, self.place.over_core(other)], core))
        both = both.astype(F32).reshape(2, parts, pieces // parts, small // 2, width)
        both = both.transpose(0, 1, 3, 2, 4).reshape(2, parts, small // 2, 4, -1)
        both = both.transpose(1, 2, 3, 0, 4).reshape(parts, small // 2, -1)
        return both, rest.astype(F32).reshape(-1, r, width).transpose(1, 0, 2).reshape(r, -1)

    def early_rows(self, value):
        return lax.psum_scatter(value, ("dp", "seq"), scatter_dimension=0, tiled=True).astype(F32)

    def weave(self, both, parts):
        r = both.shape[1]
        both = both.astype(F32).reshape(2, r, parts, 4, -1)
        return both.transpose(2, 1, 3, 0, 4).reshape(parts, r, -1)

    def sums(self, columns, rows, table, hidden, tensors):
        n, m = table.shape[0], hidden.shape[0]
        both = jnp.concatenate(
            [
                table.reshape(n, 2, 2, 4, -1).transpose(1, 2, 3, 0, 4).reshape(2, 2, 4, -1),
                hidden.reshape(m, 2, 2, 4, -1).transpose(1, 2, 3, 0, 4).reshape(2, 2, 4, -1),
            ],
            axis=-1,
        )
        size = both.shape[-1]
        both = jnp.pad(both, ((0, 0), (0, 0), (0, 0), (0, -size % 2048))).reshape(2, 2, 1, 4, 8, -1)
        grads, keys = [], []
        for key, (features, grad, _) in columns.items():
            value = product_tn(features, grad).astype(B16)
            grads.append(value.reshape(2, 2, 2, 4, value.shape[0] // 32, value.shape[1]))
            keys.append(key)
        for key, (features, grad) in rows.items():
            value = product_tn(features, grad).astype(B16)
            grads.append(value.reshape(2, 2, 1, 4, value.shape[0] // 16, value.shape[1]))
            keys.append(key)
        order = sorted(range(len(keys)), key=lambda k: keys[k])
        parts = [columns[keys[k]][2] if keys[k] in columns else 1 for k in order] + [1]
        outs = sum_all([grads[k] for k in order] + [both], parts, [t.reshape(4, -1, t.shape[-1]) for t in tensors], SUM_ROWS)
        result = {}
        for k, out in zip(order, outs):
            result[keys[k]] = out
        flat = outs[len(keys)].reshape(-1)[:size]
        edge = table.shape[1] // 16 * n
        return result, flat[:edge].reshape(n, -1), flat[edge:].reshape(m, -1), outs[len(keys) + 1 :]


class Plain:
    def __init__(self, place):
        self.place = place
        self.axes = ("dp", "core", "seq")

    def row_in(self, array):
        place = self.place
        parts = array.reshape(2, array.shape[1], 2, -1)
        got = []
        for m in range(4):
            code = place.z ^ m
            piece = lax.dynamic_index_in_dim(parts, code // 2, 0, keepdims=False)
            piece = lax.dynamic_index_in_dim(piece, code % 2, 1, keepdims=False)
            moves = []
            for c in range(2):
                for z in range(4):
                    q = m ^ z
                    moves.append((c * 4 + z, q % 2 * 4 + 2 * c + q // 2))
            got.append(lax.ppermute(piece, ("core", "seq"), moves))
        half = jnp.concatenate(xor_arrange(got, (place.z % 2) * 2 + place.core), axis=0)
        return jnp.concatenate(xor_arrange([half, place.over_core(half)], place.core), axis=1)

    def row_out(self, row):
        place = self.place
        parts = row.reshape(4, -1, 2, row.shape[1] // 2)
        mine = lax.dynamic_index_in_dim(parts, place.core, 2, keepdims=False)
        q_here = (place.z % 2) * 2 + place.core
        got = []
        for m in range(4):
            piece = lax.dynamic_index_in_dim(mine, q_here ^ m, 0, keepdims=False)
            moves = []
            for c in range(2):
                for z in range(4):
                    q = (z % 2) * 2 + c
                    moves.append((c * 4 + z, z // 2 * 4 + (m ^ q)))
            got.append(lax.ppermute(piece, ("core", "seq"), moves))
        placed = xor_arrange(got, place.z)
        return jnp.stack([jnp.concatenate(placed[2 * i : 2 * i + 2], axis=1) for i in range(2)])

    def gather(self, table, ffb, columns, rows, tensors, tensors_at):
        table = lax.all_gather(table, self.axes, axis=1, tiled=True).astype(F32)
        ffb = lax.all_gather(ffb, self.axes, axis=1, tiled=True)
        weights = {}
        for key, (value, first, number) in columns.items():
            weights[key] = self.whole_columns(value[first : first + number])
        for key, (value, first, _) in rows.items():
            weights[key] = self.whole_rows(value[first])
        return table, ffb, weights, [self.row_in(tensor) for tensor in tensors]

    def whole_columns(self, value):
        full = lax.all_gather(value, self.axes, axis=1, tiled=True)
        return lay_side(own_columns(full, self.place.core))

    def whole_rows(self, value):
        full = lax.all_gather(value, self.axes, axis=0, tiled=True)
        split = full.reshape(4, 2, full.shape[0] // 8, full.shape[1])
        mine = lax.dynamic_index_in_dim(split, self.place.core, 1, keepdims=False)
        return mine.reshape(-1, full.shape[1])

    def gather_late(self, columns, rows, after):
        return self.whole_columns(columns), self.whole_rows(rows)

    def full_columns(self, pairs):
        return lay_wide([product_tn(features, grad).astype(B16) for features, grad in pairs])

    def full_rows(self, features, grad):
        return product_tn(features, grad).astype(B16)

    def early_columns(self, full, parts):
        full = full.reshape(full.shape[0], parts, -1).transpose(1, 0, 2).astype(B16)
        return self.scatter(self.spread(full, 2), 1)

    def early_both(self, pairs, parts, features, grad):
        return self.early_columns(self.full_columns(pairs), parts), self.early_rows(self.full_rows(features, grad))

    def early_rows(self, full):
        return self.scatter(self.spread(full, 0), 0)

    def spread(self, half, axis):
        shape = half.shape[:axis] + (4, 1, half.shape[axis] // 4) + half.shape[axis + 1 :]
        half = half.reshape(shape)
        empty = jnp.zeros_like(half)
        first = jnp.where(self.place.core == 0, half, empty)
        second = jnp.where(self.place.core == 1, half, empty)
        both = jnp.concatenate([first, second], axis=axis + 1)
        return both.reshape(shape[:axis] + (-1,) + shape[axis + 3 :])

    def scatter(self, value, axis):
        return lax.psum_scatter(value, self.axes, scatter_dimension=axis, tiled=True).astype(F32)

    def sums(self, columns, rows, table, hidden, tensors):
        result = {}
        for key, (features, grad, parts) in columns.items():
            result[key] = self.early_columns(self.full_columns([(features, grad)]), parts)
        for key, (features, grad) in rows.items():
            result[key] = self.early_rows(self.full_rows(features, grad))
        small = [self.scatter(self.spread(v, 1), 1) for v in (table, hidden)]
        return result, small[0], small[1], [self.row_out(tensor) for tensor in tensors]


def on_device(
    dp,
    seq,
    src_x,
    tgt_x,
    src_seg,
    tgt_seg,
    tgt_len,
    src_lang,
    tgt_lang,
    lang_table,
    gains,
    biases,
    ff_biases,
    enc_proj,
    enc_oproj,
    enc_in,
    enc_out,
    dec_proj,
    dec_oproj,
    dec_in,
    dec_out,
    src_cot,
    tgt_cot,
):
    place = Place()
    core = place.core
    moves = Tree(place) if (dp, seq) == (4, 4) else Plain(place)
    width = enc_oproj.shape[1]
    half = width // 2
    langs = lang_table.shape[0]

    table = jnp.concatenate([lang_table, gains, biases], axis=0)
    table, ffb, weights, tensors = moves.gather(
        table,
        ff_biases,
        {0: (enc_proj, 0, 3), 2: (enc_in[None], 0, 1), 4: (dec_proj, 0, 3), 6: (dec_proj, 3, 3)},
        {1: (enc_oproj[None], 0, 1), 3: (enc_out[None], 0, 1), 5: (dec_oproj, 0, 1), 7: (dec_oproj, 1, 1)},
        [src_x, tgt_x, tgt_cot, src_cot],
        [2, 5, 8, 11],
    )
    source, target, target_cot, source_cot = tensors
    enc_qkv_w, enc_o_w, enc_in_w, enc_out_w, dec_qkv_w, dec_o_w, cross_w, cross_o_w = (
        weights[k] for k in range(8)
    )
    dec_in_w, dec_out_w = moves.gather_late(dec_in[None], dec_out, ffb)
    table, ffb_own = lax.optimization_barrier((table, own_columns(ffb, core).astype(F32)))
    languages = table[: langs + -langs % 16].astype(B16)
    gain_f = [table[langs + k : langs + k + 1] for k in range(5)]
    bias_f = [table[langs + 5 + k : langs + 6 + k] for k in range(16)]
    table_own = own_columns(table, core)
    bias_own = [table_own[langs + 5 + k : langs + 6 + k] for k in range(16)]

    meta = jnp.concatenate([src_seg, tgt_seg, tgt_len[:, None], src_lang, tgt_lang], axis=1)
    rows = jnp.where(place.z // 2 == core, meta, place.over_core(meta))
    row = lax.dynamic_index_in_dim(rows, place.z % 2, 0, keepdims=False)
    count, segs = src_seg.shape[1], src_lang.shape[1]
    s_seg, t_seg, t_len = row[:count], row[count : 2 * count], row[2 * count]
    s_lang, t_lang = row[2 * count + 1 : 2 * count + 1 + segs], row[2 * count + 1 + segs :]

    def onehot(segments, chosen):
        member = segments[:, None] == jnp.arange(segs, dtype=jnp.int32)[None, :]
        token = jnp.sum(jnp.where(member, chosen[None, :], 0), axis=1)
        return (token[:, None] == jnp.arange(langs + -langs % 16, dtype=jnp.int32)[None, :]).astype(B16)

    src_hot, tgt_hot = onehot(s_seg, s_lang), onehot(t_seg, t_lang)
    enc_masks = (block_info(False, s_seg, s_seg, t_len), s_seg[None, :], s_seg[:, None])
    dec_masks = (block_info(True, t_seg, t_seg, t_len), t_seg[None, :], t_seg[:, None])
    cross_masks = (block_info(False, t_seg, s_seg, t_len), t_seg[None, :], s_seg[:, None])

    none = jnp.zeros((1, half), F32)
    packed = (0, half // GROUP, 2 * half // GROUP)

    enc_h0 = source.astype(F32) + product(src_hot, languages)
    enc_n1 = layer_norm(enc_h0, gain_f[0], bias_f[0])
    enc_qkv_bias = jnp.concatenate([bias_own[1], none, bias_own[2]], axis=1)
    enc_qkv = (product(enc_n1, enc_qkv_w) + enc_qkv_bias).astype(B16)
    enc_mixed, enc_lse = attend_forward(False, enc_masks, enc_qkv, enc_qkv, enc_qkv, packed, half)
    enc_h1 = enc_h0 + place.both_cores(product(enc_mixed, enc_o_w)) + bias_f[3]
    enc_n2 = layer_norm(enc_h1, gain_f[1], bias_f[4])
    enc_acted, enc_slope = gelu_both(product(enc_n2, enc_in_w) + ffb_own[0:1])
    encoded = enc_h1 + place.both_cores(product(enc_acted, enc_out_w)) + bias_f[5]
    memory = encoded.astype(B16)

    dec_h0 = target.astype(F32) + product(tgt_hot, languages)
    dec_n1 = layer_norm(dec_h0, gain_f[2], bias_f[6])
    dec_qkv_bias = jnp.concatenate([bias_own[7], none, bias_own[8]], axis=1)
    dec_qkv = (product(dec_n1, dec_qkv_w) + dec_qkv_bias).astype(B16)
    dec_mixed, dec_lse = attend_forward(True, dec_masks, dec_qkv, dec_qkv, dec_qkv, packed, half)
    dec_h1 = dec_h0 + place.both_cores(product(dec_mixed, dec_o_w)) + bias_f[9]
    dec_n2 = layer_norm(dec_h1, gain_f[3], bias_f[10])
    cross_q = (product(dec_n2, cross_w[:, :half]) + bias_own[11]).astype(B16)
    cross_kv_bias = jnp.concatenate([none, bias_own[12]], axis=1)
    cross_kv = (product(memory, cross_w[:, half:]) + cross_kv_bias).astype(B16)
    apart = (0, 0, half // GROUP)
    cross_mixed, cross_lse = attend_forward(False, cross_masks, cross_q, cross_kv, cross_kv, apart, half)
    dec_h2 = dec_h1 + place.both_cores(product(cross_mixed, cross_o_w)) + bias_f[13]
    dec_n3 = layer_norm(dec_h2, gain_f[4], bias_f[14])
    dec_acted, dec_slope = gelu_both(product(dec_n3, dec_in_w) + ffb_own[1:2])
    decoded = dec_h2 + place.both_cores(product(dec_acted, dec_out_w)) + bias_f[15]

    dec_du = (product_nt(target_cot, dec_out_w) * dec_slope.astype(F32)).astype(B16)
    dec_dn3 = place.both_parts(product_nt(dec_du, dec_in_w))
    dec_out_full = moves.full_rows(dec_acted, target_cot)
    dec_in_full = moves.full_columns([(dec_n3, dec_du)])
    dec_out_grad = moves.early_rows(dec_out_full)
    dec_in_grad = moves.early_columns(dec_in_full, 1)
    grad_h2, cross_branch, cross_rows = norm_backward(dec_h2, gain_f[4], dec_dn3, target_cot)
    cross_branch, _, _ = lax.optimization_barrier((cross_branch, dec_out_full, dec_in_full))

    cross_do = product_nt(cross_branch, cross_o_w).astype(B16)
    cross_dq, cross_dkv = attend_backward(
        False, cross_masks, cross_q, cross_kv, cross_kv, apart, half, cross_mixed, cross_lse, cross_do
    )
    grad_memory = place.both_cores(product_nt(cross_dkv, cross_w[:, half:]))
    dec_dn2 = place.both_parts(product_nt(cross_dq, cross_w[:, :half]))

    cross_grad, cross_o_grad = moves.early_both(
        [(dec_n2, cross_dq), (memory, cross_dkv)], 3, cross_mixed, cross_branch
    )

    source_cot_f = source_cot.astype(F32) + grad_memory
    enc_ff_branch = source_cot_f.astype(B16)
    enc_du = (product_nt(enc_ff_branch, enc_out_w) * enc_slope.astype(F32)).astype(B16)
    enc_dn2 = place.both_parts(product_nt(enc_du, enc_in_w))

    grad_h1, self_branch, self_rows = norm_backward(dec_h1, gain_f[3], dec_dn2, grad_h2)
    dec_do = product_nt(self_branch, dec_o_w).astype(B16)
    (dec_dqkv,) = attend_backward(
        True, dec_masks, dec_qkv, dec_qkv, dec_qkv, packed, half, dec_mixed, dec_lse, dec_do
    )
    dec_dn1 = place.both_parts(product_nt(dec_dqkv, dec_qkv_w))
    target_high, target_rows, target_lang = norm_backward(dec_h0, gain_f[2], dec_dn1, grad_h1, tgt_hot)

    grad_e1, enc_branch, enc_rows = norm_backward(enc_h1, gain_f[1], enc_dn2, source_cot_f)
    enc_do = product_nt(enc_branch, enc_o_w).astype(B16)
    (enc_dqkv,) = attend_backward(
        False, enc_masks, enc_qkv, enc_qkv, enc_qkv, packed, half, enc_mixed, enc_lse, enc_do
    )
    enc_dn1 = place.both_parts(product_nt(enc_dqkv, enc_qkv_w))
    source_high, source_rows, source_lang = norm_backward(enc_h0, gain_f[0], enc_dn1, grad_e1, src_hot)

    ff_sums = jnp.stack([column_sum(enc_ff_branch), column_sum(target_cot)])
    wide = [rows[:3] for rows in (source_rows, enc_rows, target_rows, self_rows, cross_rows)]
    wide = own_columns(jnp.concatenate([source_lang + target_lang] + wide + [ff_sums], axis=0), core)
    enc_sum, dec_sum = column_sum(enc_dqkv)[None], column_sum(dec_dqkv)[None]
    narrow = [enc_sum[:, :half], enc_sum[:, 2 * half :], dec_sum[:, :half], dec_sum[:, 2 * half :]]
    narrow += [column_sum(cross_dq)[None], column_sum(cross_dkv)[None, half:]]
    small_table = jnp.concatenate([wide] + narrow, axis=0)
    at = src_hot.shape[1]
    gain_places = [at, at + 3, at + 6, at + 9, at + 12]
    bias_places = [at + k for k in (1, 17, 18, 5, 4, 15, 7, 19, 20, 11, 10, 21, 22, 14, 13, 16)]

    grads, small, ffb_grad, outputs = moves.sums(
        {
            1: (dec_n1, dec_dqkv, 3),
            2: (enc_n2, enc_du, 1),
            4: (enc_n1, enc_dqkv, 3),
        },
        {
            0: (dec_mixed, self_branch),
            3: (enc_acted, enc_ff_branch),
            5: (enc_mixed, enc_branch),
        },
        small_table,
        jnp.stack([column_sum(enc_du), column_sum(dec_du)]),
        [memory, decoded.astype(B16), source_high, target_high],
    )
    picked = lambda places: jnp.concatenate([small[k : k + 1] for k in places], axis=0)
    return (
        outputs[0],
        outputs[1],
        outputs[2].astype(F32),
        outputs[3].astype(F32),
        small[:langs],
        picked(gain_places),
        picked(bias_places),
        ffb_grad,
        grads[4],
        grads[5],
        grads[2][0],
        grads[3],
        jnp.concatenate([grads[1], cross_grad], axis=0),
        jnp.stack([grads[0], cross_o_grad]),
        dec_in_grad[0],
        dec_out_grad,
    )


def solution(mesh):
    dp, seq = mesh.shape["dp"] // 2, mesh.shape["seq"]
    pairs = Mesh(mesh.devices.reshape(dp, 2, seq), ("dp", "core", "seq"))
    both, every = ("dp", "core"), ("dp", "core", "seq")
    rows = P(both, "seq", None)
    columns = P(None, every)
    middle = P(None, every, None)
    first = P(every, None)
    weights = (columns, columns, columns, columns, middle, first, first, first, middle, middle, first, first)
    return jax.shard_map(
        functools.partial(on_device, dp, seq),
        mesh=pairs,
        in_specs=(rows, rows, P(both, None), P(both, None), P(both), P(both, None), P(both, None))
        + weights
        + (rows, rows),
        out_specs=(rows, rows, rows, rows) + weights,
        check_vma=False,
    )
```

```python
import functools

import jax
import jax.numpy as jnp
from jax import lax
from jax.experimental import pallas as pl
from jax.experimental.pallas import tpu as pltpu
from jax.sharding import Mesh
from jax.sharding import PartitionSpec as P

HEAD_DIM = 64
EPSILON = 1e-05
MASKED = -1000000000.0
BLOCK = 256
ROWS = 32
HEADS = 4
GROUP = HEADS * HEAD_DIM
B16 = jnp.bfloat16
F32 = jnp.float32


def product(left, right):
    return jnp.dot(left, right, preferred_element_type=F32)


def product_tn(left, right):
    return lax.dot_general(left, right, (((0,), (0,)), ((), ())), preferred_element_type=F32)


def product_nt(left, right):
    return lax.dot_general(left, right, (((1,), (1,)), ((), ())), preferred_element_type=F32)


def column_sum(values):
    return jnp.sum(values.astype(F32), axis=0)


def norm_parts(hidden):
    centred = hidden - jnp.mean(hidden, axis=-1, keepdims=True)
    spread = jnp.mean(centred * centred, axis=-1, keepdims=True)
    scale = lax.rsqrt(spread + EPSILON)
    return centred * scale, scale


def layer_norm(hidden, gain_row, shift_row):
    return lax.optimization_barrier((norm_parts(hidden)[0] * gain_row + shift_row).astype(B16))


def norm_backward_kernel(last, h_ref, mine_ref, other_ref, grad_ref, gain_ref, *rest):
    if last:
        hot_ref, low_ref, sums_ref, lang_ref = rest
    else:
        full_ref, low_ref, sums_ref = rest
    unit, scale = norm_parts(h_ref[...])
    down = mine_ref[...].astype(F32) + other_ref[...].astype(F32)
    weighted = down * gain_ref[...]
    step = scale * (
        weighted
        - jnp.mean(weighted, axis=-1, keepdims=True)
        - unit * jnp.mean(weighted * unit, axis=-1, keepdims=True)
    )
    full = grad_ref[...].astype(F32) + step
    low = full.astype(B16)
    low_ref[...] = low

    @pl.when(pl.program_id(0) == 0)
    def _():
        sums_ref[...] = jnp.zeros_like(sums_ref)
        if last:
            lang_ref[...] = jnp.zeros_like(lang_ref)

    for k, value in enumerate((down * unit, down, low.astype(F32))):
        sums_ref[k : k + 1, :] += jnp.sum(value, axis=0, keepdims=True)
    if last:
        hot = hot_ref[...]
        rest_low = (full - low.astype(F32)).astype(B16)
        lang_ref[...] += product_tn(hot, low) + product_tn(hot, rest_low)
    else:
        full_ref[...] = full


def norm_backward(hidden, gain_row, parts, grad, hot=None):
    count, width = hidden.shape
    last = hot is not None
    block = pl.BlockSpec((BLOCK, width), lambda i: (i, 0))
    still = lambda rows: pl.BlockSpec((rows, width), lambda i: (0, 0))
    inputs = [hidden, parts[0], parts[1], grad, gain_row] + ([hot] if last else [])
    outs = [(count, B16, block), (8, F32, still(8))]
    outs = outs + [(hot.shape[1], F32, still(hot.shape[1]))] if last else [(count, F32, block)] + outs
    return pl.pallas_call(
        functools.partial(norm_backward_kernel, last),
        grid=(count // BLOCK,),
        in_specs=[block] * 4
        + [still(1)]
        + ([pl.BlockSpec((BLOCK, hot.shape[1]), lambda i: (i, 0))] if last else []),
        out_specs=[spec for _, _, spec in outs],
        out_shape=[jax.ShapeDtypeStruct((rows, width), kind) for rows, kind, _ in outs],
        compiler_params=pltpu.CompilerParams(vmem_limit_bytes=20 * 2**20),
        cost_estimate=pl.CostEstimate(flops=30 * count * width, bytes_accessed=18 * count * width, transcendentals=0),
        name="norm_last" if last else "norm_grad",
    )(*inputs)


def gelu_both(values):
    below = 0.5 * (1.0 + lax.erf(values * (0.5**0.5)))
    density = jnp.exp(-0.5 * values * values) * (0.5 / jnp.pi) ** 0.5
    return (values * below).astype(B16), (below + values * density).astype(B16)


def ffn_backward_kernel(
    grad_ref, normed_ref, acted_ref, slope_ref, in_ref, out_ref, down_ref, in_grad_ref, out_grad_ref, sums_ref, acc_ref, up_ref
):
    step = pl.program_id(0)

    @pl.when(step == 0)
    def _():
        up_ref[...] = normed_ref[...].T
        acc_ref[...] = jnp.zeros_like(acc_ref)

    grad = grad_ref[...]
    inner = product_nt(grad, out_ref[...]) * slope_ref[...].astype(F32)
    low = inner.astype(B16)
    sums_ref[...] = jnp.sum(low.astype(F32), axis=0, keepdims=True)
    out_grad_ref[...] = product_tn(acted_ref[...], grad).astype(B16)
    in_grad_ref[...] = product(up_ref[...], low).astype(B16)
    acc_ref[...] += product_nt(low, in_ref[...])

    @pl.when(step == pl.num_programs(0) - 1)
    def _():
        down_ref[...] = acc_ref[...].astype(B16)


def ffn_backward(grad, normed, acted, slope, w_in, w_out):
    count, width = grad.shape
    hidden = acted.shape[1]
    cut = 256
    still = pl.BlockSpec((count, width), lambda i: (0, 0))
    tall = pl.BlockSpec((count, cut), lambda i: (0, i))
    side = pl.BlockSpec((width, cut), lambda i: (0, i))
    flat = pl.BlockSpec((cut, width), lambda i: (i, 0))
    return pl.pallas_call(
        ffn_backward_kernel,
        grid=(hidden // cut,),
        in_specs=[still, still, tall, tall, side, flat],
        out_specs=[still, side, flat, pl.BlockSpec((1, cut), lambda i: (0, i))],
        out_shape=[
            jax.ShapeDtypeStruct((count, width), B16),
            jax.ShapeDtypeStruct((width, hidden), B16),
            jax.ShapeDtypeStruct((hidden, width), B16),
            jax.ShapeDtypeStruct((1, hidden), F32),
        ],
        scratch_shapes=[pltpu.VMEM((count, width), F32), pltpu.VMEM((width, count), B16)],
        compiler_params=pltpu.CompilerParams(vmem_limit_bytes=40 * 2**20),
        cost_estimate=pl.CostEstimate(
            flops=8 * count * width * hidden, bytes_accessed=8 * width * hidden + 4 * count * hidden, transcendentals=0
        ),
        name="ffn_grad",
    )(grad, normed, acted, slope, w_in, w_out)


def allowed_rows(causal, kseg_ref, qseg, length, key_at, query_at):
    allowed = kseg_ref[key_at : key_at + ROWS, :] == qseg
    if causal:
        keys = key_at + lax.broadcasted_iota(jnp.int32, (ROWS, BLOCK), 0)
        queries = query_at + lax.broadcasted_iota(jnp.int32, (ROWS, BLOCK), 1)
        allowed = allowed & (keys <= queries) & ((keys < length) | (keys == queries))
    return allowed


def dot_nt(left, right):
    return lax.dot_general(left, right, (((1,), (1,)), ((), ())), preferred_element_type=F32)


def head_masked(value, axis=1):
    lane = lax.broadcasted_iota(jnp.int32, value.shape, axis) // HEAD_DIM
    zero = jnp.zeros_like(value)
    return [jnp.where(lane == h, value, zero) for h in range(HEADS)]


def dot_nn(left, right):
    return jnp.dot(left, right, preferred_element_type=F32)


def fold_rows(value, combine):
    return combine(value.reshape(value.shape[0] // 8, 8, value.shape[1]), axis=0)


def forward_kernel(
    causal,
    info_ref,
    q_ref,
    k_ref,
    v_ref,
    qseg_ref,
    kseg_ref,
    o_ref,
    lse_ref,
    vt_ref,
    s_ref,
    acc_ref,
    top_ref,
    sum_ref,
    qt_ref,
    e_ref,
):
    block = pl.program_id(1)
    blocks = k_ref.shape[0] // BLOCK
    length = info_ref[blocks * blocks]

    @pl.when(block == 0)
    def _():
        vt_ref[...] = v_ref[...].T

    qseg = qseg_ref[...]
    for h, head in enumerate(head_masked((q_ref[...] * jnp.asarray(HEAD_DIM**-0.5, B16)).T, 0)):
        qt_ref[h] = head
    top_ref[...] = jnp.full(top_ref.shape, -1e30, F32)
    sum_ref[...] = jnp.zeros_like(sum_ref)
    acc_ref[...] = jnp.zeros_like(acc_ref)
    for j in range(blocks):

        @pl.when(info_ref[block * blocks + j] > 0)
        def _(j=j):
            keys = k_ref[j * BLOCK : (j + 1) * BLOCK, :]
            for h in range(HEADS):
                s_ref[h, j * BLOCK : (j + 1) * BLOCK, :] = dot_nn(keys, qt_ref[h])
            top = [top_ref[h] for h in range(HEADS)]
            for at in range(j * BLOCK, (j + 1) * BLOCK, ROWS):
                allowed = allowed_rows(causal, kseg_ref, qseg, length, at, block * BLOCK)
                for h in range(HEADS):
                    scores = jnp.where(allowed, s_ref[h, at : at + ROWS, :], MASKED)
                    s_ref[h, at : at + ROWS, :] = scores
                    top[h] = jnp.maximum(top[h], fold_rows(scores, jnp.max))
            for h in range(HEADS):
                top_ref[h] = top[h]

    highest = [jnp.max(top_ref[h], axis=0, keepdims=True) for h in range(HEADS)]
    for j in range(blocks):

        @pl.when(info_ref[block * blocks + j] > 0)
        def _(j=j):
            for h in range(HEADS):
                total = sum_ref[h]
                for at in range(0, BLOCK, ROWS):
                    weights = jnp.exp(s_ref[h, j * BLOCK + at : j * BLOCK + at + ROWS, :] - highest[h])
                    total = total + fold_rows(weights, jnp.sum)
                    e_ref[h, at : at + ROWS, :] = weights.astype(B16)
                sum_ref[h] = total
                rows = slice(h * HEAD_DIM, (h + 1) * HEAD_DIM)
                acc_ref[rows, :] += dot_nn(vt_ref[rows, j * BLOCK : (j + 1) * BLOCK], e_ref[h])

    lse_ref[...] = jnp.zeros_like(lse_ref)
    for h in range(HEADS):
        total = jnp.sum(sum_ref[h], axis=0, keepdims=True)
        rows = slice(h * HEAD_DIM, (h + 1) * HEAD_DIM)
        acc_ref[rows, :] = acc_ref[rows, :] / total
        lse_ref[0, h : h + 1, :] = highest[h] + jnp.log(total)
    o_ref[...] = acc_ref[...].T.astype(B16)


def backward_kernel(
    causal,
    info_ref,
    q_ref,
    k_ref,
    v_ref,
    o_ref,
    do_ref,
    lse_ref,
    qseg_ref,
    kseg_ref,
    *rest,
):
    *outs, kt_ref, dqt_ref, sums_ref, done_ref, qt_ref, dot_ref, s_ref, dp_ref, p_ref, ds_ref, sems = rest
    group, block = pl.program_id(0), pl.program_id(1)
    groups = pl.num_programs(0)
    blocks = k_ref.shape[0] // BLOCK
    length = info_ref[blocks * blocks]

    @pl.when(block == 0)
    def _():
        kt_ref[...] = k_ref[...].T
        sums_ref[...] = jnp.zeros_like(sums_ref)

    qseg = qseg_ref[...]
    grads = do_ref[...]
    scaled = q_ref[...] * jnp.asarray(HEAD_DIM**-0.5, B16)
    grads_up = grads.T
    for h, head in enumerate(head_masked(scaled.T, 0)):
        qt_ref[h] = head
    for h, head in enumerate(head_masked(grads_up, 0)):
        dot_ref[h] = head
    queries_down = jnp.concatenate(head_masked(scaled), axis=0)
    grads_down = jnp.concatenate(head_masked(grads), axis=0)
    mixed = grads_up.astype(F32) * o_ref[...].T.astype(F32)
    inner = [
        jnp.sum(fold_rows(mixed[h * HEAD_DIM : (h + 1) * HEAD_DIM], jnp.sum), axis=0, keepdims=True)
        for h in range(HEADS)
    ]
    dqt_ref[...] = jnp.zeros_like(dqt_ref)
    for j in range(blocks):

        @pl.when(info_ref[block * blocks + j] > 0)
        def _(j=j):
            rows = slice(j * BLOCK, (j + 1) * BLOCK)
            keys = k_ref[rows, :]
            values = v_ref[rows, :]
            for h in range(HEADS):
                s_ref[h] = dot_nn(keys, qt_ref[h])
                dp_ref[h] = dot_nn(values, dot_ref[h])
            for at in range(0, BLOCK, ROWS):
                here = slice(at, at + ROWS)
                allowed = allowed_rows(causal, kseg_ref, qseg, length, j * BLOCK + at, block * BLOCK)
                for h in range(HEADS):
                    lanes = slice(h * BLOCK, (h + 1) * BLOCK)
                    chances = jnp.where(allowed, jnp.exp(s_ref[h, here, :] - lse_ref[0, h : h + 1, :]), 0.0)
                    p_ref[here, lanes] = chances.astype(B16)
                    ds_ref[here, lanes] = (chances * (dp_ref[h, here, :] - inner[h])).astype(B16)
            for h in range(HEADS):
                part = slice(h * HEAD_DIM, (h + 1) * HEAD_DIM)
                dqt_ref[part, :] += dot_nn(kt_ref[part, rows], ds_ref[:, h * BLOCK : (h + 1) * BLOCK])
            sums_ref[0, rows, :] += dot_nn(ds_ref[...], queries_down)
            sums_ref[1, rows, :] += dot_nn(p_ref[...], grads_down)

    here = pl.ds(pl.multiple_of(block * BLOCK, BLOCK), BLOCK)
    done_ref[0, here, :] = (dqt_ref[...].T * HEAD_DIM**-0.5).astype(B16)

    @pl.when(block == blocks - 1)
    def _():
        done_ref[1] = sums_ref[0].astype(B16)
        done_ref[2] = sums_ref[1].astype(B16)
        width = k_ref.shape[1]
        copies = []
        for k in range(3):
            out, place = (outs[0], k) if len(outs) == 1 else (outs[min(k, 1)], max(k - 1, 0))
            lanes = pl.ds(pl.multiple_of((place * groups + group) * width, width), width)
            copies.append(pltpu.make_async_copy(done_ref.at[k], out.at[:, lanes], sems.at[k]))
        for copy in copies:
            copy.start()
        for copy in copies:
            copy.wait()


def block_info(causal, query_seg, key_seg, length):
    blocks = query_seg.shape[0] // BLOCK
    query_low, query_high = query_seg[::BLOCK], query_seg[BLOCK - 1 :: BLOCK]
    key_low, key_high = key_seg[::BLOCK], key_seg[BLOCK - 1 :: BLOCK]
    meets = (key_low[None, :] <= query_high[:, None]) & (key_high[None, :] >= query_low[:, None])
    if causal:
        at = jnp.arange(blocks)
        meets = meets & (at[None, :] <= at[:, None])
    return jnp.concatenate([meets.astype(jnp.int32).reshape(-1), length[None]])


def attention_specs(count, offsets):
    query = pl.BlockSpec((BLOCK, GROUP), lambda p, i, info: (i, p + offsets[0]))
    key = pl.BlockSpec((count, GROUP), lambda p, i, info: (0, p + offsets[1]))
    value = pl.BlockSpec((count, GROUP), lambda p, i, info: (0, p + offsets[2]))
    plain = pl.BlockSpec((BLOCK, GROUP), lambda p, i, info: (i, p))
    whole = pl.BlockSpec((count, GROUP), lambda p, i, info: (0, p))
    stats = pl.BlockSpec((1, 8, BLOCK), lambda p, i, info: (p, 0, i))
    qseg = pl.BlockSpec((1, BLOCK), lambda p, i, info: (0, i))
    kseg = pl.BlockSpec((count, 1), lambda p, i, info: (0, 0))
    return query, key, value, plain, whole, stats, qseg, kseg


def attend_forward(causal, masks, queries, keys, values, offsets, width):
    info, qseg_row, kseg_column = masks
    count = queries.shape[0]
    groups = width // GROUP
    query, key, value, plain, _, stats, qseg, kseg = attention_specs(count, offsets)
    return pl.pallas_call(
        functools.partial(forward_kernel, causal),
        grid_spec=pltpu.PrefetchScalarGridSpec(
            num_scalar_prefetch=1,
            grid=(groups, count // BLOCK),
            in_specs=[query, key, value, qseg, kseg],
            out_specs=[plain, stats],
            scratch_shapes=[pltpu.VMEM((GROUP, count), B16), pltpu.VMEM((HEADS, count, BLOCK), F32), pltpu.VMEM((GROUP, BLOCK), F32)]
            + [pltpu.VMEM((HEADS, 8, BLOCK), F32)] * 2
            + [pltpu.VMEM((HEADS, GROUP, BLOCK), B16), pltpu.VMEM((HEADS, BLOCK, BLOCK), B16)],
        ),
        out_shape=[
            jax.ShapeDtypeStruct((count, width), B16),
            jax.ShapeDtypeStruct((groups, 8, count), F32),
        ],
        compiler_params=pltpu.CompilerParams(vmem_limit_bytes=20 * 2**20),
        cost_estimate=pl.CostEstimate(
            flops=2 * 2 * count * count * width * 2, bytes_accessed=count * width * 8, transcendentals=0
        ),
        name="attend_causal" if causal else "attend",
    )(info, queries, keys, values, qseg_row, kseg_column)


def attend_backward(causal, masks, queries, keys, values, offsets, width, mixed, lse, grad):
    widths = (3 * width,) if queries is keys else (width, 2 * width)
    info, qseg_row, kseg_column = masks
    count = queries.shape[0]
    groups = width // GROUP
    query, key, value, plain, _, stats, qseg, kseg = attention_specs(count, offsets)
    return pl.pallas_call(
        functools.partial(backward_kernel, causal),
        grid_spec=pltpu.PrefetchScalarGridSpec(
            num_scalar_prefetch=1,
            grid=(groups, count // BLOCK),
            in_specs=[query, key, value, plain, plain, stats, qseg, kseg],
            out_specs=[pl.BlockSpec(memory_space=pl.ANY)] * len(widths),
            scratch_shapes=[
                pltpu.VMEM((GROUP, count), B16),
                pltpu.VMEM((GROUP, BLOCK), F32),
                pltpu.VMEM((2, count, GROUP), F32),
                pltpu.VMEM((3, count, GROUP), B16),
                pltpu.VMEM((HEADS, GROUP, BLOCK), B16),
                pltpu.VMEM((HEADS, GROUP, BLOCK), B16),
                pltpu.VMEM((HEADS, BLOCK, BLOCK), F32),
                pltpu.VMEM((HEADS, BLOCK, BLOCK), F32),
                pltpu.VMEM((BLOCK, HEADS * BLOCK), B16),
                pltpu.VMEM((BLOCK, HEADS * BLOCK), B16),
                pltpu.SemaphoreType.DMA((3,)),
            ],
        ),
        out_shape=[jax.ShapeDtypeStruct((count, w), B16) for w in widths],
        compiler_params=pltpu.CompilerParams(vmem_limit_bytes=20 * 2**20),
        cost_estimate=pl.CostEstimate(
            flops=5 * 2 * count * count * width * 2, bytes_accessed=count * width * 16, transcendentals=0
        ),
        name="attend_grad_causal" if causal else "attend_grad",
    )(info, queries, keys, values, mixed, grad, lse, qseg_row, kseg_column)


MESH = pl.DeviceIdType.MESH
GATHER_LAGS = (0, 1, 2, 3)
ROW_LAG = 4
SUM_CUT = 20
SUM_ROWS = [1, 3, 5, 7]


def own_columns(array, core):
    w = array.shape[-1] // 8
    runs = [array[..., k * w : (k + 1) * w] for k in range(8)]
    return jnp.concatenate([jnp.where(core == 0, runs[k], runs[k + 1]) for k in range(0, 8, 2)], axis=-1)


def lay_side(array):
    return jnp.concatenate([array[i] for i in range(array.shape[0])], axis=1)


def lay_wide(arrays):
    return arrays[0] if len(arrays) == 1 else jnp.concatenate(arrays, axis=1)


def xor_arrange(pieces, place):
    pieces, bit = list(pieces), 0
    while 1 << bit < len(pieces):
        odd = ((place >> bit) & 1) == 1
        pieces = [jnp.where(odd, pieces[k ^ (1 << bit)], pieces[k]) for k in range(len(pieces))]
        bit += 1
    return pieces


class Here:
    def __init__(self):
        self.at = lax.axis_index("dp")
        self.c = lax.axis_index("core")
        self.z = lax.axis_index("seq")
        self.x = self.at % 2
        self.y = self.at // 2
        self.core_peer = (self.at, 1 - self.c, self.z)
        self.x_peer = (self.at + 1 - 2 * self.x, self.c, self.z)
        self.y_peer = (self.at + 2 - 4 * self.y, self.c, self.z)
        self.edge = (self.z % 3) == 0
        self.inner = jnp.logical_not(self.edge)

    def z_flip(self, j):
        return (self.z // 2 + j // 2) % 2 * 2 + (self.z % 2 + j % 2) % 2

    def z_peer(self, j):
        return (self.at, self.c, self.z_flip(j))

    def enter(self):
        barrier = pltpu.get_barrier_semaphore()
        peers = [self.x_peer, self.y_peer, self.core_peer]
        for j in range(1, 4):
            peers += [(self.at, self.c, self.z_flip(j)), (self.at, 1 - self.c, self.z_flip(j))]
        for peer in peers:
            pl.semaphore_signal(barrier, inc=1, device_id=peer, device_id_type=MESH)
        pl.semaphore_wait(barrier, len(peers))


def remote(source, target, send_sem, recv_sem, peer):
    return pltpu.make_async_remote_copy(
        src_ref=source,
        dst_ref=target,
        send_sem=send_sem,
        recv_sem=recv_sem,
        device_id=peer,
        device_id_type=MESH,
    )


class GatherItem:
    def __init__(self, here, source, first, kind, out, start, size, send, recv, local):
        self.here, self.source, self.first, self.kind, self.out = here, source, first, kind, out
        self.send, self.recv, self.local = send, recv, local
        self.start, self.size = start, size
        self.all = pl.ds(start, size)
        self.sides = [pl.ds(start, size // 2), pl.ds(start + size // 2, size // 2)]
        if kind == "small":
            self.sides = [self.all]
        self.core = 0 if kind == "rows" else here.c
        self.copies = {}

    def move(self, slot, region, peer, arrive=None):
        recv = self.recv.at[slot if arrive is None else arrive]
        self.copies[slot] = remote(region, region, self.send.at[slot], recv, peer)
        return self.copies[slot]

    def runs(self, core):
        w = self.source.shape[-1] // 8
        for q in range(self.start // w, (self.start + self.size) // w):
            lanes = pl.ds(pl.multiple_of((q % 4 * 2 + core) * w, 128), w)
            yield self.source.at[self.first + q // 4, :, lanes], pl.ds(q * w, w)

    def begin(self):
        here = self.here
        place = self.out.at[here.y, here.x, self.core, here.z]
        block = self.out.at[here.y, here.x, self.core, here.z, :, self.all]
        self.own = pltpu.make_async_copy(block, block, self.local)
        if self.kind == "columns":
            for source, lanes in self.runs(here.c):
                pltpu.make_async_copy(source, place.at[:, lanes], self.local).start()
            for source, lanes in self.runs(1 - here.c):
                remote(source, place.at[:, lanes], self.send.at[0], self.recv.at[0], here.core_peer).start()
        else:
            source = self.source.at[self.first, :, self.all]
            pltpu.make_async_copy(source, block, self.local).start()
            if self.kind == "small":
                remote(source, block, self.send.at[0], self.recv.at[0], here.core_peer).start()
        if self.kind != "rows":
            self.copies[0] = remote(block, block, self.send.at[0], self.recv.at[0], here.core_peer)

    def stage_z(self):
        here = self.here
        self.own.wait()
        if self.kind != "rows":
            self.copies[0].wait_recv()
        block = self.out.at[here.y, here.x, :, here.z, :, self.all]
        self.move(1, block, here.z_peer(1)).start()
        self.move(2, block, here.z_peer(2)).start()
        pl.when(here.inner)(self.move(3, block, here.z_peer(3)).start)

    def stage_pass(self):
        here = self.here
        self.copies[2].wait_recv()
        block = self.out.at[here.y, here.x, :, here.z_flip(2), :, self.all]
        pl.when(here.inner)(self.move(8, block, here.z_peer(1), arrive=3).start)

    def stage_one(self):
        here = self.here
        self.copies[1].wait_recv()
        self.copies[3].wait_recv()
        for k, peer in list(enumerate((here.x_peer, here.y_peer)))[: len(self.sides)]:
            self.move(4 + k, self.out.at[here.y, here.x, :, :, :, self.sides[k]], peer).start()

    def stage_two(self):
        here = self.here
        self.copies[4].wait_recv()
        self.move(6, self.out.at[here.y, :, :, :, :, self.sides[0]], here.y_peer).start()
        if len(self.sides) == 2:
            self.copies[5].wait_recv()
            self.move(7, self.out.at[:, here.x, :, :, :, self.sides[1]], here.x_peer).start()

    def finish(self):
        for k in range(len(self.sides)):
            self.copies[6 + k].wait_recv()
        for slot, copy in self.copies.items():
            if slot in (3, 8):
                pl.when(self.here.inner)(copy.wait_send)
            else:
                copy.wait_send()


class RowIn:
    def __init__(self, here, source, out, send, recv, local):
        self.here, self.source, self.out = here, source, out
        self.send, self.recv, self.local = send, recv, local
        self.half = source.shape[-1] // 2

    def lanes(self, f):
        return pl.ds(f * self.half, self.half) if isinstance(f, int) else pl.ds(pl.multiple_of(f * self.half, 128), self.half)

    def parts(self):
        here = self.here
        for i in range(2):
            for f in range(2):
                source = self.source.at[i, :, self.lanes(f)]
                target = self.out.at[here.z, :, self.lanes(f)]
                self_sent = (2 * here.c + i == here.z) & (here.c == f)
                peer = (here.at, f, 2 * here.c + i)
                away = remote(source, target, self.send.at[2 * i + f], self.recv.at[here.z], peer)
                stay = pltpu.make_async_copy(source, target, self.local)
                yield self_sent, away, stay

    def begin(self):
        for self_sent, away, stay in self.parts():
            pl.when(self_sent)(stay.start)
            pl.when(jnp.logical_not(self_sent))(away.start)

    def across(self):
        here = self.here
        lanes = self.lanes(here.c)
        for k in range(4):
            target = self.out.at[k, :, lanes]
            from_self = (here.z == k) & (here.z // 2 == here.c)
            stay = pltpu.make_async_copy(target, target, self.local)
            away = remote(target, target, self.send.at[0], self.recv.at[k], here.core_peer)
            pl.when(from_self)(stay.wait)
            pl.when(jnp.logical_not(from_self))(away.wait_recv)
        region = self.out.at[:, :, lanes]
        self.copy = remote(region, region, self.send.at[4], self.recv.at[4], here.core_peer)
        self.copy.start()

    def finish(self):
        self.copy.wait()
        for self_sent, away, _ in self.parts():
            pl.when(jnp.logical_not(self_sent))(away.wait_send)


def gather_kernel(kinds, cuts, rows_at, refs):
    here = Here()
    refs = list(refs)
    take = lambda n: [refs.pop(0) for _ in range(n)]
    count = len(kinds)
    ins = take(count)
    row_ins = take(len(rows_at))
    outs = take(count)
    row_outs = take(len(rows_at))
    send, recv, local, row_send, row_recv, row_local = refs
    items = []
    for k, (first, kind) in enumerate(kinds):
        size = outs[k].shape[-1] // cuts[k]
        for cut in range(cuts[k]):
            n = len(items)
            sems = send.at[n], recv.at[n], local.at[n]
            items.append(GatherItem(here, ins[k], first, kind, outs[k], cut * size, size, *sems))
    count = len(items)
    rows = [
        RowIn(here, row_ins[t], row_outs[t], row_send.at[t], row_recv.at[t], row_local.at[t])
        for t in range(len(rows_at))
    ]
    here.enter()
    for item in items:
        item.begin()
    steps = (GatherItem.stage_z, GatherItem.stage_pass, GatherItem.stage_one, GatherItem.stage_two)
    for step in range(count + GATHER_LAGS[-1] + 1):
        for t, start in enumerate(rows_at):
            if start == step:
                rows[t].begin()
            if min(start + ROW_LAG, count + GATHER_LAGS[-1]) == step:
                rows[t].across()
        for stage, lag in zip(steps, GATHER_LAGS):
            if 0 <= step - lag < count:
                stage(items[step - lag])
    for item in items:
        item.finish()
    for row in rows:
        row.finish()


def gather_all(sources, rows, rows_at):
    kinds = [(first, kind) for _, first, _, kind in sources]
    inputs = [source[0] for source in sources] + list(rows)
    shapes, cuts = [], []
    for array, _, number, kind in sources:
        _, r, n = array.shape
        n = number * n // 2 if kind == "columns" else n
        shapes.append(jax.ShapeDtypeStruct((2, 2, 1 if kind == "rows" else 2, 4, r, n), array.dtype))
        cuts.append(2 if r * n * (2 if kind == "columns" else 1) > 2**16 else 1)
    shapes += [jax.ShapeDtypeStruct((4,) + row.shape[1:], row.dtype) for row in rows]
    count, tensors = sum(cuts), len(rows)
    hbm = pl.BlockSpec(memory_space=pl.ANY)

    def kernel(*refs):
        gather_kernel(kinds, cuts, rows_at, refs)

    dma = pltpu.SemaphoreType.DMA
    return pl.pallas_call(
        kernel,
        in_specs=[hbm] * len(inputs),
        out_specs=[hbm] * len(shapes),
        out_shape=shapes,
        scratch_shapes=[
            dma((count, 9)),
            dma((count, 9)),
            dma((count,)),
            dma((tensors, 5)),
            dma((tensors, 5)),
            dma((tensors,)),
        ],
        compiler_params=pltpu.CompilerParams(collective_id=0, has_side_effects=True),
        name="gather_all",
    )(*inputs)


class SumItem:
    def __init__(self, here, source, out, start, scratch, send, recv, local):
        self.here, self.source, self.out = here, source, out
        self.own, self.b1, self.b2, self.b3, self.met = scratch[:5]
        self.columns = source.shape[2] == 2
        if self.columns:
            self.b4, self.b4s = scratch[5:]
        self.send, self.recv, self.local = send, recv, local
        size = self.own.shape[-1]
        self.half = size // 2
        self.sides = pl.ds(0, self.half), pl.ds(self.half, self.half)
        self.cut = slice(start, start + size)
        self.source_sides = pl.ds(start, self.half), pl.ds(start + self.half, self.half)
        self.copies = {}

    def make(self, slot, source, target, peer):
        self.copies[slot] = remote(source, target, self.send.at[slot], self.recv.at[slot], peer)
        return self.copies[slot]

    def go(self, slot, source, target, peer):
        self.make(slot, source, target, peer).start()

    def blocks(self, body):
        cores = self.b2.shape[0]

        def step(k, carry):
            body(k // 4, k % 4)
            return carry

        lax.fori_loop(0, cores * 4, step, 0)

    def stage_one(self):
        here, (a, b), source = self.here, self.sides, self.source
        first, second = self.source_sides
        self.go(0, source.at[:, 1 - here.x, :, :, :, first], self.b1.at[:, :, :, :, a], here.x_peer)
        self.go(1, source.at[1 - here.y, :, :, :, :, second], self.b1.at[:, :, :, :, b], here.y_peer)
        self.loads = [
            pltpu.make_async_copy(source.at[:, here.x, :, :, :, first], self.own.at[:, :, :, :, a], self.local.at[0]),
            pltpu.make_async_copy(source.at[here.y, :, :, :, :, second], self.own.at[:, :, :, :, b], self.local.at[1]),
        ]
        for load in self.loads:
            load.start()

        @pl.when(here.edge)
        def _():
            self.b3[2] = jnp.zeros(self.b3.shape[1:], self.b3.dtype)

    def stage_two(self):
        here = self.here
        for side, near, peer in ((0, here.y, here.y_peer), (1, here.x, here.x_peer)):
            lanes = self.sides[side]
            away = 1 - near
            self.loads[side].wait()
            self.copies[side].wait_recv()

            def add(c, z, away=away, lanes=lanes):
                total = self.own[away, c, z, :, lanes].astype(F32) + self.b1[away, c, z, :, lanes].astype(F32)
                self.own[away, c, z, :, lanes] = total.astype(self.own.dtype)

            self.blocks(add)
            self.go(2 + side, self.own.at[away, :, :, :, lanes], self.b2.at[:, :, :, lanes], peer)

    def stage_three(self):
        here = self.here
        for side, near in ((0, here.y), (1, here.x)):
            lanes = self.sides[side]
            self.copies[2 + side].wait_recv()

            def add(c, z, near=near, lanes=lanes):
                total = self.own[near, c, z, :, lanes].astype(F32) + self.b1[near, c, z, :, lanes].astype(F32)
                total = total + self.b2[c, z, :, lanes].astype(F32)
                self.b2[c, z, :, lanes] = total.astype(self.b2.dtype)

            self.blocks(add)
        piece = lambda j: self.b2.at[:, here.z_flip(j)]
        self.go(4, piece(1), self.b3.at[0], here.z_peer(1))
        pl.when(here.edge)(self.make(5, piece(2), self.b3.at[1], here.z_peer(2)).start)
        pl.when(here.inner)(self.make(6, piece(3), self.b3.at[2], here.z_peer(3)).start)
        pl.when(here.edge)(self.make(8, piece(3), self.met, here.z_peer(1)).start)

    def stage_meet(self):
        here = self.here

        @pl.when(here.inner)
        def _():
            self.copies[8].wait_recv()
            for c in range(self.b2.shape[0]):
                place = here.z_flip(2)
                total = self.b2[c, place].astype(F32) + self.met[c].astype(F32)
                self.b2[c, place] = total.astype(self.b2.dtype)
            self.copies[5].start()

    def total(self, c):
        total = self.b2[c, self.here.z].astype(F32)
        for j in range(3):
            total = total + self.b3[j, c].astype(F32)
        return total

    def place(self, value, core):
        w = self.out.shape[-1] // 8
        for k in range(value.shape[1] // w):
            q = self.cut.start // w + k
            lanes = pl.ds(pl.multiple_of((q % 4 * 2 + core) * w, 128), w)
            self.out[q // 4, :, lanes] = value[:, k * w : (k + 1) * w]

    def stage_four(self):
        here = self.here
        self.copies[4].wait_recv()
        self.copies[5].wait_recv()
        pl.when(here.inner)(self.copies[6].wait_recv)
        if self.columns:
            self.b4s[...] = self.total(1 - here.c).astype(self.b4s.dtype)
            self.go(7, self.b4s, self.b4, here.core_peer)
            self.place(self.total(here.c), here.c)
        else:
            self.out[:, self.cut] = self.total(0)

    def finish(self):
        if self.columns:
            self.copies[7].wait_recv()
            self.place(self.b4[...].astype(F32), 1 - self.here.c)
        for slot, copy in self.copies.items():
            if slot == 6:
                pl.when(self.here.inner)(copy.wait_send)
            elif slot == 8:
                pl.when(self.here.edge)(copy.wait_send)
            else:
                copy.wait_send()


class RowOut:
    def __init__(self, here, source, out, send, recv, local):
        self.here, self.source, self.out = here, source, out
        self.send, self.recv, self.local = send, recv, local
        self.half = source.shape[-1] // 2

    def parts(self):
        here = self.here
        lanes = pl.ds(pl.multiple_of(here.c * self.half, 128), self.half)
        for k in range(4):
            source = self.source.at[k, :, lanes]
            target = self.out.at[here.z % 2, :, lanes]
            self_sent = (here.z == k) & (here.z // 2 == here.c)
            peer = (here.at, here.z // 2, k)
            away = remote(source, target, self.send.at[k], self.recv.at[here.z % 2 * 2 + here.c], peer)
            yield self_sent, away, pltpu.make_async_copy(source, target, self.local)

    def begin(self):
        for self_sent, away, stay in self.parts():
            pl.when(self_sent)(stay.start)
            pl.when(jnp.logical_not(self_sent))(away.start)

    def finish(self):
        here = self.here
        for i in range(2):
            for f in range(2):
                target = self.out.at[i, :, pl.ds(f * self.half, self.half)]
                from_self = (2 * here.c + i == here.z) & (here.c == f)
                away = remote(target, target, self.send.at[0], self.recv.at[2 * i + f], here.core_peer)
                stay = pltpu.make_async_copy(target, target, self.local)
                pl.when(from_self)(stay.wait)
                pl.when(jnp.logical_not(from_self))(away.wait_recv)
        for self_sent, away, _ in self.parts():
            pl.when(jnp.logical_not(self_sent))(away.wait_send)


def sum_kernel(column_flags, cuts, rows_at, refs):
    here = Here()
    refs = list(refs)
    take = lambda n: [refs.pop(0) for _ in range(n)]
    grads, tensors = len(column_flags), len(rows_at)
    sources, row_sources = take(grads), take(tensors)
    outs, row_outs = take(grads), take(tensors)
    scratch = [[take(7 if columns else 5) for _ in range(cut)] for columns, cut in zip(column_flags, cuts)]
    send, recv, local, row_send, row_recv, row_local = refs
    items = []
    for k in range(grads):
        for cut in range(cuts[k]):
            n, start = len(items), cut * (sources[k].shape[-1] // cuts[k])
            items.append(
                SumItem(here, sources[k], outs[k], start, scratch[k][cut], send.at[n], recv.at[n], local.at[n])
            )
    count = len(items)
    rows = [
        RowOut(here, row_sources[t], row_outs[t], row_send.at[t], row_recv.at[t], row_local.at[t])
        for t in range(tensors)
    ]
    here.enter()
    for step in range(count + 5):
        if step < count:
            items[step].stage_one()
        if 0 <= step - 1 < count:
            items[step - 1].stage_two()
        if 0 <= step - 2 < count:
            items[step - 2].stage_three()
        if 0 <= step - 3 < count:
            items[step - 3].stage_meet()
        if 0 <= step - 4 < count:
            items[step - 4].stage_four()
        if 0 <= step - 5 < count:
            items[step - 5].finish()
        for t, start in enumerate(rows_at):
            if start == step:
                rows[t].begin()
    for row in rows:
        row.finish()


def sum_all(grads, parts, rows, rows_at):
    flags = [grad.shape[2] == 2 for grad in grads]
    hbm = pl.BlockSpec(memory_space=pl.ANY)
    vmem = pl.BlockSpec(memory_space=pltpu.VMEM)
    shapes, scratch, cuts = [], [], []
    for grad, columns, number in zip(grads, flags, parts):
        _, _, cores, places, r, n = grad.shape
        shapes.append(jax.ShapeDtypeStruct((number, r, 2 * n // number) if columns else (r, n), F32))
        cuts.append(2 if grad.size > 2**SUM_CUT else 1)
        n = n // cuts[-1]
        sizes = [(2, cores, places, r, n)] * 2 + [(cores, places, r, n), (3, cores, r, n), (cores, r, n)]
        sizes += [(r, n)] * 2 if columns else []
        scratch += [pltpu.VMEM(size, grad.dtype) for size in sizes] * cuts[-1]
    count, tensors = sum(cuts), len(rows)
    row_shapes = [jax.ShapeDtypeStruct((2,) + row.shape[1:], row.dtype) for row in rows]

    def kernel(*refs):
        sum_kernel(flags, cuts, rows_at, refs)

    dma = pltpu.SemaphoreType.DMA
    return pl.pallas_call(
        kernel,
        in_specs=[hbm] * (len(grads) + tensors),
        out_specs=[vmem] * len(grads) + [hbm] * tensors,
        out_shape=shapes + row_shapes,
        scratch_shapes=scratch
        + [
            dma((count, 9)),
            dma((count, 9)),
            dma((count, 2)),
            dma((tensors, 4)),
            dma((tensors, 4)),
            dma((tensors,)),
        ],
        compiler_params=pltpu.CompilerParams(
            collective_id=1, has_side_effects=True, vmem_limit_bytes=60 * 2**20
        ),
        name="sum_all",
    )(*grads, *rows)


class Place:
    def __init__(self):
        self.core = lax.axis_index("core")
        self.z = lax.axis_index("seq")

    def over_core(self, value):
        return lax.ppermute(value, "core", [(0, 1), (1, 0)])

    def both_parts(self, part):
        part = part.astype(B16)
        return part, self.over_core(part)

    def both_cores(self, part):
        mine, other = self.both_parts(part)
        return mine.astype(F32) + other.astype(F32)


class Tree:
    def __init__(self, place):
        self.place = place

    def gather(self, table, ffb, columns, rows, tensors, tensors_at):
        n, r = table.shape
        small = jnp.pad(table, ((0, 128 - n), (0, 0))).T
        small = jnp.concatenate([small, jnp.pad(ffb, ((0, 16 - ffb.shape[0]), (0, 0)))], axis=0)
        sources = {-1: (small[None], 0, 1, "small")}
        for key, value in columns.items():
            sources[key] = value + ("columns",)
        for key, value in rows.items():
            sources[key] = value + ("rows",)
        keys = sorted(sources)
        outs = gather_all([sources[key] for key in keys], tensors, tensors_at)
        whole = {key: out for key, out in zip(keys, outs)}
        small = self.gathered = whole.pop(-1)
        table = small[..., :r, :].reshape(-1, 128).astype(F32).T
        ffb = small[..., r : r + ffb.shape[0], :].reshape(32, ffb.shape[0], -1).transpose(1, 0, 2)
        weights = {key: value.reshape(-1, value.shape[-1]) for key, value in whole.items()}
        return table, ffb.reshape(ffb.shape[0], -1), weights, [out.reshape(-1, out.shape[-1]) for out in outs[len(keys) :]]

    def prepare_late(self, columns, rows):
        core = self.place.core
        mine, other = lay_side(own_columns(columns, core)), lay_side(own_columns(columns, 1 - core))
        both = jnp.stack(xor_arrange([mine, self.place.over_core(other)], core))
        width = rows.shape[1]
        wide = both.shape[2] // width
        parts = [both[:, :, k * width : (k + 1) * width].reshape(-1, width) for k in range(wide)]
        return jnp.concatenate(parts + [rows], axis=0)

    def gather_late(self, local):
        width, wide = local.shape[1], 2
        local, _ = lax.optimization_barrier((local, self.gathered))
        full = lax.all_gather(local, ("dp", "seq"), axis=0, tiled=False)
        r = local.shape[0] // (2 * wide)
        first = [full[:, k * r : (k + 1) * r].reshape(4, 4, 2, -1, width) for k in range(wide)]
        first = [part.transpose(0, 2, 1, 3, 4).reshape(-1, width) for part in first]
        return lay_wide(first), full[:, wide * r :].reshape(-1, width)

    def full_columns(self, pairs):
        return lay_wide([product_tn(features, grad).astype(B16) for features, grad in pairs])

    def full_rows(self, features, grad):
        return product_tn(features, grad).astype(B16)

    def early_columns(self, value, parts):
        core = self.place.core
        value = value.reshape(4, 2, 4, -1, value.shape[1]).transpose(0, 2, 1, 3, 4)
        value = value.reshape(16, -1, value.shape[-1])
        total = lax.psum_scatter(value, ("dp", "seq"), scatter_dimension=0, tiled=True)
        total = total.reshape(2, -1, total.shape[-1])
        mine = lax.dynamic_index_in_dim(total, core, 0, keepdims=False)
        other = lax.dynamic_index_in_dim(total, 1 - core, 0, keepdims=False)
        both = jnp.stack(xor_arrange([mine, self.place.over_core(other)], core))
        return self.weave(both, parts)

    def early_both(self, pairs, parts, features, grad):
        core = self.place.core
        values = [product_tn(f, g).astype(B16) for f, g in pairs]
        width = min([v.shape[1] for v in values] + [grad.shape[1]])
        cut = [v[:, k : k + width] for v in values for k in range(0, v.shape[1], width)]
        cut = [v.reshape(4, 2, 4, -1, width).transpose(0, 2, 1, 3, 4).reshape(16, -1, width) for v in cut]
        rows = product_tn(features, grad).astype(B16)
        rows = rows.reshape(16, -1, rows.shape[1])
        r = rows.shape[1]
        cut += [rows[:, :, k : k + width] for k in range(0, rows.shape[2], width)]
        total = lax.psum_scatter(jnp.concatenate(cut, axis=1), ("dp", "seq"), scatter_dimension=0, tiled=True)[0]
        pieces, small = len(cut) - rows.shape[2] // width, cut[0].shape[1]
        columns, rest = total[: small * pieces].reshape(pieces, 2, small // 2, width), total[small * pieces :]
        mine = lax.dynamic_index_in_dim(columns, core, 1, keepdims=False)
        other = lax.dynamic_index_in_dim(columns, 1 - core, 1, keepdims=False)
        both = jnp.stack(xor_arrange([mine, self.place.over_core(other)], core))
        both = both.astype(F32).reshape(2, parts, pieces // parts, small // 2, width)
        both = both.transpose(0, 1, 3, 2, 4).reshape(2, parts, small // 2, 4, -1)
        both = both.transpose(1, 2, 3, 0, 4).reshape(parts, small // 2, -1)
        return both, rest.astype(F32).reshape(-1, r, width).transpose(1, 0, 2).reshape(r, -1)

    def early_rows(self, value):
        return lax.psum_scatter(value, ("dp", "seq"), scatter_dimension=0, tiled=True).astype(F32)

    def weave(self, both, parts):
        r = both.shape[1]
        both = both.astype(F32).reshape(2, r, parts, 4, -1)
        return both.transpose(2, 1, 3, 0, 4).reshape(parts, r, -1)

    def sums(self, columns, rows, table, hidden, tensors):
        n, m = table.shape[0], hidden.shape[0]
        both = jnp.concatenate(
            [
                table.reshape(n, 2, 2, 4, -1).transpose(1, 2, 3, 0, 4).reshape(2, 2, 4, -1),
                hidden.reshape(m, 2, 2, 4, -1).transpose(1, 2, 3, 0, 4).reshape(2, 2, 4, -1),
            ],
            axis=-1,
        )
        size = both.shape[-1]
        both = jnp.pad(both, ((0, 0), (0, 0), (0, 0), (0, -size % 2048))).reshape(2, 2, 1, 4, 8, -1)
        grads, keys = [], []
        for key, (value, _) in columns.items():
            grads.append(value.reshape(2, 2, 2, 4, value.shape[0] // 32, value.shape[1]))
            keys.append(key)
        for key, value in rows.items():
            grads.append(value.reshape(2, 2, 1, 4, value.shape[0] // 16, value.shape[1]))
            keys.append(key)
        order = sorted(range(len(keys)), key=lambda k: keys[k])
        parts = [columns[keys[k]][1] if keys[k] in columns else 1 for k in order] + [1]
        outs = sum_all([grads[k] for k in order] + [both], parts, [t.reshape(4, -1, t.shape[-1]) for t in tensors], SUM_ROWS)
        result = {}
        for k, out in zip(order, outs):
            result[keys[k]] = out
        flat = outs[len(keys)].reshape(-1)[:size]
        edge = table.shape[1] // 16 * n
        return result, flat[:edge].reshape(n, -1), flat[edge:].reshape(m, -1), outs[len(keys) + 1 :]


class Plain:
    def __init__(self, place):
        self.place = place
        self.axes = ("dp", "core", "seq")

    def row_in(self, array):
        place = self.place
        parts = array.reshape(2, array.shape[1], 2, -1)
        got = []
        for m in range(4):
            code = place.z ^ m
            piece = lax.dynamic_index_in_dim(parts, code // 2, 0, keepdims=False)
            piece = lax.dynamic_index_in_dim(piece, code % 2, 1, keepdims=False)
            moves = []
            for c in range(2):
                for z in range(4):
                    q = m ^ z
                    moves.append((c * 4 + z, q % 2 * 4 + 2 * c + q // 2))
            got.append(lax.ppermute(piece, ("core", "seq"), moves))
        half = jnp.concatenate(xor_arrange(got, (place.z % 2) * 2 + place.core), axis=0)
        return jnp.concatenate(xor_arrange([half, place.over_core(half)], place.core), axis=1)

    def row_out(self, row):
        place = self.place
        parts = row.reshape(4, -1, 2, row.shape[1] // 2)
        mine = lax.dynamic_index_in_dim(parts, place.core, 2, keepdims=False)
        q_here = (place.z % 2) * 2 + place.core
        got = []
        for m in range(4):
            piece = lax.dynamic_index_in_dim(mine, q_here ^ m, 0, keepdims=False)
            moves = []
            for c in range(2):
                for z in range(4):
                    q = (z % 2) * 2 + c
                    moves.append((c * 4 + z, z // 2 * 4 + (m ^ q)))
            got.append(lax.ppermute(piece, ("core", "seq"), moves))
        placed = xor_arrange(got, place.z)
        return jnp.stack([jnp.concatenate(placed[2 * i : 2 * i + 2], axis=1) for i in range(2)])

    def gather(self, table, ffb, columns, rows, tensors, tensors_at):
        table = lax.all_gather(table, self.axes, axis=1, tiled=True).astype(F32)
        ffb = lax.all_gather(ffb, self.axes, axis=1, tiled=True)
        weights = {}
        for key, (value, first, number) in columns.items():
            weights[key] = self.whole_columns(value[first : first + number])
        for key, (value, first, _) in rows.items():
            weights[key] = self.whole_rows(value[first])
        return table, ffb, weights, [self.row_in(tensor) for tensor in tensors]

    def whole_columns(self, value):
        full = lax.all_gather(value, self.axes, axis=1, tiled=True)
        return lay_side(own_columns(full, self.place.core))

    def whole_rows(self, value):
        full = lax.all_gather(value, self.axes, axis=0, tiled=True)
        split = full.reshape(4, 2, full.shape[0] // 8, full.shape[1])
        mine = lax.dynamic_index_in_dim(split, self.place.core, 1, keepdims=False)
        return mine.reshape(-1, full.shape[1])

    def prepare_late(self, columns, rows):
        return columns, rows

    def gather_late(self, prepared):
        columns, rows = prepared
        return self.whole_columns(columns), self.whole_rows(rows)

    def full_columns(self, pairs):
        return lay_wide([product_tn(features, grad).astype(B16) for features, grad in pairs])

    def full_rows(self, features, grad):
        return product_tn(features, grad).astype(B16)

    def early_columns(self, full, parts):
        full = full.reshape(full.shape[0], parts, -1).transpose(1, 0, 2).astype(B16)
        return self.scatter(self.spread(full, 2), 1)

    def early_both(self, pairs, parts, features, grad):
        return self.early_columns(self.full_columns(pairs), parts), self.early_rows(self.full_rows(features, grad))

    def early_rows(self, full):
        return self.scatter(self.spread(full, 0), 0)

    def spread(self, half, axis):
        shape = half.shape[:axis] + (4, 1, half.shape[axis] // 4) + half.shape[axis + 1 :]
        half = half.reshape(shape)
        empty = jnp.zeros_like(half)
        first = jnp.where(self.place.core == 0, half, empty)
        second = jnp.where(self.place.core == 1, half, empty)
        both = jnp.concatenate([first, second], axis=axis + 1)
        return both.reshape(shape[:axis] + (-1,) + shape[axis + 3 :])

    def scatter(self, value, axis):
        return lax.psum_scatter(value, self.axes, scatter_dimension=axis, tiled=True).astype(F32)

    def sums(self, columns, rows, table, hidden, tensors):
        result = {}
        for key, (value, parts) in columns.items():
            result[key] = self.early_columns(value, parts)
        for key, value in rows.items():
            result[key] = self.early_rows(value)
        small = [self.scatter(self.spread(v, 1), 1) for v in (table, hidden)]
        return result, small[0], small[1], [self.row_out(tensor) for tensor in tensors]


def on_device(
    dp,
    seq,
    src_x,
    tgt_x,
    src_seg,
    tgt_seg,
    tgt_len,
    src_lang,
    tgt_lang,
    lang_table,
    gains,
    biases,
    ff_biases,
    enc_proj,
    enc_oproj,
    enc_in,
    enc_out,
    dec_proj,
    dec_oproj,
    dec_in,
    dec_out,
    src_cot,
    tgt_cot,
):
    place = Place()
    core = place.core
    moves = Tree(place) if (dp, seq) == (4, 4) else Plain(place)
    width = enc_oproj.shape[1]
    half = width // 2
    langs = lang_table.shape[0]

    table = jnp.concatenate([lang_table, gains, biases], axis=0)
    late = moves.prepare_late(dec_in[None], dec_out)
    table, late = lax.optimization_barrier((table, late))
    table, ffb, weights, tensors = moves.gather(
        table,
        ff_biases,
        {0: (enc_proj, 0, 3), 2: (enc_in[None], 0, 1), 4: (dec_proj, 0, 3), 6: (dec_proj, 3, 3)},
        {1: (enc_oproj[None], 0, 1), 3: (enc_out[None], 0, 1), 5: (dec_oproj, 0, 1), 7: (dec_oproj, 1, 1)},
        [src_x, tgt_x, tgt_cot, src_cot],
        [2, 5, 8, 11],
    )
    source, target, target_cot, source_cot = tensors
    enc_qkv_w, enc_o_w, enc_in_w, enc_out_w, dec_qkv_w, dec_o_w, cross_w, cross_o_w = (
        weights[k] for k in range(8)
    )
    dec_in_w, dec_out_w = moves.gather_late(late)
    table, ffb_own = lax.optimization_barrier((table, own_columns(ffb, core).astype(F32)))
    languages = table[: langs + -langs % 16].astype(B16)
    gain_f = [table[langs + k : langs + k + 1] for k in range(5)]
    bias_f = [table[langs + 5 + k : langs + 6 + k] for k in range(16)]
    table_own = own_columns(table, core)
    bias_own = [table_own[langs + 5 + k : langs + 6 + k] for k in range(16)]

    meta = jnp.concatenate([src_seg, tgt_seg, tgt_len[:, None], src_lang, tgt_lang], axis=1)
    rows = jnp.where(place.z // 2 == core, meta, place.over_core(meta))
    row = lax.dynamic_index_in_dim(rows, place.z % 2, 0, keepdims=False)
    count, segs = src_seg.shape[1], src_lang.shape[1]
    s_seg, t_seg, t_len = row[:count], row[count : 2 * count], row[2 * count]
    s_lang, t_lang = row[2 * count + 1 : 2 * count + 1 + segs], row[2 * count + 1 + segs :]

    def onehot(segments, chosen):
        member = segments[:, None] == jnp.arange(segs, dtype=jnp.int32)[None, :]
        token = jnp.sum(jnp.where(member, chosen[None, :], 0), axis=1)
        return (token[:, None] == jnp.arange(langs + -langs % 16, dtype=jnp.int32)[None, :]).astype(B16)

    src_hot, tgt_hot = onehot(s_seg, s_lang), onehot(t_seg, t_lang)
    enc_masks = (block_info(False, s_seg, s_seg, t_len), s_seg[None, :], s_seg[:, None])
    dec_masks = (block_info(True, t_seg, t_seg, t_len), t_seg[None, :], t_seg[:, None])
    cross_masks = (block_info(False, t_seg, s_seg, t_len), t_seg[None, :], s_seg[:, None])

    none = jnp.zeros((1, half), F32)
    packed = (0, half // GROUP, 2 * half // GROUP)

    enc_h0 = source.astype(F32) + product(src_hot, languages)
    enc_n1 = layer_norm(enc_h0, gain_f[0], bias_f[0])
    enc_qkv_bias = jnp.concatenate([bias_own[1], none, bias_own[2]], axis=1)
    enc_qkv = (product(enc_n1, enc_qkv_w) + enc_qkv_bias).astype(B16)
    enc_mixed, enc_lse = attend_forward(False, enc_masks, enc_qkv, enc_qkv, enc_qkv, packed, half)
    enc_h1 = enc_h0 + place.both_cores(product(enc_mixed, enc_o_w)) + bias_f[3]
    enc_n2 = layer_norm(enc_h1, gain_f[1], bias_f[4])
    enc_acted, enc_slope = gelu_both(product(enc_n2, enc_in_w) + ffb_own[0:1])
    encoded = enc_h1 + place.both_cores(product(enc_acted, enc_out_w)) + bias_f[5]
    memory = encoded.astype(B16)

    dec_h0 = target.astype(F32) + product(tgt_hot, languages)
    dec_n1 = layer_norm(dec_h0, gain_f[2], bias_f[6])
    dec_qkv_bias = jnp.concatenate([bias_own[7], none, bias_own[8]], axis=1)
    dec_qkv = (product(dec_n1, dec_qkv_w) + dec_qkv_bias).astype(B16)
    dec_mixed, dec_lse = attend_forward(True, dec_masks, dec_qkv, dec_qkv, dec_qkv, packed, half)
    dec_h1 = dec_h0 + place.both_cores(product(dec_mixed, dec_o_w)) + bias_f[9]
    dec_n2 = layer_norm(dec_h1, gain_f[3], bias_f[10])
    cross_q = (product(dec_n2, cross_w[:, :half]) + bias_own[11]).astype(B16)
    cross_kv_bias = jnp.concatenate([none, bias_own[12]], axis=1)
    cross_kv = (product(memory, cross_w[:, half:]) + cross_kv_bias).astype(B16)
    apart = (0, 0, half // GROUP)
    cross_mixed, cross_lse = attend_forward(False, cross_masks, cross_q, cross_kv, cross_kv, apart, half)
    dec_h2 = dec_h1 + place.both_cores(product(cross_mixed, cross_o_w)) + bias_f[13]
    dec_n3 = layer_norm(dec_h2, gain_f[4], bias_f[14])
    dec_acted, dec_slope = gelu_both(product(dec_n3, dec_in_w) + ffb_own[1:2])
    decoded = dec_h2 + place.both_cores(product(dec_acted, dec_out_w)) + bias_f[15]

    dec_du = (product_nt(target_cot, dec_out_w) * dec_slope.astype(F32)).astype(B16)
    dec_dn3 = place.both_parts(product_nt(dec_du, dec_in_w))
    dec_out_full = moves.full_rows(dec_acted, target_cot)
    dec_in_full = moves.full_columns([(dec_n3, dec_du)])
    dec_out_grad = moves.early_rows(dec_out_full)
    dec_in_grad = moves.early_columns(dec_in_full, 1)
    grad_h2, cross_branch, cross_rows = norm_backward(dec_h2, gain_f[4], dec_dn3, target_cot)
    cross_branch, _, _ = lax.optimization_barrier((cross_branch, dec_out_full, dec_in_full))

    cross_do = product_nt(cross_branch, cross_o_w).astype(B16)
    cross_dq, cross_dkv = attend_backward(
        False, cross_masks, cross_q, cross_kv, cross_kv, apart, half, cross_mixed, cross_lse, cross_do
    )
    grad_memory = place.both_cores(product_nt(cross_dkv, cross_w[:, half:]))
    dec_dn2 = place.both_parts(product_nt(cross_dq, cross_w[:, :half]))

    cross_grad, cross_o_grad = moves.early_both(
        [(dec_n2, cross_dq), (memory, cross_dkv)], 3, cross_mixed, cross_branch
    )

    source_cot_f = source_cot.astype(F32) + grad_memory
    enc_ff_branch = source_cot_f.astype(B16)
    enc_down, enc_in_full, enc_out_full, enc_hidden = ffn_backward(
        enc_ff_branch, enc_n2, enc_acted, enc_slope, enc_in_w, enc_out_w
    )
    enc_dn2 = place.both_parts(enc_down)

    grad_h1, self_branch, self_rows = norm_backward(dec_h1, gain_f[3], dec_dn2, grad_h2)
    dec_do = product_nt(self_branch, dec_o_w).astype(B16)
    (dec_dqkv,) = attend_backward(
        True, dec_masks, dec_qkv, dec_qkv, dec_qkv, packed, half, dec_mixed, dec_lse, dec_do
    )
    dec_dn1 = place.both_parts(product_nt(dec_dqkv, dec_qkv_w))
    target_high, target_rows, target_lang = norm_backward(dec_h0, gain_f[2], dec_dn1, grad_h1, tgt_hot)

    grad_e1, enc_branch, enc_rows = norm_backward(enc_h1, gain_f[1], enc_dn2, source_cot_f)
    enc_do = product_nt(enc_branch, enc_o_w).astype(B16)
    (enc_dqkv,) = attend_backward(
        False, enc_masks, enc_qkv, enc_qkv, enc_qkv, packed, half, enc_mixed, enc_lse, enc_do
    )
    enc_dn1 = place.both_parts(product_nt(enc_dqkv, enc_qkv_w))
    source_high, source_rows, source_lang = norm_backward(enc_h0, gain_f[0], enc_dn1, grad_e1, src_hot)

    ff_sums = jnp.stack([column_sum(enc_ff_branch), column_sum(target_cot)])
    wide = [rows[:3] for rows in (source_rows, enc_rows, target_rows, self_rows, cross_rows)]
    wide = own_columns(jnp.concatenate([source_lang + target_lang] + wide + [ff_sums], axis=0), core)
    enc_sum, dec_sum = column_sum(enc_dqkv)[None], column_sum(dec_dqkv)[None]
    narrow = [enc_sum[:, :half], enc_sum[:, 2 * half :], dec_sum[:, :half], dec_sum[:, 2 * half :]]
    narrow += [column_sum(cross_dq)[None], column_sum(cross_dkv)[None, half:]]
    small_table = jnp.concatenate([wide] + narrow, axis=0)
    at = src_hot.shape[1]
    gain_places = [at, at + 3, at + 6, at + 9, at + 12]
    bias_places = [at + k for k in (1, 17, 18, 5, 4, 15, 7, 19, 20, 11, 10, 21, 22, 14, 13, 16)]

    grads, small, ffb_grad, outputs = moves.sums(
        {
            1: (moves.full_columns([(dec_n1, dec_dqkv)]), 3),
            2: (enc_in_full, 1),
            4: (moves.full_columns([(enc_n1, enc_dqkv)]), 3),
        },
        {
            0: moves.full_rows(dec_mixed, self_branch),
            3: enc_out_full,
            5: moves.full_rows(enc_mixed, enc_branch),
        },
        small_table,
        jnp.concatenate([enc_hidden, column_sum(dec_du)[None]], axis=0),
        [memory, decoded.astype(B16), source_high, target_high],
    )
    picked = lambda places: jnp.concatenate([small[k : k + 1] for k in places], axis=0)
    return (
        outputs[0],
        outputs[1],
        outputs[2].astype(F32),
        outputs[3].astype(F32),
        small[:langs],
        picked(gain_places),
        picked(bias_places),
        ffb_grad,
        grads[4],
        grads[5],
        grads[2][0],
        grads[3],
        jnp.concatenate([grads[1], cross_grad], axis=0),
        jnp.stack([grads[0], cross_o_grad]),
        dec_in_grad[0],
        dec_out_grad,
    )


def solution(mesh):
    dp, seq = mesh.shape["dp"] // 2, mesh.shape["seq"]
    pairs = Mesh(mesh.devices.reshape(dp, 2, seq), ("dp", "core", "seq"))
    both, every = ("dp", "core"), ("dp", "core", "seq")
    rows = P(both, "seq", None)
    columns = P(None, every)
    middle = P(None, every, None)
    first = P(every, None)
    weights = (columns, columns, columns, columns, middle, first, first, first, middle, middle, first, first)
    return jax.shard_map(
        functools.partial(on_device, dp, seq),
        mesh=pairs,
        in_specs=(rows, rows, P(both, None), P(both, None), P(both), P(both, None), P(both, None))
        + weights
        + (rows, rows),
        out_specs=(rows, rows, rows, rows) + weights,
        check_vma=False,
    )
```
